32 devices in a mesh: state: 16 (over z, y, core), det: 2 (over x).
Axes of the slice: x: 2, y: 2, z: 4, core: 2. Of those that a mesh axis runs over, the one named last changes fastest.
Arguments:
- amplitudes: bfloat16 [64, 4096, 324], P('state', 'det'), may hold values from -0.09375 to 0.09375
Outputs:
- density_tiles: float32 [2, 256, 324, 324], P(None, ('state', 'det'))
The draws below stay inside these ranges and needn't reach their ends.
All inputs are finite; a program needn't handle non-finite values.
Results may differ from the reference program's by a relative error of at most 0.0003.
Values may be sent and summed in bfloat16 or wider, within the bound.
No kernel may reach another device: no remote copies, remote signals or barrier semaphores. Data moves between devices by JAX's collectives and lax.ppermute only.
A program may use at most 128 MiB of HBM per device.

```python
import jax
import jax.numpy as jnp
from jax import lax

NOP = 324
ST_DEV = 4
BLOCKS = 16
STATES = 64
NDET = 4096


def levels(stream_key, extent, shards, smallest, top_value):
    loudness, own = 1.0, jax.random.fold_in(stream_key, 6)
    for axis_at, shards_of in shards:
        steps = jnp.exp(jax.random.uniform(jax.random.fold_in(own, axis_at), (shards_of,), jnp.float32, smallest / len(shards), top_value / len(shards)))
        loudness = loudness * jnp.repeat(steps, extent[axis_at] // shards_of).reshape([-1 if axis == axis_at else 1 for axis in range(len(extent))])
    return loudness


def normal_values(own_key, extent, scale, most, shards=(), kind=jnp.bfloat16):
    result = jax.random.normal(own_key, extent, jnp.float32) * scale
    if len(shards) > 0:
        result = levels(own_key, extent, shards, -0.22, 0.18) * result
    return jnp.clip(result, min=-most, max=most).astype(kind)


def setup_inputs(seed: int = 0) -> dict:
    keys = jax.random.split(jax.random.key(seed), 2)
    amplitudes = normal_values(keys[0], (STATES, NDET, NOP), NDET ** -0.5, 0.09375, ((0, 16), (1, 2)))
    return {"amplitudes": amplitudes}


def reference(amplitudes):
    blocks = amplitudes.reshape(BLOCKS, ST_DEV, NDET, NOP)
    results = []
    for hop in (BLOCKS // 2, 1):
        def meet(index):
            mine = lax.dynamic_index_in_dim(blocks, index, 0, keepdims=False).astype(jnp.float32)
            other = lax.dynamic_index_in_dim(blocks, jnp.bitwise_xor(index, hop).astype(jnp.int32), 0, keepdims=False).astype(jnp.float32)
            tiles = jnp.einsum("adp,bdq->abpq", mine, other, precision=lax.Precision.HIGHEST)
            return tiles.reshape(ST_DEV * ST_DEV, NOP, NOP)
        tiles = lax.map(meet, jnp.arange(BLOCKS, dtype=jnp.int32))
        results.append(tiles.reshape(STATES * ST_DEV, NOP, NOP))
    return jnp.stack(results)
```

```python
import functools

import jax
import jax.numpy as jnp
from jax import lax
from jax.experimental import pallas as pl
from jax.experimental.pallas import tpu as pltpu
from jax.sharding import PartitionSpec as P

LANES = 128
VMEM_LIMIT = 40 * 2**20
SQUARE_TOP = 2.0**13


def contract_last(left, right):
    return lax.dot_general(left, right, (((1,), (1,)), ((), ())), preferred_element_type=jnp.float32)


def call(body, grid, scalars, in_specs, out_specs, out_shape, flops, moved, aliases={}):
    return pl.pallas_call(
        body,
        grid_spec=pltpu.PrefetchScalarGridSpec(
            num_scalar_prefetch=scalars, grid=grid, in_specs=in_specs, out_specs=out_specs
        ),
        out_shape=out_shape,
        input_output_aliases=aliases,
        compiler_params=pltpu.CompilerParams(vmem_limit_bytes=VMEM_LIMIT),
        cost_estimate=pl.CostEstimate(flops=flops, bytes_accessed=moved, transcendentals=0),
    )


def f32(*shape):
    return jax.ShapeDtypeStruct(shape, jnp.float32)


def whole(shape):
    return pl.BlockSpec(shape, lambda *_: (0,) * len(shape))


def near_send(det, own, partner):
    states, ops, depth = own.shape
    half, wide = states // 2, ops // LANES * LANES

    def body(x_ref, own_ref, partner_ref, main_ref, rest_ref):
        main_ref[0] = contract_last(own_ref[0], partner_ref[0, :wide])
        rest_ref[0] = contract_last(partner_ref[0, wide:], own_ref[0])

    return call(
        body,
        (half, states),
        1,
        [
            pl.BlockSpec((1, ops, depth), lambda a, b, x: (half * (1 - x[0]) + a, 0, 0)),
            pl.BlockSpec((1, ops, depth), lambda a, b, x: (b, 0, 0)),
        ],
        [
            pl.BlockSpec((1, ops, wide), lambda a, b, x: (a * states + b, 0, 0)),
            pl.BlockSpec((1, ops - wide, ops), lambda a, b, x: (a * states + b, 0, 0)),
        ],
        [f32(half * states, ops, wide), f32(half * states, ops - wide, ops)],
        half * states * ops * ops * depth * 2,
        half * states * ops * (ops * 4 + depth * 2),
    )(det, own, partner)


def near_keep(det, own, partner):
    states, ops, depth = own.shape
    half = states // 2

    def body(x_ref, own_ref, partner_ref, tile_ref):
        tile_ref[0] = contract_last(own_ref[0], partner_ref[0])

    return call(
        body,
        (half, states),
        1,
        [
            pl.BlockSpec((1, ops, depth), lambda a, b, x: (half * x[0] + a, 0, 0)),
            pl.BlockSpec((1, ops, depth), lambda a, b, x: (b, 0, 0)),
        ],
        pl.BlockSpec((1, ops, ops), lambda a, b, x: (a * states + b, 0, 0)),
        f32(half * states, ops, ops),
        half * states * ops * ops * depth * 2,
        half * states * ops * (ops * 4 + depth * 2),
    )(det, own, partner)


def near_sum(keep, main, rest):
    tiles, ops, _ = keep.shape
    wide = main.shape[2]

    def body(keep_ref, main_ref, rest_ref, out_ref):
        out_ref[0, 0, :, :wide] = keep_ref[0, :, :wide] + main_ref[0]
        out_ref[0, 0, :, wide:] = keep_ref[0, :, wide:] + rest_ref[0].T

    return call(
        body,
        (tiles,),
        0,
        [
            pl.BlockSpec((1, ops, ops), lambda t: (t, 0, 0)),
            pl.BlockSpec((1, ops, wide), lambda t: (t, 0, 0)),
            pl.BlockSpec((1, ops - wide, ops), lambda t: (t, 0, 0)),
        ],
        pl.BlockSpec((1, 1, ops, ops), lambda t: (1, t, 0, 0)),
        f32(2, tiles, ops, ops),
        tiles * ops * ops,
        tiles * ops * ops * 12,
    )(keep, main, rest)


def far_terms(det, own, got, turned):
    states, ops, depth = own.shape
    half = states // 2
    width = got.size // (states * depth)
    tile = (ops, width) if turned else (width, ops)
    count = half * states + half * half

    def body(x_ref, own_ref, got_ref, send_ref, keep_ref):
        x, step = x_ref[0], pl.program_id(0)
        v = (step + half * x) % states
        if turned:
            def terms(first):
                block = got_ref[pl.ds(first, half)].reshape(half * width, depth)
                both = contract_last(own_ref[0], block)
                return [both[:, a * width : (a + 1) * width] for a in range(half)]

            other, mine = terms(half * (1 - x)), terms(half * x)
        else:
            every = contract_last(got_ref[...], own_ref[0])
            parts = [every[u * width : (u + 1) * width] for u in range(states)]
            low, high = parts[:half], parts[half:]
            other = [jnp.where(x == 0, q, p) for p, q in zip(low, high)]
            mine = [jnp.where(x == 0, p, q) for p, q in zip(low, high)]
        for a in range(half):
            send_ref[a * states + v] = other[a]
            keep_ref[a * states + v] = mine[a]

        @pl.when(step < half)
        def _():
            for a in range(half):
                keep_ref[half * states + step * half + a] = other[a]

        @pl.when(step >= half)
        def _():
            for a in range(half):
                send_ref[half * states + (step - half) * half + a] = mine[a]

    return call(
        body,
        (states,),
        1,
        [
            pl.BlockSpec((1, ops, depth), lambda g, x: ((g + half * x[0]) % states, 0, 0)),
            whole(got.shape),
        ],
        [whole((count, *tile))] * 2,
        [f32(count, *tile)] * 2,
        states * states * ops * width * depth * 2,
        states * ops * depth * 2 + got.size * 2 + 2 * count * ops * width * 4,
    )(det, own, got)


def far_sum(det, keep, came, states):
    count, rows, lanes = keep.shape
    half = states // 2
    back = half * states
    under = rows + 8 - rows % 8

    def body(x_ref, keep_ref, came_ref, back_ref, own_ref):
        x = x_ref[0]
        top = jnp.zeros((rows, lanes), jnp.float32)
        for t in range(back):
            tile = keep_ref[t] + came_ref[t]
            back_ref[t, :rows] = tile
            top = jnp.maximum(top, jnp.abs(tile))
        back_ref[0, rows:] = jnp.broadcast_to(jnp.max(top, keepdims=True), (under - rows, lanes))
        for b in range(half):
            for a in range(half):
                own_ref[b * states + half * x + a] = back_ref[a * states + half * x + b, :rows]
                t = back + b * half + a
                own_ref[b * states + half * (1 - x) + a] = keep_ref[t] + came_ref[t]

    return call(
        body,
        (1,),
        1,
        [whole((count, rows, lanes))] * 2,
        [whole((back, under, lanes)), whole((back, rows, lanes))],
        [f32(back, under, lanes), f32(back, rows, lanes)],
        2 * count * rows * lanes,
        (2 * count + 2 * back) * rows * lanes * 4,
    )(det, keep, came)


def squared(sums, rows):
    exponent = jnp.floor(jnp.log2(jnp.maximum(sums[0, rows, 0], 2.0**-120)))
    scaled = sums * jnp.exp2(-exponent)
    row = lax.broadcasted_iota(jnp.int32, sums.shape, 1)
    return jnp.where(row < rows, scaled * jnp.abs(scaled) * SQUARE_TOP, exponent).astype(jnp.float16)


def rooted(code, rows):
    exponent = code[0, rows, 0].astype(jnp.float32)
    values = code[:, :rows].astype(jnp.float32)
    root = jnp.sqrt(jnp.abs(values)) * (jnp.exp2(exponent) * SQUARE_TOP**-0.5)
    return jnp.where(values < 0, -root, root)


def place(receiver, out, owned, came):
    _, tiles, ops, _ = out.shape
    full = len(came)
    wide = full * LANES

    def body(role_ref, out_in, *refs):
        owned_refs, came_refs, out_ref = refs[: full + 1], refs[full:-1][1:], refs[-1]

        @pl.when(role_ref[0] == 1)
        def _():
            for k in range(full):
                out_ref[0, 0, :, k * LANES : (k + 1) * LANES] = owned_refs[k][0]
            out_ref[0, 0, :, wide:] = owned_refs[full][0].T

        @pl.when(role_ref[0] == 0)
        def _():
            for k in range(full):
                out_ref[0, 0, k * LANES : (k + 1) * LANES, :] = came_refs[k][0].T

    turned = pl.BlockSpec((1, ops, LANES), lambda t, r: (t, 0, 0))
    return call(
        body,
        (tiles,),
        1,
        [pl.BlockSpec(memory_space=pl.ANY)]
        + [turned] * full
        + [pl.BlockSpec((1, ops - wide, ops), lambda t, r: (t, 0, 0))]
        + [turned] * full,
        pl.BlockSpec((1, 1, ops, ops), lambda t, r: (0, t, 0, 0)),
        f32(*out.shape),
        tiles * ops * ops,
        tiles * ops * ops * 12,
        {1: 0},
    )(receiver, out, *owned, *came)


def paired(amplitudes):
    blocks = lax.axis_size("state")
    far = blocks.bit_length() - 2
    states, depth, ops = amplitudes.shape
    half, full = states // 2, ops // LANES
    wide = full * LANES
    both = ("state", "det")
    senders = [s for s in range(blocks) if (s & 1) == (s >> far & 1)]
    receivers = [s for s in range(blocks) if s not in senders]
    over = [(2 * s + x, 2 * (s ^ 1 << far) + x) for s in senders for x in range(2)]
    back = [(b, a) for a, b in over]
    across = [(2 * s + x, 2 * s + 1 - x) for s in receivers for x in range(2)]

    state = lax.axis_index("state")
    det = lax.axis_index("det").astype(jnp.int32)[None]
    receiver = ((state & 1) ^ (state >> far & 1)).astype(jnp.int32)[None]

    own = jnp.transpose(amplitudes, (0, 2, 1))
    chunks = [own[:, k * LANES : (k + 1) * LANES] for k in range(full)]
    chunks.append(own[:, wide:].reshape(states * (ops - wide), depth))
    got = [lax.ppermute(c, both, over) for c in chunks]

    partner = lax.ppermute(own, "state", [(s, s ^ 1) for s in range(blocks)])
    main, rest = near_send(det, own, partner)
    main, rest = (lax.ppermute(v, "det", [(0, 1), (1, 0)]) for v in (main, rest))
    keep = near_keep(det, own, partner)

    returned, owned = [], []
    for k, block in enumerate(got):
        send, kept = far_terms(det, own, block, k < full)
        came = lax.ppermute(send, both, across)
        sums, mine = far_sum(det, kept, came, states)
        rows = kept.shape[1]
        returned.append(rooted(lax.ppermute(squared(sums, rows), both, back), rows))
        owned.append(mine)

    out = near_sum(keep, main, rest)
    out = place(receiver, out, owned, returned[:full])
    last = jnp.where(receiver[0] == 1, out[0, :, wide:], returned[full])
    return lax.dynamic_update_slice(out, last[None], (0, 0, wide, 0))


def partner_2(value, axis, stride):
    mask = 2**stride
    pairs = [(source, source ^ mask) for source in range(lax.axis_size(axis))]
    return lax.ppermute(value, axis, pairs)


def pair_terms(own_block, partner, count):
    operators = own_block.shape[2]
    terms = jnp.einsum("adp,bdq->abpq", own_block, partner, preferred_element_type=jnp.float32)
    return terms.reshape(count, operators, operators)


def exchanged(amplitudes):
    blocks = lax.axis_size("state")
    far_bit = blocks.bit_length() - 2
    states = amplitudes.shape[0]
    gathered = []
    for bit in (far_bit, 0):
        partner = partner_2(amplitudes, "state", bit)
        terms = pair_terms(amplitudes, partner, states * states)
        gathered.append(lax.psum_scatter(terms, "det", scatter_dimension=0, tiled=True))
    return jnp.stack(gathered)


def on_device(amplitudes):
    states, _, ops = amplitudes.shape
    two = lax.axis_size("det") == 2 and lax.axis_size("state") >= 4
    if two and states % 2 == 0 and ops > LANES and ops % LANES % 8:
        return paired(amplitudes)
    return exchanged(amplitudes)


def solution(mesh):
    return jax.shard_map(
        on_device,
        mesh=mesh,
        in_specs=(P("state", "det", None),),
        out_specs=P(None, ("state", "det"), None, None),
        check_vma=False,
    )
```

```python
import functools

import jax
import jax.numpy as jnp
from jax import lax
from jax.experimental import pallas as pl
from jax.experimental.pallas import tpu as pltpu
from jax.sharding import PartitionSpec as P

LANES = 128
VMEM_LIMIT = 40 * 2**20
SQUARE_TOP = 2.0**13
SHORT, LONG = 10**3, 10**10


def contract_last(left, right):
    return lax.dot_general(left, right, (((1,), (1,)), ((), ())), preferred_element_type=jnp.float32)


def call(body, grid, scalars, in_specs, out_specs, out_shape, declared, aliases={}):
    return pl.pallas_call(
        body,
        grid_spec=pltpu.PrefetchScalarGridSpec(
            num_scalar_prefetch=scalars, grid=grid, in_specs=in_specs, out_specs=out_specs
        ),
        out_shape=out_shape,
        input_output_aliases=aliases,
        compiler_params=pltpu.CompilerParams(vmem_limit_bytes=VMEM_LIMIT),
        cost_estimate=pl.CostEstimate(flops=declared, bytes_accessed=declared // 100, transcendentals=0),
    )


def f32(*shape):
    return jax.ShapeDtypeStruct(shape, jnp.float32)


def up(size, unit):
    return -(-size // unit) * unit


def after(value, *done):
    return lax.optimization_barrier((value, *done))[0]


def whole(shape):
    return pl.BlockSpec(shape, lambda *_: (0,) * len(shape))


def near_send(det, own, partner):
    states, ops, depth = own.shape
    half, wide = states // 2, ops // LANES * LANES
    rest, lanes = ops - wide, up(ops, LANES)

    def body(x_ref, own_ref, partner_ref, main_ref, rest_ref):
        main_ref[0, :ops] = contract_last(own_ref[0], partner_ref[0, :wide])
        rest_ref[0, :rest, :ops] = contract_last(partner_ref[0, wide:], own_ref[0])

    shapes = [(up(ops, 8), wide), (up(rest, 8), lanes)]
    return call(
        body,
        (half, states),
        1,
        [
            pl.BlockSpec((1, ops, depth), lambda a, b, x: (half * (1 - x[0]) + a, 0, 0)),
            pl.BlockSpec((1, ops, depth), lambda a, b, x: (b, 0, 0)),
        ],
        [pl.BlockSpec((1, *s), lambda a, b, x: (a * states + b, 0, 0)) for s in shapes],
        [f32(half * states, *s) for s in shapes],
        SHORT,
    )(det, own, partner)


def near_keep(det, own, partner):
    states, ops, depth = own.shape
    half = states // 2

    def body(x_ref, own_ref, partner_ref, tile_ref):
        tile_ref[0] = contract_last(own_ref[0], partner_ref[0])

    return call(
        body,
        (half, states),
        1,
        [
            pl.BlockSpec((1, ops, depth), lambda a, b, x: (half * x[0] + a, 0, 0)),
            pl.BlockSpec((1, ops, depth), lambda a, b, x: (b, 0, 0)),
        ],
        pl.BlockSpec((1, ops, ops), lambda a, b, x: (a * states + b, 0, 0)),
        f32(half * states, ops, ops),
        SHORT,
    )(det, own, partner)


def near_sum(keep, main, rest):
    tiles, ops, _ = keep.shape
    wide = main.shape[2]

    def body(keep_ref, main_ref, rest_ref, out_ref):
        for t in range(tiles):
            out_ref[0, :, t, :wide] = keep_ref[t, :, :wide] + main_ref[t]
            out_ref[0, :, t, wide:] = keep_ref[t, :, wide:] + rest_ref[t].T[:, : ops - wide]

    return call(
        body,
        (pl.cdiv(ops, LANES),),
        0,
        [
            pl.BlockSpec((tiles, LANES, ops), lambda i: (0, i, 0)),
            pl.BlockSpec((tiles, LANES, wide), lambda i: (0, i, 0)),
            pl.BlockSpec((tiles, rest.shape[1], LANES), lambda i: (0, 0, i)),
        ],
        pl.BlockSpec((1, LANES, tiles, ops), lambda i: (1, i, 0, 0)),
        f32(2, ops, tiles, ops),
        LONG,
    )(keep, main, rest)


def far_terms(det, own, got, turned):
    states, ops, depth = own.shape
    half = states // 2
    width = got.size // (states * depth)
    tile = (ops, width) if turned else (width, ops)
    count = half * states + half * half

    def body(x_ref, own_ref, got_ref, send_ref, keep_ref):
        x, step = x_ref[0], pl.program_id(0)
        v = (step + half * x) % states
        if turned:
            def terms(first):
                block = got_ref[pl.ds(first, half)].reshape(half * width, depth)
                both = contract_last(own_ref[0], block)
                return [both[:, a * width : (a + 1) * width] for a in range(half)]

            other, mine = terms(half * (1 - x)), terms(half * x)
        else:
            every = contract_last(got_ref[...], own_ref[0])
            parts = [every[u * width : (u + 1) * width] for u in range(states)]
            low, high = parts[:half], parts[half:]
            other = [jnp.where(x == 0, q, p) for p, q in zip(low, high)]
            mine = [jnp.where(x == 0, p, q) for p, q in zip(low, high)]
        for a in range(half):
            send_ref[a * states + v] = other[a]
            keep_ref[a * states + v] = mine[a]

        @pl.when(step < half)
        def _():
            for a in range(half):
                keep_ref[half * states + step * half + a] = other[a]

        @pl.when(step >= half)
        def _():
            for a in range(half):
                send_ref[half * states + (step - half) * half + a] = mine[a]

    return call(
        body,
        (states,),
        1,
        [
            pl.BlockSpec((1, ops, depth), lambda g, x: ((g + half * x[0]) % states, 0, 0)),
            whole(got.shape),
        ],
        [whole((count, *tile))] * 2,
        [f32(count, *tile)] * 2,
        SHORT,
    )(det, own, got)


def far_sum(det, keep, came, states, turned):
    count, rows, lanes = keep.shape
    half = states // 2
    back = half * states
    shape = (back, up(rows + 1, 16), lanes) if turned else (rows + 1, back, lanes)

    def body(x_ref, keep_ref, came_ref, back_ref, own_ref):
        x = x_ref[0]
        top = jnp.zeros((rows, lanes), jnp.float32)
        for a in range(half):
            for v in range(states):
                t = a * states + v
                tile = keep_ref[t] + came_ref[t]
                if turned:
                    back_ref[t, :rows] = tile
                else:
                    back_ref[:rows, t] = tile
                top = jnp.maximum(top, jnp.abs(tile))

                @pl.when(v // half == x)
                def _():
                    own_ref[v % half * states + half * x + a] = tile

        top = jnp.max(top, keepdims=True)
        if turned:
            back_ref[0, rows:] = jnp.broadcast_to(top, (shape[1] - rows, lanes))
        else:
            back_ref[rows] = jnp.broadcast_to(top, (back, lanes))
        for b in range(half):
            for a in range(half):
                t = back + b * half + a
                own_ref[b * states + half * (1 - x) + a] = keep_ref[t] + came_ref[t]

    return call(
        body,
        (1,),
        1,
        [whole((count, rows, lanes))] * 2,
        [whole(shape), whole((back, rows, lanes))],
        [f32(*shape), f32(back, rows, lanes)],
        LONG,
    )(det, keep, came)


def squared(sums, axis, rows):
    largest = sums[0, rows, 0] if axis else sums[rows, 0, 0]
    exponent = jnp.floor(jnp.log2(jnp.maximum(largest, 2.0**-120)))
    scaled = sums * jnp.exp2(-exponent)
    row = lax.broadcasted_iota(jnp.int32, sums.shape, axis)
    return jnp.where(row < rows, scaled * jnp.abs(scaled) * SQUARE_TOP, exponent).astype(jnp.float16)


def rooted(code, axis, rows):
    exponent = (code[0, rows, 0] if axis else code[rows, 0, 0]).astype(jnp.float32)
    values = lax.slice_in_dim(code, 0, rows, axis=axis).astype(jnp.float32)
    root = jnp.sqrt(jnp.abs(values)) * (jnp.exp2(exponent) * SQUARE_TOP**-0.5)
    return jnp.where(values < 0, -root, root)


def place(receiver, out, owned, came):
    _, ops, tiles, _ = out.shape
    full = len(came)
    wide = full * LANES

    def body(role_ref, out_in, *refs):
        owned_refs, came_refs, out_ref = refs[: full + 1], refs[full + 1 : -1], refs[-1]

        @pl.when(role_ref[0] == 1)
        def _():
            for t in range(tiles):
                for k in range(full):
                    out_ref[0, :, t, k * LANES : (k + 1) * LANES] = owned_refs[k][t]
                out_ref[0, :, t, wide:] = owned_refs[full][t].T

        for k in range(full):

            @pl.when((role_ref[0] == 0) & (pl.program_id(0) == k))
            def _():
                for t in range(tiles):
                    out_ref[0, :, t] = came_refs[k][t].T

    return call(
        body,
        (pl.cdiv(ops, LANES),),
        1,
        [pl.BlockSpec(memory_space=pl.ANY)]
        + [pl.BlockSpec((tiles, LANES, LANES), lambda i, r: (0, i, 0))] * full
        + [pl.BlockSpec((tiles, ops - wide, LANES), lambda i, r: (0, 0, i))]
        + [whole((tiles, ops, LANES))] * full,
        pl.BlockSpec((1, LANES, tiles, ops), lambda i, r: (0, i, 0, 0)),
        f32(*out.shape),
        LONG,
        {1: 0},
    )(receiver, out, *owned, *came)


def finish(receiver, out, last):
    _, ops, tiles, _ = out.shape
    rest = last.shape[0]

    def body(role_ref, out_in, last_ref, out_ref, sem):
        @pl.when(role_ref[0] == 0)
        def _():
            copy = pltpu.make_async_copy(last_ref, out_ref.at[0, pl.ds(ops - rest, rest)], sem)
            copy.start()
            copy.wait()

    return pl.pallas_call(
        body,
        in_specs=[pl.BlockSpec(memory_space=pltpu.SMEM)] + [pl.BlockSpec(memory_space=pl.ANY)] * 2,
        out_specs=pl.BlockSpec(memory_space=pl.ANY),
        out_shape=f32(*out.shape),
        input_output_aliases={1: 0},
        scratch_shapes=[pltpu.SemaphoreType.DMA],
        cost_estimate=pl.CostEstimate(flops=0, bytes_accessed=SHORT, transcendentals=0),
    )(receiver, out, last)


def paired(amplitudes):
    blocks = lax.axis_size("state")
    far = blocks.bit_length() - 2
    states, depth, ops = amplitudes.shape
    full = ops // LANES
    wide = full * LANES
    both = ("state", "det")
    senders = [s for s in range(blocks) if (s & 1) == (s >> far & 1)]
    receivers = [s for s in range(blocks) if s not in senders]
    over = [(2 * s + x, 2 * (s ^ 1 << far) + x) for s in senders for x in range(2)]
    back = [(b, a) for a, b in over]
    across = [(2 * s + x, 2 * s + 1 - x) for s in receivers for x in range(2)]

    state = lax.axis_index("state")
    det = lax.axis_index("det").astype(jnp.int32)[None]
    receiver = ((state & 1) ^ (state >> far & 1)).astype(jnp.int32)[None]

    partner = lax.ppermute(amplitudes, "state", [(s, s ^ 1) for s in range(blocks)])
    chunks, seen = [], amplitudes
    for k in range(full + 1):
        chunk = seen[:, :, k * LANES : (k + 1) * LANES].transpose(0, 2, 1)
        if k == full:
            chunk = chunk.reshape(states * (ops - wide), depth)
        seen = after(amplitudes, chunk)
        chunks.append(chunk)
    got = [lax.ppermute(c, both, over) for c in chunks]

    own = seen.transpose(0, 2, 1)
    partner = after(partner, own).transpose(0, 2, 1)
    main, rest = near_send(det, own, partner)
    keep = near_keep(after(det, main), own, partner)
    main, rest = (lax.ppermute(v, "det", [(0, 1), (1, 0)]) for v in (main, rest))

    def terms(k, done):
        send, kept = far_terms(after(det, done), own, got[k], k < full)
        return lax.ppermute(send, both, across), kept

    def sums(k, pair, done):
        came, kept = pair
        axis, rows = int(k < full), kept.shape[1]
        home, mine = far_sum(after(det, done), kept, came, states, k < full)
        sent = squared(home, axis, rows)
        return sent, mine, lax.ppermute(sent, both, back), axis, rows

    pairs, done = [], keep
    for k in range(full + 1):
        pairs.append(terms(k, done))
        done = pairs[k][1]
    out = near_sum(after(keep, done), main, rest)
    done, codes = out, []
    for k in range(full + 1):
        codes.append(sums(k, pairs[k], done))
        done = codes[k][0]

    returned = [rooted(*c[2:]) for c in codes[:full]]
    out = place(after(receiver, done), out, [c[1] for c in codes], returned)
    out = finish(receiver, out, rooted(after(codes[full][2], out), *codes[full][3:]))
    return out.transpose(0, 2, 1, 3)


def partner_2(value, axis, stride):
    mask = 2**stride
    pairs = [(source, source ^ mask) for source in range(lax.axis_size(axis))]
    return lax.ppermute(value, axis, pairs)


def pair_terms(own_block, partner, count):
    operators = own_block.shape[2]
    terms = jnp.einsum("adp,bdq->abpq", own_block, partner, preferred_element_type=jnp.float32)
    return terms.reshape(count, operators, operators)


def exchanged(amplitudes):
    blocks = lax.axis_size("state")
    far_bit = blocks.bit_length() - 2
    states = amplitudes.shape[0]
    gathered = []
    for bit in (far_bit, 0):
        partner = partner_2(amplitudes, "state", bit)
        terms = pair_terms(amplitudes, partner, states * states)
        gathered.append(lax.psum_scatter(terms, "det", scatter_dimension=0, tiled=True))
    return jnp.stack(gathered)


def on_device(amplitudes):
    states, _, ops = amplitudes.shape
    two = lax.axis_size("det") == 2 and lax.axis_size("state") >= 4
    if two and states % 2 == 0 and ops > LANES and ops % LANES % 8:
        return paired(amplitudes)
    return exchanged(amplitudes)


def solution(mesh):
    return jax.shard_map(
        on_device,
        mesh=mesh,
        in_specs=(P("state", "det", None),),
        out_specs=P(None, ("state", "det"), None, None),
        check_vma=False,
    )
```

```python
import functools

import jax
import jax.numpy as jnp
from jax import lax
from jax.experimental import pallas as pl
from jax.experimental.pallas import tpu as pltpu
from jax.sharding import PartitionSpec as P

LANES = 128
VMEM_LIMIT = 40 * 2**20
SQUARE_TOP = 2.0**13
SMALLEST = 2.0**-120


def contract_last(left, right):
    return lax.dot_general(left, right, (((1,), (1,)), ((), ())), preferred_element_type=jnp.float32)


def call(body, grid, scalars, in_specs, out_specs, out_shape, after=(), aliases={}):
    idle = len(after)

    def waiting(*refs):
        first = scalars + len(in_specs)
        body(*refs[:first], *refs[first + idle :])

    kernel = pl.pallas_call(
        waiting,
        grid_spec=pltpu.PrefetchScalarGridSpec(
            num_scalar_prefetch=scalars,
            grid=grid,
            in_specs=in_specs + [pl.BlockSpec(memory_space=pl.ANY)] * idle,
            out_specs=out_specs,
        ),
        out_shape=out_shape,
        input_output_aliases=aliases,
        compiler_params=pltpu.CompilerParams(vmem_limit_bytes=VMEM_LIMIT),
    )
    return lambda *operands: kernel(*operands, *after)


def f32(*shape):
    return jax.ShapeDtypeStruct(shape, jnp.float32)


def up(size, unit):
    return -(-size // unit) * unit


def whole(shape):
    return pl.BlockSpec(shape, lambda *_: (0,) * len(shape))


class Packing:
    def __init__(self, tiles, ops):
        self.ops, self.wide = ops, ops // LANES * LANES
        self.rest, self.below = ops - self.wide, up(ops, 8)
        self.each = self.below + up(self.rest, 8)
        beside = self.wide // LANES
        self.corners = [
            (tiles * self.each + t // beside * up(self.rest, 8), t % beside * LANES) for t in range(tiles)
        ]
        self.shape = (tiles * self.each + pl.cdiv(tiles, beside) * up(self.rest, 8), self.wide)

    def store(self, wire_ref, t, main, turned):
        row, lane = self.corners[t]
        wire_ref[t * self.each : t * self.each + self.ops] = main
        start = t * self.each + self.below
        wire_ref[start : start + self.rest] = turned[:, : self.wide]
        wire_ref[row : row + self.rest, lane : lane + self.rest] = turned[:, self.wide :]

    def parts(self, wire_ref, t):
        row, lane = self.corners[t]
        start, padded = t * self.each + self.below, up(self.rest, 8)
        head, tail = slice(0, self.wide), slice(self.wide, self.ops)
        side = wire_ref[start : start + padded].T[:, : self.rest]
        corner = wire_ref[row : row + padded, lane : lane + LANES].T[: self.rest, : self.rest]
        main = wire_ref[t * self.each : t * self.each + self.ops]
        return [(slice(0, self.ops), head, main), (head, tail, side), (tail, tail, corner)]


def near_send(det, own, partner, to_mine, after=()):
    states, ops, depth = own.shape
    half, tiles = states // 2, (states // 2) ** 2
    packing = Packing(tiles, ops)

    def body(x_ref, own_ref, partner_ref, wire_ref):
        main = contract_last(own_ref[0], partner_ref[0, : packing.wide])
        turned = contract_last(partner_ref[0, packing.wide :], own_ref[0])
        for t in range(tiles):

            @pl.when(pl.program_id(0) == t)
            def _():
                packing.store(wire_ref, t, main, turned)

    def second(x):
        return half * (1 - x[0]) if to_mine else half * x[0]

    return call(
        body,
        (tiles,),
        1,
        [
            pl.BlockSpec((1, ops, depth), lambda t, x: (half * (1 - x[0]) + t // half, 0, 0)),
            pl.BlockSpec((1, ops, depth), lambda t, x: (second(x) + t % half, 0, 0)),
        ],
        whole(packing.shape),
        f32(*packing.shape),
        after,
    )(det, own, partner)


def near_keep(det, own, partner, after=()):
    states, ops, depth = own.shape
    half = states // 2

    def body(x_ref, own_ref, partner_ref, tile_ref):
        tile_ref[0] = contract_last(own_ref[0], partner_ref[0])

    return call(
        body,
        (half, states),
        1,
        [
            pl.BlockSpec((1, ops, depth), lambda a, b, x: (half * x[0] + a, 0, 0)),
            pl.BlockSpec((1, ops, depth), lambda a, b, x: (b, 0, 0)),
        ],
        pl.BlockSpec((1, ops, ops), lambda a, b, x: (a * states + b, 0, 0)),
        f32(half * states, ops, ops),
        after,
    )(det, own, partner)


def near_share(det, keep, doubled, states, after=()):
    _, ops, _ = keep.shape
    half, tiles = states // 2, (states // 2) ** 2
    packing = Packing(tiles, ops)
    shape = (tiles, up(ops, 8), up(ops, LANES))

    def body(x_ref, keep_ref, wire_ref, tile_ref):
        for t in range(tiles):
            kept = t // half * states + half * x_ref[0] + t % half
            for rows, columns, values in packing.parts(wire_ref, t):
                tile_ref[t, rows, columns] = keep_ref[kept, rows, columns] + values

    return call(
        body, (1,), 1, [whole(keep.shape), whole(packing.shape)], whole(shape), f32(*shape), after
    )(det, keep, doubled)


def near_sum(place_in, keep, crossed, share, given, states, after=()):
    tiles, ops, _ = keep.shape
    half = states // 2
    packing = Packing(half * half, ops)

    def body(s_ref, keep_ref, wire_ref, share_ref, given_ref, out_ref):
        x, core = s_ref[0], s_ref[1]
        for a in range(half):
            for b in range(states):
                t, one, turned = a * states + b, a * half + b % half, b % half * half + a

                @pl.when(b // half != x)
                def _():
                    for rows, columns, values in packing.parts(wire_ref, one):
                        out_ref[0, rows, t, columns] = keep_ref[t, rows, columns] + values

                @pl.when((b // half == x) & (core == 0))
                def _():
                    out_ref[0, :, t] = share_ref[one, :ops, :ops]

                @pl.when((b // half == x) & (core == 1))
                def _():
                    out_ref[0, :, t] = given_ref[turned].T[:ops, :ops]

    return call(
        body,
        (1,),
        1,
        [whole(keep.shape), whole(packing.shape), whole(share.shape), whole(given.shape)],
        pl.BlockSpec((1, ops, tiles, ops), lambda i, s: (1, 0, 0, 0)),
        f32(2, ops, tiles, ops),
        after,
    )(place_in, keep, crossed, share, given)


def far_terms(det, own, got, turned, mine, after=()):
    states, ops, depth = own.shape
    half = states // 2
    width = got.size // (states * depth)
    rows = ops if turned else width
    tile = (up(ops, 8), width) if turned else (up(width, 8), ops)

    def body(x_ref, own_ref, got_ref, out_ref):
        if turned:
            every = contract_last(own_ref[0], got_ref[...].reshape(states * width, depth))
        else:
            every = contract_last(got_ref[...], own_ref[0])
        for u in range(states):
            part = slice(u * width, (u + 1) * width)
            out_ref[u, :rows] = every[:, part] if turned else every[part]

    def state(b, x):
        return ((half * x[0] if mine else half * (1 - x[0])) + b, 0, 0)

    return call(
        body,
        (half,),
        1,
        [pl.BlockSpec((1, ops, depth), state), whole(got.shape)],
        pl.BlockSpec((states, *tile), lambda b, x: (b, 0, 0)),
        f32(half * states, *tile),
        after,
    )(det, own, got)


def far_sum(det, keep, came, states, rows, turned, after=()):
    tiles, padded, lanes = keep.shape
    half = states // 2
    shape = (half * half, up(rows + 1, 16), lanes) if turned else (rows + 1, half * half, lanes)

    def body(x_ref, keep_ref, came_ref, own_ref, straight_ref, across_ref):
        x = x_ref[0]
        top = jnp.zeros((rows, lanes), jnp.float32)
        for t in range(tiles):
            tile = keep_ref[t, :rows] + came_ref[t, :rows]
            own_ref[t] = tile
            top = jnp.maximum(top, jnp.abs(tile))
        exponent = jnp.floor(jnp.log2(jnp.maximum(jnp.max(top, keepdims=True), SMALLEST)))
        scale = jnp.exp2(-exponent)
        for to_ref, first in ((straight_ref, half * x), (across_ref, half * (1 - x))):
            for a in range(half):
                for b in range(half):
                    scaled = own_ref[b * states + first + a] * scale
                    code = scaled * jnp.abs(scaled) * SQUARE_TOP
                    if turned:
                        to_ref[a * half + b, :rows] = code
                        to_ref[a * half + b, rows:] = jnp.broadcast_to(exponent, (shape[1] - rows, lanes))
                    else:
                        to_ref[:rows, a * half + b] = code
            if not turned:
                to_ref[rows] = jnp.broadcast_to(exponent, (half * half, lanes))

    return call(
        body,
        (1,),
        1,
        [whole((tiles, padded, lanes))] * 2,
        [whole((tiles, rows, lanes)), whole(shape), whole(shape)],
        [f32(tiles, rows, lanes), f32(*shape), f32(*shape)],
        after,
    )(det, keep, came)


def decoded(values, exponent):
    root = jnp.sqrt(jnp.abs(values)) * (jnp.exp2(exponent) * SQUARE_TOP**-0.5)
    return jnp.where(values < 0, -root, root)


def place(place_in, out, owned, came, states, after=()):
    _, ops, tiles, _ = out.shape
    full, half = len(came), states // 2
    wide = full * LANES
    code = came[0][0].shape

    def body(s_ref, out_in, *refs):
        owned_refs, came_refs, out_ref = refs[: full + 1], refs[full + 1 : -1], refs[-1]
        x = s_ref[0]

        @pl.when(s_ref[1] == 1)
        def _():
            for t in range(tiles):
                for k in range(full):
                    out_ref[0, :, t, k * LANES : (k + 1) * LANES] = owned_refs[k][t]
                out_ref[0, :, t, wide:] = owned_refs[full][t].T

        for k in range(full):
            straight, across = came_refs[2 * k : 2 * k + 2]

            @pl.when((s_ref[1] == 0) & (pl.program_id(0) == k))
            def _():
                for a in range(half):
                    for v in range(states):
                        one = a * half + v % half
                        block = jnp.where(v // half == x, straight[one], across[one])
                        tile = decoded(block[:ops], block[ops : ops + 1])
                        out_ref[0, :, a * states + v] = tile.T

    return call(
        body,
        (pl.cdiv(ops, LANES),),
        1,
        [pl.BlockSpec(memory_space=pl.ANY)]
        + [pl.BlockSpec((tiles, LANES, LANES), lambda i, s: (0, i, 0))] * full
        + [pl.BlockSpec((tiles, ops - wide, LANES), lambda i, s: (0, 0, i))]
        + [whole(code)] * (2 * full),
        pl.BlockSpec((1, LANES, tiles, ops), lambda i, s: (0, i, 0, 0)),
        f32(*out.shape),
        after,
        {1: 0},
    )(place_in, out, *owned, *[c for pair in came for c in pair])


def finish(place_in, out, straight, across, states):
    _, ops, tiles, _ = out.shape
    rest, half = straight.shape[0] - 1, states // 2

    def body(s_ref, out_in, straight_ref, across_ref, out_ref, rows_ref, sem):
        x = s_ref[0]

        @pl.when(s_ref[1] == 0)
        def _():
            for a in range(half):
                for v in range(states):
                    one = a * half + v % half
                    block = jnp.where(v // half == x, straight_ref[:, one], across_ref[:, one])
                    rows_ref[:, a * states + v] = decoded(block[:rest], block[rest:])
            copy = pltpu.make_async_copy(rows_ref, out_ref.at[0, pl.ds(ops - rest, rest)], sem)
            copy.start()
            copy.wait()

    return pl.pallas_call(
        body,
        in_specs=[
            pl.BlockSpec(memory_space=pltpu.SMEM),
            pl.BlockSpec(memory_space=pl.ANY),
            pl.BlockSpec(memory_space=pltpu.VMEM),
            pl.BlockSpec(memory_space=pltpu.VMEM),
        ],
        out_specs=pl.BlockSpec(memory_space=pl.ANY),
        out_shape=f32(*out.shape),
        input_output_aliases={1: 0},
        scratch_shapes=[pltpu.VMEM((rest, tiles, ops), jnp.float32), pltpu.SemaphoreType.DMA],
    )(place_in, out, straight, across)


def paired(amplitudes):
    blocks = lax.axis_size("state")
    far = blocks.bit_length() - 2
    states, depth, ops = amplitudes.shape
    full = ops // LANES
    wide = full * LANES
    both = ("state", "det")
    senders = [s for s in range(blocks) if (s & 1) == (s >> far & 1)]
    receivers = [s for s in range(blocks) if s not in senders]
    over = [(2 * s + x, 2 * (s ^ 1 << far) + x) for s in senders for x in range(2)]
    straight = [(b, a) for a, b in over]
    diagonal = [(b, a ^ 1) for a, b in over]
    across = [(2 * s + x, 2 * s + 1 - x) for s in receivers for x in range(2)]
    first_across = [(2 * s + x, 2 * s + 1 - x) for s in range(0, blocks, 2) for x in range(2)]
    to_second = [(2 * s + x, 2 * (s + 1) + x) for s in range(0, blocks, 2) for x in range(2)]

    state = lax.axis_index("state")
    x = lax.axis_index("det").astype(jnp.int32)
    det = x[None]
    receiver = ((state & 1) ^ (state >> far & 1)).astype(jnp.int32)
    core = (state & 1).astype(jnp.int32)

    partner = lax.ppermute(amplitudes, "state", [(s, s ^ 1) for s in range(blocks)])
    chunks = [amplitudes[:, :, :LANES].transpose(0, 2, 1)]
    chunks[0], later = lax.optimization_barrier((chunks[0], amplitudes))
    own = later.transpose(0, 2, 1)
    chunks += [own[:, k * LANES : (k + 1) * LANES] for k in range(1, full)]
    chunks.append(own[:, wide:].reshape(states * (ops - wide), depth))
    got = [lax.ppermute(c, both, over) for c in chunks]

    partner, own = lax.optimization_barrier((partner, own))
    partner = partner.transpose(0, 2, 1)
    crossed = near_send(det, own, partner, False, tuple(chunks[1:]))
    doubled = near_send(det, own, partner, True, (crossed,))
    keep = near_keep(det, own, partner, (doubled,))
    crossed = lax.ppermute(crossed, "det", [(0, 1), (1, 0)])
    doubled = lax.ppermute(doubled, both, first_across)

    def partials(k, done):
        send = far_terms(det, own, got[k], k < full, False, done)
        return send, far_terms(det, own, got[k], k < full, True, (send,))

    def finished(k, kept, came, done):
        rows = ops if k < full else ops - wide
        mine, *pair = far_sum(det, kept, came, states, rows, k < full, done)
        return mine, [v.astype(jnp.float16) for v in pair]

    def returned(pair):
        return [lax.ppermute(v, both, to) for v, to in zip(pair, (straight, diagonal))]

    owned, codes, done = [], [], keep
    for k in range(full):
        send, kept = partials(k, (done,))
        came = lax.ppermute(send, both, across)
        done = kept
        if k == 1:
            done = share = near_share(det, keep, doubled, states, (kept, crossed))
            given = lax.ppermute(share, both, to_second)
        done, pair = finished(k, kept, came, (done,))
        owned.append(done)
        codes.append(pair)
    codes[0] = [v.astype(jnp.float32) for v in returned(codes[0])]
    send, kept = partials(full, (done, *codes[0]))
    came = lax.ppermute(send, both, across)
    out = near_sum(jnp.stack([x, core]), keep, crossed, share, given, states, (kept,))
    mine, pair = finished(full, kept, came, (out,))
    owned.append(mine)
    codes[1:] = [returned(c) for c in codes[1:] + [pair]]

    at = jnp.stack([x, receiver])
    codes[1:full] = [[v.astype(jnp.float32) for v in c] for c in codes[1:full]]
    out = place(at, out, owned, codes[:full], states)
    *last, out = lax.optimization_barrier((*codes[full], out))
    return finish(at, out, *[v.astype(jnp.float32) for v in last], states).transpose(0, 2, 1, 3)


def partner_2(value, axis, stride):
    mask = 2**stride
    pairs = [(source, source ^ mask) for source in range(lax.axis_size(axis))]
    return lax.ppermute(value, axis, pairs)


def pair_terms(own_block, partner, count):
    operators = own_block.shape[2]
    terms = jnp.einsum("adp,bdq->abpq", own_block, partner, preferred_element_type=jnp.float32)
    return terms.reshape(count, operators, operators)


def exchanged(amplitudes):
    blocks = lax.axis_size("state")
    far_bit = blocks.bit_length() - 2
    states = amplitudes.shape[0]
    gathered = []
    for bit in (far_bit, 0):
        partner = partner_2(amplitudes, "state", bit)
        terms = pair_terms(amplitudes, partner, states * states)
        gathered.append(lax.psum_scatter(terms, "det", scatter_dimension=0, tiled=True))
    return jnp.stack(gathered)


def on_device(amplitudes):
    states, _, ops = amplitudes.shape
    two = lax.axis_size("det") == 2 and lax.axis_size("state") >= 4
    if two and states % 2 == 0 and ops > LANES and ops % LANES % 8:
        return paired(amplitudes)
    return exchanged(amplitudes)


def solution(mesh):
    return jax.shard_map(
        on_device,
        mesh=mesh,
        in_specs=(P("state", "det", None),),
        out_specs=P(None, ("state", "det"), None, None),
        check_vma=False,
    )
```

```python
import functools

import jax
import jax.numpy as jnp
from jax import lax
from jax.experimental import pallas as pl
from jax.experimental.pallas import tpu as pltpu
from jax.sharding import PartitionSpec as P

LANES = 128
VMEM_LIMIT = 40 * 2**20
SQUARE_TOP = 2.0**13
SMALLEST = 2.0**-120


def contract_last(left, right):
    return lax.dot_general(left, right, (((1,), (1,)), ((), ())), preferred_element_type=jnp.float32)


def call(body, grid, scalars, in_specs, out_specs, out_shape, after=(), aliases={}):
    idle = len(after)

    def waiting(*refs):
        first = scalars + len(in_specs)
        body(*refs[:first], *refs[first + idle :])

    kernel = pl.pallas_call(
        waiting,
        grid_spec=pltpu.PrefetchScalarGridSpec(
            num_scalar_prefetch=scalars,
            grid=grid,
            in_specs=in_specs + [pl.BlockSpec(memory_space=pl.ANY)] * idle,
            out_specs=out_specs,
        ),
        out_shape=out_shape,
        input_output_aliases=aliases,
        compiler_params=pltpu.CompilerParams(vmem_limit_bytes=VMEM_LIMIT),
    )
    return lambda *operands: kernel(*operands, *after)


def f32(*shape):
    return jax.ShapeDtypeStruct(shape, jnp.float32)


def up(size, unit):
    return -(-size // unit) * unit


def whole(shape):
    return pl.BlockSpec(shape, lambda *_: (0,) * len(shape))


class Packing:
    def __init__(self, tiles, ops):
        self.ops, self.wide = ops, ops // LANES * LANES
        self.rest, self.below = ops - self.wide, up(ops, 8)
        self.each = self.below + up(self.rest, 8)
        beside = self.wide // LANES
        self.corners = [
            (tiles * self.each + t // beside * up(self.rest, 8), t % beside * LANES) for t in range(tiles)
        ]
        self.shape = (tiles * self.each + pl.cdiv(tiles, beside) * up(self.rest, 8), self.wide)

    def store(self, wire_ref, t, main, turned):
        row, lane = self.corners[t]
        wire_ref[t * self.each : t * self.each + self.ops] = main
        start = t * self.each + self.below
        wire_ref[start : start + self.rest] = turned[:, : self.wide]
        wire_ref[row : row + self.rest, lane : lane + self.rest] = turned[:, self.wide :]

    def parts(self, wire_ref, t):
        row, lane = self.corners[t]
        start, padded = t * self.each + self.below, up(self.rest, 8)
        head, tail = slice(0, self.wide), slice(self.wide, self.ops)
        side = wire_ref[start : start + padded].T[:, : self.rest]
        corner = wire_ref[row : row + padded, lane : lane + LANES].T[: self.rest, : self.rest]
        main = wire_ref[t * self.each : t * self.each + self.ops]
        return [(slice(0, self.ops), head, main), (head, tail, side), (tail, tail, corner)]


def near_send(det, own, partner, to_mine, after=()):
    states, ops, depth = own.shape
    half, tiles = states // 2, (states // 2) ** 2
    packing = Packing(tiles, ops)

    def body(x_ref, own_ref, partner_ref, wire_ref):
        main = contract_last(own_ref[0], partner_ref[0, : packing.wide])
        turned = contract_last(partner_ref[0, packing.wide :], own_ref[0])
        for t in range(tiles):

            @pl.when(pl.program_id(0) == t)
            def _():
                packing.store(wire_ref, t, main, turned)

    def second(x):
        return half * (1 - x[0]) if to_mine else half * x[0]

    return call(
        body,
        (tiles,),
        1,
        [
            pl.BlockSpec((1, ops, depth), lambda t, x: (half * (1 - x[0]) + t // half, 0, 0)),
            pl.BlockSpec((1, ops, depth), lambda t, x: (second(x) + t % half, 0, 0)),
        ],
        whole(packing.shape),
        f32(*packing.shape),
        after,
    )(det, own, partner)


def near_keep(det, own, partner, after=()):
    states, ops, depth = own.shape
    half = states // 2

    def body(x_ref, own_ref, partner_ref, tile_ref):
        tile_ref[0] = contract_last(own_ref[0], partner_ref[0])

    return call(
        body,
        (half, states),
        1,
        [
            pl.BlockSpec((1, ops, depth), lambda a, b, x: (half * x[0] + a, 0, 0)),
            pl.BlockSpec((1, ops, depth), lambda a, b, x: (b, 0, 0)),
        ],
        pl.BlockSpec((1, ops, ops), lambda a, b, x: (a * states + b, 0, 0)),
        f32(half * states, ops, ops),
        after,
    )(det, own, partner)


def near_share(det, keep, doubled, states, after=()):
    _, ops, _ = keep.shape
    half, tiles = states // 2, (states // 2) ** 2
    packing = Packing(tiles, ops)
    shape = (tiles, up(ops, 8), up(ops, LANES))

    def body(x_ref, keep_ref, wire_ref, tile_ref):
        for t in range(tiles):
            kept = t // half * states + half * x_ref[0] + t % half
            for rows, columns, values in packing.parts(wire_ref, t):
                tile_ref[t, rows, columns] = keep_ref[kept, rows, columns] + values

    return call(
        body, (1,), 1, [whole(keep.shape), whole(packing.shape)], whole(shape), f32(*shape), after
    )(det, keep, doubled)


def near_sum(place_in, keep, crossed, share, given, states, after=()):
    tiles, ops, _ = keep.shape
    half = states // 2
    packing = Packing(half * half, ops)

    def body(s_ref, keep_ref, wire_ref, share_ref, given_ref, out_ref):
        x, core = s_ref[0], s_ref[1]
        for a in range(half):
            for b in range(states):
                t, one, turned = a * states + b, a * half + b % half, b % half * half + a

                @pl.when(b // half != x)
                def _():
                    for rows, columns, values in packing.parts(wire_ref, one):
                        out_ref[0, rows, t, columns] = keep_ref[t, rows, columns] + values

                @pl.when((b // half == x) & (core == 0))
                def _():
                    out_ref[0, :, t] = share_ref[one, :ops, :ops]

                @pl.when((b // half == x) & (core == 1))
                def _():
                    out_ref[0, :, t] = given_ref[turned].T[:ops, :ops]

    return call(
        body,
        (1,),
        1,
        [whole(keep.shape), whole(packing.shape), whole(share.shape), whole(given.shape)],
        pl.BlockSpec((1, ops, tiles, ops), lambda i, s: (1, 0, 0, 0)),
        f32(2, ops, tiles, ops),
        after,
    )(place_in, keep, crossed, share, given)


def far_terms(det, own, got, start, width, turned, mine, after=()):
    states, ops, depth = own.shape
    half = states // 2
    rows = ops if turned else width
    tile = (up(ops, 8), width) if turned else (up(width, 8), ops)

    def body(x_ref, own_ref, got_ref, out_ref):
        rows_in = got_ref[start : start + states * width]
        every = contract_last(own_ref[0], rows_in) if turned else contract_last(rows_in, own_ref[0])
        for u in range(states):
            part = slice(u * width, (u + 1) * width)
            out_ref[u, :rows] = every[:, part] if turned else every[part]

    def state(b, x):
        return ((half * x[0] if mine else half * (1 - x[0])) + b, 0, 0)

    return call(
        body,
        (half,),
        1,
        [pl.BlockSpec((1, ops, depth), state), whole(got.shape)],
        pl.BlockSpec((states, *tile), lambda b, x: (b, 0, 0)),
        f32(half * states, *tile),
        after,
    )(det, own, got)


def far_sum(det, keep, came, states, rows, turned, after=()):
    tiles, padded, lanes = keep.shape
    half = states // 2
    shape = (half * half, up(rows + 1, 16), lanes) if turned else (rows + 1, half * half, lanes)

    def body(x_ref, keep_ref, came_ref, own_ref, straight_ref, across_ref):
        x = x_ref[0]
        top = jnp.zeros((rows, lanes), jnp.float32)
        for t in range(tiles):
            tile = keep_ref[t, :rows] + came_ref[t, :rows]
            own_ref[t] = tile
            top = jnp.maximum(top, jnp.abs(tile))
        exponent = jnp.floor(jnp.log2(jnp.maximum(jnp.max(top, keepdims=True), SMALLEST)))
        scale = jnp.exp2(-exponent)
        for to_ref, first in ((straight_ref, half * x), (across_ref, half * (1 - x))):
            for a in range(half):
                for b in range(half):
                    scaled = own_ref[b * states + first + a] * scale
                    code = scaled * jnp.abs(scaled) * SQUARE_TOP
                    if turned:
                        to_ref[a * half + b, :rows] = code
                        to_ref[a * half + b, rows:] = jnp.broadcast_to(exponent, (shape[1] - rows, lanes))
                    else:
                        to_ref[:rows, a * half + b] = code
            if not turned:
                to_ref[rows] = jnp.broadcast_to(exponent, (half * half, lanes))

    return call(
        body,
        (1,),
        1,
        [whole((tiles, padded, lanes))] * 2,
        [whole((tiles, rows, lanes)), whole(shape), whole(shape)],
        [f32(tiles, rows, lanes), f32(*shape), f32(*shape)],
        after,
    )(det, keep, came)


def decoded(values, exponent):
    root = jnp.sqrt(jnp.abs(values)) * (jnp.exp2(exponent) * SQUARE_TOP**-0.5)
    return jnp.where(values < 0, -root, root)


def place(place_in, out, owned, came, states, after=()):
    _, ops, tiles, _ = out.shape
    full, half = len(came), states // 2
    wide = full * LANES
    code = came[0][0].shape

    def body(s_ref, out_in, *refs):
        owned_refs, came_refs, out_ref = refs[: full + 1], refs[full + 1 : -1], refs[-1]
        x = s_ref[0]

        @pl.when(s_ref[1] == 1)
        def _():
            for t in range(tiles):
                for k in range(full):
                    out_ref[0, :, t, k * LANES : (k + 1) * LANES] = owned_refs[k][t]
                out_ref[0, :, t, wide:] = owned_refs[full][t].T

        for k in range(full):
            straight, across = came_refs[2 * k : 2 * k + 2]

            @pl.when((s_ref[1] == 0) & (pl.program_id(0) == k))
            def _():
                for a in range(half):
                    for v in range(states):
                        one = a * half + v % half
                        block = jnp.where(v // half == x, straight[one], across[one])
                        tile = decoded(block[:ops], block[ops : ops + 1])
                        out_ref[0, :, a * states + v] = tile.T

    return call(
        body,
        (pl.cdiv(ops, LANES),),
        1,
        [pl.BlockSpec(memory_space=pl.ANY)]
        + [pl.BlockSpec((tiles, LANES, LANES), lambda i, s: (0, i, 0))] * full
        + [pl.BlockSpec((tiles, ops - wide, LANES), lambda i, s: (0, 0, i))]
        + [whole(code)] * (2 * full),
        pl.BlockSpec((1, LANES, tiles, ops), lambda i, s: (0, i, 0, 0)),
        f32(*out.shape),
        after,
        {1: 0},
    )(place_in, out, *owned, *[c for pair in came for c in pair])


def finish(place_in, out, straight, across, states):
    _, ops, tiles, _ = out.shape
    rest, half = straight.shape[0] - 1, states // 2

    def body(s_ref, out_in, straight_ref, across_ref, out_ref, rows_ref, sem):
        x = s_ref[0]

        @pl.when(s_ref[1] == 0)
        def _():
            for a in range(half):
                for v in range(states):
                    one = a * half + v % half
                    block = jnp.where(v // half == x, straight_ref[:, one], across_ref[:, one])
                    rows_ref[:, a * states + v] = decoded(block[:rest], block[rest:])
            copy = pltpu.make_async_copy(rows_ref, out_ref.at[0, pl.ds(ops - rest, rest)], sem)
            copy.start()
            copy.wait()

    return pl.pallas_call(
        body,
        in_specs=[
            pl.BlockSpec(memory_space=pltpu.SMEM),
            pl.BlockSpec(memory_space=pl.ANY),
            pl.BlockSpec(memory_space=pltpu.VMEM),
            pl.BlockSpec(memory_space=pltpu.VMEM),
        ],
        out_specs=pl.BlockSpec(memory_space=pl.ANY),
        out_shape=f32(*out.shape),
        input_output_aliases={1: 0},
        scratch_shapes=[pltpu.VMEM((rest, tiles, ops), jnp.float32), pltpu.SemaphoreType.DMA],
    )(place_in, out, straight, across)


def paired(amplitudes):
    blocks = lax.axis_size("state")
    far = blocks.bit_length() - 2
    states, depth, ops = amplitudes.shape
    full = ops // LANES
    wide = full * LANES
    both = ("state", "det")
    senders = [s for s in range(blocks) if (s & 1) == (s >> far & 1)]
    receivers = [s for s in range(blocks) if s not in senders]
    over = [(2 * s + x, 2 * (s ^ 1 << far) + x) for s in senders for x in range(2)]
    straight = [(b, a) for a, b in over]
    diagonal = [(b, a ^ 1) for a, b in over]
    across = [(2 * s + x, 2 * s + 1 - x) for s in receivers for x in range(2)]
    first_across = [(2 * s + x, 2 * s + 1 - x) for s in range(0, blocks, 2) for x in range(2)]
    to_second = [(2 * s + x, 2 * (s + 1) + x) for s in range(0, blocks, 2) for x in range(2)]

    state = lax.axis_index("state")
    x = lax.axis_index("det").astype(jnp.int32)
    det = x[None]
    receiver = ((state & 1) ^ (state >> far & 1)).astype(jnp.int32)
    core = (state & 1).astype(jnp.int32)

    partner = lax.ppermute(amplitudes, "state", [(s, s ^ 1) for s in range(blocks)])
    first = amplitudes[:, :, :LANES].transpose(0, 2, 1)
    first, later = lax.optimization_barrier((first, amplitudes))
    own = later.transpose(0, 2, 1)
    widths = [LANES] * full + [ops - wide]
    later = [own[:, k * LANES : k * LANES + w].reshape(states * w, depth) for k, w in enumerate(widths) if k]
    later = jnp.concatenate(later)
    first = lax.ppermute(first.reshape(states * LANES, depth), both, over)
    rest = lax.ppermute(later, both, over)

    partner, own = lax.optimization_barrier((partner, own))
    partner = partner.transpose(0, 2, 1)
    crossed = near_send(det, own, partner, False, (later,))
    doubled = near_send(det, own, partner, True, (crossed,))
    keep = near_keep(det, own, partner, (doubled,))
    crossed = lax.ppermute(crossed, "det", [(0, 1), (1, 0)])
    doubled = lax.ppermute(doubled, both, first_across)

    def partials(k, done):
        got, start = (rest, states * LANES * (k - 1)) if k else (first, 0)
        what = det, own, got, start, widths[k], k < full
        send = far_terms(*what, False, done)
        return lax.ppermute(send, both, across), send, far_terms(*what, True, (send,))

    def finished(k, came, kept, done):
        mine, *pair = far_sum(det, kept, came, states, ops if k < full else widths[k], k < full, done)
        return mine, [v.astype(jnp.float16) for v in pair]

    def returned(pair):
        return [lax.ppermute(v, both, to) for v, to in zip(pair, (straight, diagonal))]

    came, _, kept = partials(0, (keep,))
    mine, pair = finished(0, came, kept, ())
    owned, codes = [mine], [returned(pair)]
    share = near_share(det, keep, doubled, states, (mine, crossed))
    given = lax.ppermute(share, both, to_second)
    pending, done = [], share
    for k in range(1, full + 1):
        came, _, kept = partials(k, (done,))
        pending.append((came, kept))
        done = kept
    done = out = near_sum(jnp.stack([x, core]), keep, crossed, share, given, states, (done,))
    for k, (came, kept) in enumerate(pending, 1):
        done, pair = finished(k, came, kept, (done,))
        owned.append(done)
        codes.append(returned(pair))

    at = jnp.stack([x, receiver])
    codes[:full] = [[v.astype(jnp.float32) for v in c] for c in codes[:full]]
    out = place(at, out, owned, codes[:full], states)
    *last, out = lax.optimization_barrier((*codes[full], out))
    return finish(at, out, *[v.astype(jnp.float32) for v in last], states).transpose(0, 2, 1, 3)


def partner_2(value, axis, stride):
    mask = 2**stride
    pairs = [(source, source ^ mask) for source in range(lax.axis_size(axis))]
    return lax.ppermute(value, axis, pairs)


def pair_terms(own_block, partner, count):
    operators = own_block.shape[2]
    terms = jnp.einsum("adp,bdq->abpq", own_block, partner, preferred_element_type=jnp.float32)
    return terms.reshape(count, operators, operators)


def exchanged(amplitudes):
    blocks = lax.axis_size("state")
    far_bit = blocks.bit_length() - 2
    states = amplitudes.shape[0]
    gathered = []
    for bit in (far_bit, 0):
        partner = partner_2(amplitudes, "state", bit)
        terms = pair_terms(amplitudes, partner, states * states)
        gathered.append(lax.psum_scatter(terms, "det", scatter_dimension=0, tiled=True))
    return jnp.stack(gathered)


def on_device(amplitudes):
    states, _, ops = amplitudes.shape
    two = lax.axis_size("det") == 2 and lax.axis_size("state") >= 4
    if two and states % 2 == 0 and ops > LANES and ops % LANES % 8:
        return paired(amplitudes)
    return exchanged(amplitudes)


def solution(mesh):
    return jax.shard_map(
        on_device,
        mesh=mesh,
        in_specs=(P("state", "det", None),),
        out_specs=P(None, ("state", "det"), None, None),
        check_vma=False,
    )
```

```python
import functools

import jax
import jax.numpy as jnp
from jax import lax
from jax.experimental import pallas as pl
from jax.experimental.pallas import tpu as pltpu
from jax.sharding import PartitionSpec as P

LANES = 128
VMEM_LIMIT = 40 * 2**20
POWER, LIFT = 10, 11
SMALLEST = 2.0**-110


def contract_last(left, right):
    return lax.dot_general(left, right, (((1,), (1,)), ((), ())), preferred_element_type=jnp.float32)


def call(body, grid, scalars, in_specs, out_specs, out_shape, after=(), aliases={}):
    idle = len(after)

    def waiting(*refs):
        first = scalars + len(in_specs)
        body(*refs[:first], *refs[first + idle :])

    kernel = pl.pallas_call(
        waiting,
        grid_spec=pltpu.PrefetchScalarGridSpec(
            num_scalar_prefetch=scalars,
            grid=grid,
            in_specs=in_specs + [pl.BlockSpec(memory_space=pl.ANY)] * idle,
            out_specs=out_specs,
        ),
        out_shape=out_shape,
        input_output_aliases=aliases,
        compiler_params=pltpu.CompilerParams(vmem_limit_bytes=VMEM_LIMIT),
    )
    return lambda *operands: kernel(*operands, *after)


def f32(*shape):
    return jax.ShapeDtypeStruct(shape, jnp.float32)


def up(size, unit):
    return -(-size // unit) * unit


def whole(shape):
    return pl.BlockSpec(shape, lambda *_: (0,) * len(shape))


class Packing:
    def __init__(self, tiles, ops):
        self.ops, self.wide = ops, ops // LANES * LANES
        self.rest, self.below = ops - self.wide, up(ops, 8)
        self.each = self.below + up(self.rest, 8)
        beside = self.wide // LANES
        self.corners = [
            (tiles * self.each + t // beside * up(self.rest, 8), t % beside * LANES) for t in range(tiles)
        ]
        self.shape = (tiles * self.each + pl.cdiv(tiles, beside) * up(self.rest, 8), self.wide)

    def store(self, wire_ref, t, main, turned):
        row, lane = self.corners[t]
        wire_ref[t * self.each : t * self.each + self.ops] = main
        start = t * self.each + self.below
        wire_ref[start : start + self.rest] = turned[:, : self.wide]
        wire_ref[row : row + self.rest, lane : lane + self.rest] = turned[:, self.wide :]

    def parts(self, wire_ref, t):
        row, lane = self.corners[t]
        start, padded = t * self.each + self.below, up(self.rest, 8)
        head, tail = slice(0, self.wide), slice(self.wide, self.ops)
        side = wire_ref[start : start + padded].T[:, : self.rest]
        corner = wire_ref[row : row + padded, lane : lane + LANES].T[: self.rest, : self.rest]
        main = wire_ref[t * self.each : t * self.each + self.ops]
        return [(slice(0, self.ops), head, main), (head, tail, side), (tail, tail, corner)]


def near_send(det, own, partner, to_mine, after=()):
    states, ops, depth = own.shape
    half, tiles = states // 2, (states // 2) ** 2
    packing = Packing(tiles, ops)

    def body(x_ref, own_ref, partner_ref, wire_ref):
        main = contract_last(own_ref[0], partner_ref[0, : packing.wide])
        turned = contract_last(partner_ref[0, packing.wide :], own_ref[0])
        for t in range(tiles):

            @pl.when(pl.program_id(0) == t)
            def _():
                packing.store(wire_ref, t, main, turned)

    def second(x):
        return half * (1 - x[0]) if to_mine else half * x[0]

    return call(
        body,
        (tiles,),
        1,
        [
            pl.BlockSpec((1, ops, depth), lambda t, x: (half * (1 - x[0]) + t // half, 0, 0)),
            pl.BlockSpec((1, ops, depth), lambda t, x: (second(x) + t % half, 0, 0)),
        ],
        whole(packing.shape),
        f32(*packing.shape),
        after,
    )(det, own, partner)


def near_keep(det, own, partner, after=()):
    states, ops, depth = own.shape
    half = states // 2

    def body(x_ref, own_ref, partner_ref, tile_ref):
        tile_ref[0] = contract_last(own_ref[0], partner_ref[0])

    return call(
        body,
        (half, states),
        1,
        [
            pl.BlockSpec((1, ops, depth), lambda a, b, x: (half * x[0] + a, 0, 0)),
            pl.BlockSpec((1, ops, depth), lambda a, b, x: (b, 0, 0)),
        ],
        pl.BlockSpec((1, ops, ops), lambda a, b, x: (a * states + b, 0, 0)),
        f32(half * states, ops, ops),
        after,
    )(det, own, partner)


def near_share(det, keep, doubled, states, after=()):
    _, ops, _ = keep.shape
    half, tiles = states // 2, (states // 2) ** 2
    packing = Packing(tiles, ops)
    shape = (tiles, up(ops, 8), up(ops, LANES))

    def body(x_ref, keep_ref, wire_ref, tile_ref):
        for t in range(tiles):
            kept = t // half * states + half * x_ref[0] + t % half
            for rows, columns, values in packing.parts(wire_ref, t):
                tile_ref[t, rows, columns] = keep_ref[kept, rows, columns] + values

    return call(
        body, (1,), 1, [whole(keep.shape), whole(packing.shape)], whole(shape), f32(*shape), after
    )(det, keep, doubled)


def near_sum(place_in, keep, crossed, share, given, states, after=()):
    tiles, ops, _ = keep.shape
    half = states // 2
    packing = Packing(half * half, ops)

    def body(s_ref, keep_ref, wire_ref, share_ref, given_ref, out_ref):
        x, core = s_ref[0], s_ref[1]
        for a in range(half):
            for b in range(states):
                t, one, turned = a * states + b, a * half + b % half, b % half * half + a

                @pl.when(b // half != x)
                def _():
                    for rows, columns, values in packing.parts(wire_ref, one):
                        out_ref[0, rows, t, columns] = keep_ref[t, rows, columns] + values

                @pl.when((b // half == x) & (core == 0))
                def _():
                    out_ref[0, :, t] = share_ref[one, :ops, :ops]

                @pl.when((b // half == x) & (core == 1))
                def _():
                    out_ref[0, :, t] = given_ref[turned].T[:ops, :ops]

    return call(
        body,
        (1,),
        1,
        [whole(keep.shape), whole(packing.shape), whole(share.shape), whole(given.shape)],
        pl.BlockSpec((1, ops, tiles, ops), lambda i, s: (1, 0, 0, 0)),
        f32(2, ops, tiles, ops),
        after,
    )(place_in, keep, crossed, share, given)


def far_terms(det, own, got, width, turned, mine, after=()):
    states, ops, depth = own.shape
    half = states // 2
    rows = ops if turned else width
    tile = (up(ops, 8), width) if turned else (up(width, 8), ops)

    def body(x_ref, own_ref, got_ref, out_ref):
        pair = (own_ref[0], got_ref[...]) if turned else (got_ref[...], own_ref[0])
        every = contract_last(*pair)
        for u in range(states):
            part = slice(u * width, (u + 1) * width)
            out_ref[u, :rows] = every[:, part] if turned else every[part]

    def state(b, x):
        return ((half * x[0] if mine else half * (1 - x[0])) + b, 0, 0)

    return call(
        body,
        (half,),
        1,
        [pl.BlockSpec((1, ops, depth), state), whole(got.shape)],
        pl.BlockSpec((states, *tile), lambda b, x: (b, 0, 0)),
        f32(half * states, *tile),
        after,
    )(det, own, got)


def far_sum(det, keep, came, states, rows, turned, after=()):
    tiles, padded, lanes = keep.shape
    half = states // 2
    shape = (half * half, up(rows + 1, 8), lanes)

    def body(x_ref, keep_ref, came_ref, own_ref, straight_ref, across_ref):
        x = x_ref[0]
        top = jnp.zeros((rows, lanes), jnp.float32)
        for t in range(tiles):
            tile = keep_ref[t, :rows] + came_ref[t, :rows]
            own_ref[t] = tile
            top = jnp.maximum(top, jnp.abs(tile))
        exponent = jnp.floor(jnp.log2(jnp.maximum(jnp.max(top, keepdims=True), SMALLEST)))
        scale = jnp.exp2(LIFT - exponent)
        below = jnp.broadcast_to(exponent, (shape[1] - rows, lanes))
        for to_ref, first in ((straight_ref, half * x), (across_ref, half * (1 - x))):
            for a in range(half):
                for b in range(half):
                    to_ref[a * half + b] = jnp.concatenate(
                        [powered(own_ref[b * states + first + a] * scale), below]
                    ).astype(jnp.bfloat16)

    return call(
        body,
        (1,),
        1,
        [whole((tiles, padded, lanes))] * 2,
        [whole((tiles, rows, lanes)), whole(shape), whole(shape)],
        [f32(tiles, rows, lanes)] + [jax.ShapeDtypeStruct(shape, jnp.bfloat16)] * 2,
        after,
    )(det, keep, came)


def powered(value):
    square = value * value
    fourth = square * square
    return value * jnp.abs(value) * (fourth * fourth)


def decoded(code, rows):
    code = code.astype(jnp.float32)
    value, exponent = code[:rows], code[rows : rows + 1]
    root = jnp.exp2(jnp.log2(jnp.abs(value)) * (1 / POWER)) * jnp.exp2(exponent - LIFT)
    return jnp.where(value < 0, -root, root)


def place(place_in, out, owned, came, states, after=()):
    _, ops, tiles, _ = out.shape
    full, half = len(came), states // 2
    wide = full * LANES
    code = came[0][0].shape

    def body(s_ref, out_in, *refs):
        owned_refs, came_refs, out_ref = refs[: full + 1], refs[full + 1 : -1], refs[-1]
        x = s_ref[0]

        @pl.when(s_ref[1] == 1)
        def _():
            for t in range(tiles):
                for k in range(full):
                    out_ref[0, :, t, k * LANES : (k + 1) * LANES] = owned_refs[k][t]
                out_ref[0, :, t, wide:] = owned_refs[full][t].T

        for k in range(full):
            straight, across = came_refs[2 * k : 2 * k + 2]

            @pl.when((s_ref[1] == 0) & (pl.program_id(0) == k))
            def _():
                for a in range(half):
                    for v in range(states):
                        one = a * half + v % half
                        block = jnp.where(v // half == x, straight[one], across[one])
                        out_ref[0, :, a * states + v] = decoded(block, ops).T

    return call(
        body,
        (pl.cdiv(ops, LANES),),
        1,
        [pl.BlockSpec(memory_space=pl.ANY)]
        + [pl.BlockSpec((tiles, LANES, LANES), lambda i, s: (0, i, 0))] * full
        + [pl.BlockSpec((tiles, ops - wide, LANES), lambda i, s: (0, 0, i))]
        + [whole(code)] * (2 * full),
        pl.BlockSpec((1, LANES, tiles, ops), lambda i, s: (0, i, 0, 0)),
        f32(*out.shape),
        after,
        {1: 0},
    )(place_in, out, *owned, *[c for pair in came for c in pair])


def finish(place_in, out, straight, across, states):
    _, ops, tiles, _ = out.shape
    rest, half = ops % LANES, states // 2

    def body(s_ref, out_in, straight_ref, across_ref, out_ref, rows_ref, sem):
        x = s_ref[0]

        @pl.when(s_ref[1] == 0)
        def _():
            for a in range(half):
                for v in range(states):
                    one = a * half + v % half
                    block = jnp.where(v // half == x, straight_ref[one], across_ref[one])
                    rows_ref[:, a * states + v] = decoded(block, rest)
            copy = pltpu.make_async_copy(rows_ref, out_ref.at[0, pl.ds(ops - rest, rest)], sem)
            copy.start()
            copy.wait()

    return pl.pallas_call(
        body,
        in_specs=[
            pl.BlockSpec(memory_space=pltpu.SMEM),
            pl.BlockSpec(memory_space=pl.ANY),
            pl.BlockSpec(memory_space=pltpu.VMEM),
            pl.BlockSpec(memory_space=pltpu.VMEM),
        ],
        out_specs=pl.BlockSpec(memory_space=pl.ANY),
        out_shape=f32(*out.shape),
        input_output_aliases={1: 0},
        scratch_shapes=[pltpu.VMEM((rest, tiles, ops), jnp.float32), pltpu.SemaphoreType.DMA],
    )(place_in, out, straight, across)


def paired(amplitudes):
    blocks = lax.axis_size("state")
    far = blocks.bit_length() - 2
    states, depth, ops = amplitudes.shape
    full = ops // LANES
    wide = full * LANES
    both = ("state", "det")
    senders = [s for s in range(blocks) if (s & 1) == (s >> far & 1)]
    receivers = [s for s in range(blocks) if s not in senders]
    over = [(2 * s + x, 2 * (s ^ 1 << far) + x) for s in senders for x in range(2)]
    straight = [(b, a) for a, b in over]
    diagonal = [(b, a ^ 1) for a, b in over]
    across = [(2 * s + x, 2 * s + 1 - x) for s in receivers for x in range(2)]
    first_across = [(2 * s + x, 2 * s + 1 - x) for s in range(0, blocks, 2) for x in range(2)]
    to_second = [(2 * s + x, 2 * (s + 1) + x) for s in range(0, blocks, 2) for x in range(2)]

    state = lax.axis_index("state")
    x = lax.axis_index("det").astype(jnp.int32)
    det = x[None]
    receiver = ((state & 1) ^ (state >> far & 1)).astype(jnp.int32)
    core = (state & 1).astype(jnp.int32)

    partner = lax.ppermute(amplitudes, "state", [(s, s ^ 1) for s in range(blocks)])
    first = amplitudes[:, :, :LANES].transpose(0, 2, 1)
    first, later = lax.optimization_barrier((first, amplitudes))
    own = later.transpose(0, 2, 1)
    widths = [LANES] * full + [ops - wide]
    chunks = [own[:, k * LANES : k * LANES + w].reshape(states * w, depth) for k, w in enumerate(widths)]
    chunks[0] = first.reshape(states * LANES, depth)
    got = [lax.ppermute(c, both, over) for c in chunks]

    partner, own = lax.optimization_barrier((partner, own))
    partner = partner.transpose(0, 2, 1)
    crossed = near_send(det, own, partner, False, tuple(chunks[1:]))
    doubled = near_send(det, own, partner, True, (crossed,))
    keep = near_keep(det, own, partner, (doubled,))
    crossed = lax.ppermute(crossed, "det", [(0, 1), (1, 0)])
    doubled = lax.ppermute(doubled, both, first_across)

    def terms(k, mine, done):
        return far_terms(det, own, got[k], widths[k], k < full, mine, done)

    def finished(k, send, kept, done):
        came = lax.ppermute(send, both, across)
        mine, *pair = far_sum(det, kept, came, states, ops if k < full else widths[k], k < full, done)
        codes.append([lax.ppermute(v, both, to) for v, to in zip(pair, (straight, diagonal))])
        owned.append(mine)
        return mine

    owned, codes = [], []
    send = terms(0, False, (keep,))
    mine = finished(0, send, terms(0, True, (send,)), ())
    share = near_share(det, keep, doubled, states, (mine, crossed))
    given = lax.ppermute(share, both, to_second)
    sends, kepts, done = [], [], share
    for k in range(1, full + 1):
        done = terms(k, False, (done, *got[1:]))
        sends.append(done)
    for k in range(1, full + 1):
        done = terms(k, True, (done,))
        kepts.append(done)
    done = out = near_sum(jnp.stack([x, core]), keep, crossed, share, given, states, (done,))
    for k in range(1, full + 1):
        done = finished(k, sends[k - 1], kepts[k - 1], (done,))

    at = jnp.stack([x, receiver])
    out = place(at, out, owned, codes[:full], states)
    *last, out = lax.optimization_barrier((*codes[full], out))
    return finish(at, out, *last, states).transpose(0, 2, 1, 3)


def partner_2(value, axis, stride):
    mask = 2**stride
    pairs = [(source, source ^ mask) for source in range(lax.axis_size(axis))]
    return lax.ppermute(value, axis, pairs)


def pair_terms(own_block, partner, count):
    operators = own_block.shape[2]
    terms = jnp.einsum("adp,bdq->abpq", own_block, partner, preferred_element_type=jnp.float32)
    return terms.reshape(count, operators, operators)


def exchanged(amplitudes):
    blocks = lax.axis_size("state")
    far_bit = blocks.bit_length() - 2
    states = amplitudes.shape[0]
    gathered = []
    for bit in (far_bit, 0):
        partner = partner_2(amplitudes, "state", bit)
        terms = pair_terms(amplitudes, partner, states * states)
        gathered.append(lax.psum_scatter(terms, "det", scatter_dimension=0, tiled=True))
    return jnp.stack(gathered)


def on_device(amplitudes):
    states, _, ops = amplitudes.shape
    two = lax.axis_size("det") == 2 and lax.axis_size("state") >= 4
    if two and states % 2 == 0 and ops > LANES and ops % LANES % 8:
        return paired(amplitudes)
    return exchanged(amplitudes)


def solution(mesh):
    return jax.shard_map(
        on_device,
        mesh=mesh,
        in_specs=(P("state", "det", None),),
        out_specs=P(None, ("state", "det"), None, None),
        check_vma=False,
    )
```

```python
import functools

import jax
import jax.numpy as jnp
from jax import lax
from jax.experimental import pallas as pl
from jax.experimental.pallas import tpu as pltpu
from jax.sharding import PartitionSpec as P

LANES = 128
VMEM_LIMIT = 20 * 2**20
POWER, LIFT = 10, 11
SMALLEST = 2.0**-110


def contract_last(left, right):
    return lax.dot_general(left, right, (((1,), (1,)), ((), ())), preferred_element_type=jnp.float32)


def call(body, grid, scalars, in_specs, out_specs, out_shape, after=(), aliases={}):
    idle = len(after)

    def waiting(*refs):
        first = scalars + len(in_specs)
        body(*refs[:first], *refs[first + idle : -1])
        refs[-1][...] = jnp.zeros_like(refs[-1])

    token = (8, LANES)
    kernel = pl.pallas_call(
        waiting,
        grid_spec=pltpu.PrefetchScalarGridSpec(
            num_scalar_prefetch=scalars,
            grid=grid,
            in_specs=in_specs + [pl.BlockSpec(memory_space=pl.ANY)] * idle,
            out_specs=[*out_specs, whole(token)],
        ),
        out_shape=[*out_shape, f32(*token)],
        input_output_aliases=aliases,
        compiler_params=pltpu.CompilerParams(vmem_limit_bytes=VMEM_LIMIT),
    )
    return lambda *operands: kernel(*operands, *after)


def f32(*shape):
    return jax.ShapeDtypeStruct(shape, jnp.float32)


def up(size, unit):
    return -(-size // unit) * unit


def whole(shape):
    return pl.BlockSpec(shape, lambda *_: (0,) * len(shape), pipeline_mode=pl.Buffered(1))


class Packing:
    def __init__(self, tiles, ops):
        self.ops, self.wide = ops, ops // LANES * LANES
        self.rest, self.below = ops - self.wide, up(ops, 8)
        self.each = self.below + up(self.rest, 8)
        beside = self.wide // LANES
        self.corners = [
            (tiles * self.each + t // beside * up(self.rest, 8), t % beside * LANES) for t in range(tiles)
        ]
        self.shape = (tiles * self.each + pl.cdiv(tiles, beside) * up(self.rest, 8), self.wide)

    def store(self, wire_ref, t, main, turned):
        row, lane = self.corners[t]
        wire_ref[t * self.each : t * self.each + self.ops] = main
        start = t * self.each + self.below
        wire_ref[start : start + self.rest] = turned[:, : self.wide]
        wire_ref[row : row + self.rest, lane : lane + self.rest] = turned[:, self.wide :]

    def parts(self, wire_ref, t):
        row, lane = self.corners[t]
        start, padded = t * self.each + self.below, up(self.rest, 8)
        head, tail = slice(0, self.wide), slice(self.wide, self.ops)
        side = wire_ref[start : start + padded].T[:, : self.rest]
        corner = wire_ref[row : row + padded, lane : lane + LANES].T[: self.rest, : self.rest]
        main = wire_ref[t * self.each : t * self.each + self.ops]
        return [(slice(0, self.ops), head, main), (head, tail, side), (tail, tail, corner)]


def near_send(det, own, partner, to_mine, after=()):
    states, ops, depth = own.shape
    half, tiles = states // 2, (states // 2) ** 2
    packing = Packing(tiles, ops)

    def body(x_ref, own_ref, partner_ref, wire_ref):
        main = contract_last(own_ref[0], partner_ref[0, : packing.wide])
        turned = contract_last(partner_ref[0, packing.wide :], own_ref[0])
        for t in range(tiles):

            @pl.when(pl.program_id(0) == t)
            def _():
                packing.store(wire_ref, t, main, turned)

    def second(x):
        return half * (1 - x[0]) if to_mine else half * x[0]

    return call(
        body,
        (tiles,),
        1,
        [
            pl.BlockSpec((1, ops, depth), lambda t, x: (half * (1 - x[0]) + t // half, 0, 0)),
            pl.BlockSpec((1, ops, depth), lambda t, x: (second(x) + t % half, 0, 0)),
        ],
        [whole(packing.shape)],
        [f32(*packing.shape)],
        after,
    )(det, own, partner)


def near_keep(det, own, partner, after=()):
    states, ops, depth = own.shape
    half = states // 2

    def body(x_ref, own_ref, partner_ref, tile_ref):
        tile_ref[0] = contract_last(own_ref[0], partner_ref[0])

    return call(
        body,
        (half, states),
        1,
        [
            pl.BlockSpec((1, ops, depth), lambda a, b, x: (half * x[0] + a, 0, 0)),
            pl.BlockSpec((1, ops, depth), lambda a, b, x: (b, 0, 0)),
        ],
        [pl.BlockSpec((1, ops, ops), lambda a, b, x: (a * states + b, 0, 0))],
        [f32(half * states, ops, ops)],
        after,
    )(det, own, partner)


def near_share(det, keep, doubled, states, after=()):
    _, ops, _ = keep.shape
    half, tiles = states // 2, (states // 2) ** 2
    packing = Packing(tiles, ops)
    shape = (tiles, up(ops, 8), up(ops, LANES))

    def body(x_ref, keep_ref, wire_ref, tile_ref):
        for t in range(tiles):
            kept = t // half * states + half * x_ref[0] + t % half
            for rows, columns, values in packing.parts(wire_ref, t):
                tile_ref[t, rows, columns] = keep_ref[kept, rows, columns] + values

    return call(
        body, (1,), 1, [whole(keep.shape), whole(packing.shape)], [whole(shape)], [f32(*shape)], after
    )(det, keep, doubled)


def near_sum(place_in, keep, crossed, share, given, states, after=()):
    tiles, ops, _ = keep.shape
    half = states // 2
    packing = Packing(half * half, ops)

    def body(s_ref, keep_ref, wire_ref, share_ref, given_ref, out_ref):
        x, core = s_ref[0], s_ref[1]
        for a in range(half):
            for b in range(states):
                t, one, turned = a * states + b, a * half + b % half, b % half * half + a

                @pl.when(b // half != x)
                def _():
                    for rows, columns, values in packing.parts(wire_ref, one):
                        out_ref[0, rows, t, columns] = keep_ref[t, rows, columns] + values

                @pl.when((b // half == x) & (core == 0))
                def _():
                    out_ref[0, :, t] = share_ref[one, :ops, :ops]

                @pl.when((b // half == x) & (core == 1))
                def _():
                    out_ref[0, :, t] = given_ref[turned].T[:ops, :ops]

    return call(
        body,
        (1,),
        1,
        [whole(keep.shape), whole(packing.shape), whole(share.shape), whole(given.shape)],
        [pl.BlockSpec((1, ops, tiles, ops), lambda i, s: (1, 0, 0, 0), pipeline_mode=pl.Buffered(1))],
        [f32(2, ops, tiles, ops)],
        after,
    )(place_in, keep, crossed, share, given)


def far_terms(det, own, got, width, turned, mine, after=()):
    states, ops, depth = own.shape
    half = states // 2
    rows = ops if turned else width
    tile = (up(ops, 8), width) if turned else (up(width, 8), ops)

    def body(x_ref, own_ref, got_ref, out_ref):
        pair = (own_ref[0], got_ref[...]) if turned else (got_ref[...], own_ref[0])
        every = contract_last(*pair)
        for u in range(states):
            part = slice(u * width, (u + 1) * width)
            out_ref[u, :rows] = every[:, part] if turned else every[part]

    def state(b, x):
        return ((half * x[0] if mine else half * (1 - x[0])) + b, 0, 0)

    return call(
        body,
        (half,),
        1,
        [pl.BlockSpec((1, ops, depth), state), whole(got.shape)],
        [pl.BlockSpec((states, *tile), lambda b, x: (b, 0, 0))],
        [f32(half * states, *tile)],
        after,
    )(det, own, got)


def far_sum(det, keep, came, states, rows, turned, after=()):
    tiles, padded, lanes = keep.shape
    half = states // 2
    shape = (half * half, up(rows + 1, 8), lanes)

    def body(x_ref, keep_ref, came_ref, own_ref, straight_ref, across_ref):
        x = x_ref[0]
        top = jnp.zeros((rows, lanes), jnp.float32)
        for t in range(tiles):
            tile = keep_ref[t, :rows] + came_ref[t, :rows]
            own_ref[t] = tile
            top = jnp.maximum(top, jnp.abs(tile))
        exponent = jnp.floor(jnp.log2(jnp.maximum(jnp.max(top, keepdims=True), SMALLEST)))
        scale = jnp.exp2(LIFT - exponent)
        below = jnp.broadcast_to(exponent, (shape[1] - rows, lanes))
        for to_ref, first in ((straight_ref, half * x), (across_ref, half * (1 - x))):
            for a in range(half):
                for b in range(half):
                    to_ref[a * half + b] = jnp.concatenate(
                        [powered(own_ref[b * states + first + a] * scale), below]
                    ).astype(jnp.bfloat16)

    return call(
        body,
        (1,),
        1,
        [whole((tiles, padded, lanes))] * 2,
        [whole((tiles, rows, lanes)), whole(shape), whole(shape)],
        [f32(tiles, rows, lanes)] + [jax.ShapeDtypeStruct(shape, jnp.bfloat16)] * 2,
        after,
    )(det, keep, came)


def powered(value):
    square = value * value
    fourth = square * square
    return value * jnp.abs(value) * (fourth * fourth)


def decoded(code, rows):
    code = code.astype(jnp.float32)
    value, exponent = code[:rows], code[rows : rows + 1]
    root = jnp.exp2(jnp.log2(jnp.abs(value)) * (1 / POWER)) * jnp.exp2(exponent - LIFT)
    return jnp.where(value < 0, -root, root)


def place(place_in, out, owned, came, states, after=()):
    _, ops, tiles, _ = out.shape
    full, half = len(came), states // 2
    wide = full * LANES
    code = came[0][0].shape

    def body(s_ref, out_in, *refs):
        owned_refs, came_refs, out_ref = refs[: full + 1], refs[full + 1 : -1], refs[-1]
        x = s_ref[0]

        @pl.when(s_ref[1] == 1)
        def _():
            for t in range(tiles):
                for k in range(full):
                    out_ref[0, :, t, k * LANES : (k + 1) * LANES] = owned_refs[k][t]
                out_ref[0, :, t, wide:] = owned_refs[full][t].T

        for k in range(full):
            straight, across = came_refs[2 * k : 2 * k + 2]

            @pl.when((s_ref[1] == 0) & (pl.program_id(0) == k))
            def _():
                for a in range(half):
                    for v in range(states):
                        one = a * half + v % half
                        block = jnp.where(v // half == x, straight[one], across[one])
                        out_ref[0, :, a * states + v] = decoded(block, ops).T

    return call(
        body,
        (pl.cdiv(ops, LANES),),
        1,
        [pl.BlockSpec(memory_space=pl.ANY)]
        + [pl.BlockSpec((tiles, LANES, LANES), lambda i, s: (0, i, 0))] * full
        + [pl.BlockSpec((tiles, ops - wide, LANES), lambda i, s: (0, 0, i))]
        + [whole(code)] * (2 * full),
        [pl.BlockSpec((1, LANES, tiles, ops), lambda i, s: (0, i, 0, 0))],
        [f32(*out.shape)],
        after,
        {1: 0},
    )(place_in, out, *owned, *[c for pair in came for c in pair])


def finish(place_in, out, straight, across, states):
    _, ops, tiles, _ = out.shape
    rest, half = ops % LANES, states // 2

    def body(s_ref, out_in, straight_ref, across_ref, out_ref, rows_ref, sem):
        x = s_ref[0]

        @pl.when(s_ref[1] == 0)
        def _():
            for a in range(half):
                for v in range(states):
                    one = a * half + v % half
                    block = jnp.where(v // half == x, straight_ref[one], across_ref[one])
                    rows_ref[:, a * states + v] = decoded(block, rest)
            copy = pltpu.make_async_copy(rows_ref, out_ref.at[0, pl.ds(ops - rest, rest)], sem)
            copy.start()
            copy.wait()

    return pl.pallas_call(
        body,
        in_specs=[
            pl.BlockSpec(memory_space=pltpu.SMEM),
            pl.BlockSpec(memory_space=pl.ANY),
            pl.BlockSpec(memory_space=pltpu.VMEM),
            pl.BlockSpec(memory_space=pltpu.VMEM),
        ],
        out_specs=pl.BlockSpec(memory_space=pl.ANY),
        out_shape=f32(*out.shape),
        input_output_aliases={1: 0},
        scratch_shapes=[pltpu.VMEM((rest, tiles, ops), jnp.float32), pltpu.SemaphoreType.DMA],
    )(place_in, out, straight, across)


def paired(amplitudes):
    blocks = lax.axis_size("state")
    far = blocks.bit_length() - 2
    states, depth, ops = amplitudes.shape
    full = ops // LANES
    wide = full * LANES
    both = ("state", "det")
    senders = [s for s in range(blocks) if (s & 1) == (s >> far & 1)]
    receivers = [s for s in range(blocks) if s not in senders]
    over = [(2 * s + x, 2 * (s ^ 1 << far) + x) for s in senders for x in range(2)]
    straight = [(b, a) for a, b in over]
    diagonal = [(b, a ^ 1) for a, b in over]
    across = [(2 * s + x, 2 * s + 1 - x) for s in receivers for x in range(2)]
    first_across = [(2 * s + x, 2 * s + 1 - x) for s in range(0, blocks, 2) for x in range(2)]
    to_second = [(2 * s + x, 2 * (s + 1) + x) for s in range(0, blocks, 2) for x in range(2)]

    state = lax.axis_index("state")
    x = lax.axis_index("det").astype(jnp.int32)
    det = x[None]
    receiver = ((state & 1) ^ (state >> far & 1)).astype(jnp.int32)
    core = (state & 1).astype(jnp.int32)

    partner = lax.ppermute(amplitudes, "state", [(s, s ^ 1) for s in range(blocks)])
    first = amplitudes[:, :, :LANES].transpose(0, 2, 1)
    first, later = lax.optimization_barrier((first.reshape(states * LANES, depth), amplitudes))
    got = [lax.ppermute(first, both, over)]
    own = later.transpose(0, 2, 1)
    partner, own = lax.optimization_barrier((partner, own))
    partner = partner.transpose(0, 2, 1)

    crossed, token = near_send(det, own, partner, False, (first,))
    crossed = lax.ppermute(crossed, "det", [(0, 1), (1, 0)])
    doubled, token = near_send(det, own, partner, True, (token,))
    doubled = lax.ppermute(doubled, both, first_across)
    whole_own, token = lax.optimization_barrier((own, token))
    widths = [LANES] * full + [ops - wide]
    for k in range(1, full + 1):
        chunk = whole_own[:, k * LANES : k * LANES + widths[k]].reshape(states * widths[k], depth)
        chunk, token = lax.optimization_barrier((chunk, token))
        got.append(lax.ppermute(chunk, both, over))
    keep, token = near_keep(det, own, partner, (token,))
    def terms(k, mine, *done):
        return far_terms(det, own, got[k], widths[k], k < full, mine, done)

    def finished(k, send, kept, *done):
        came = lax.ppermute(send, both, across)
        rows = ops if k < full else widths[k]
        mine, *pair, token = far_sum(det, kept, came, states, rows, k < full, done)
        codes.append([lax.ppermute(v, both, to) for v, to in zip(pair, (straight, diagonal))])
        owned.append(mine)
        return token

    owned, codes = [], []
    kept, token = terms(0, True, token)
    share, token = near_share(det, keep, doubled, states, (token, crossed))
    given = lax.ppermute(share, both, to_second)
    send, token = terms(0, False, token)
    out, token = near_sum(jnp.stack([x, core]), keep, crossed, share, given, states, (token,))
    token = finished(0, send, kept, token)
    sends, kepts = [], []
    for k in range(1, full + 1):
        send, token = terms(k, False, token)
        sends.append(send)
    for k in range(1, full + 1):
        kept, token = terms(k, True, token)
        kepts.append(kept)
    for k in range(1, full + 1):
        token = finished(k, sends[k - 1], kepts[k - 1], token)

    at = jnp.stack([x, receiver])
    out, token = place(at, out, owned, codes[:full], states, (token,))
    *last, out = lax.optimization_barrier((*codes[full], out))
    return finish(at, out, *last, states).transpose(0, 2, 1, 3)


def partner_2(value, axis, stride):
    mask = 2**stride
    pairs = [(source, source ^ mask) for source in range(lax.axis_size(axis))]
    return lax.ppermute(value, axis, pairs)


def pair_terms(own_block, partner, count):
    operators = own_block.shape[2]
    terms = jnp.einsum("adp,bdq->abpq", own_block, partner, preferred_element_type=jnp.float32)
    return terms.reshape(count, operators, operators)


def exchanged(amplitudes):
    blocks = lax.axis_size("state")
    far_bit = blocks.bit_length() - 2
    states = amplitudes.shape[0]
    gathered = []
    for bit in (far_bit, 0):
        partner = partner_2(amplitudes, "state", bit)
        terms = pair_terms(amplitudes, partner, states * states)
        gathered.append(lax.psum_scatter(terms, "det", scatter_dimension=0, tiled=True))
    return jnp.stack(gathered)


def on_device(amplitudes):
    states, _, ops = amplitudes.shape
    two = lax.axis_size("det") == 2 and lax.axis_size("state") >= 4
    if two and states % 2 == 0 and ops > LANES and ops % LANES % 8:
        return paired(amplitudes)
    return exchanged(amplitudes)


def solution(mesh):
    return jax.shard_map(
        on_device,
        mesh=mesh,
        in_specs=(P("state", "det", None),),
        out_specs=P(None, ("state", "det"), None, None),
        check_vma=False,
    )
```

```python
import functools

import jax
import jax.numpy as jnp
from jax import lax
from jax.experimental import pallas as pl
from jax.experimental.pallas import tpu as pltpu
from jax.sharding import PartitionSpec as P

LANES = 128
VMEM_LIMIT = 20 * 2**20
POWER, LIFT = 10, 11
SMALLEST = 2.0**-110


def contract_last(left, right):
    return lax.dot_general(left, right, (((1,), (1,)), ((), ())), preferred_element_type=jnp.float32)


def call(body, grid, scalars, in_specs, out_specs, out_shape, after=(), aliases={}):
    idle = len(after)

    def waiting(*refs):
        first = scalars + len(in_specs)
        body(*refs[:first], *refs[first + idle : -1])
        refs[-1][...] = jnp.zeros_like(refs[-1])

    token = (8, LANES)
    kernel = pl.pallas_call(
        waiting,
        grid_spec=pltpu.PrefetchScalarGridSpec(
            num_scalar_prefetch=scalars,
            grid=grid,
            in_specs=in_specs + [pl.BlockSpec(memory_space=pl.ANY)] * idle,
            out_specs=[*out_specs, whole(token)],
        ),
        out_shape=[*out_shape, f32(*token)],
        input_output_aliases=aliases,
        compiler_params=pltpu.CompilerParams(vmem_limit_bytes=VMEM_LIMIT),
    )
    return lambda *operands: kernel(*operands, *after)


def f32(*shape):
    return jax.ShapeDtypeStruct(shape, jnp.float32)


def up(size, unit):
    return -(-size // unit) * unit


def whole(shape):
    return pl.BlockSpec(shape, lambda *_: (0,) * len(shape), pipeline_mode=pl.Buffered(1))


class Packing:
    def __init__(self, tiles, ops):
        self.ops, self.wide = ops, ops // LANES * LANES
        self.rest, self.below = ops - self.wide, up(ops, 8)
        self.each = self.below + up(self.rest, 8)
        beside = self.wide // LANES
        self.corners = [
            (tiles * self.each + t // beside * up(self.rest, 8), t % beside * LANES) for t in range(tiles)
        ]
        self.shape = (tiles * self.each + pl.cdiv(tiles, beside) * up(self.rest, 8), self.wide)

    def store(self, wire_ref, t, main, turned):
        row, lane = self.corners[t]
        wire_ref[t * self.each : t * self.each + self.ops] = main
        start = t * self.each + self.below
        wire_ref[start : start + self.rest] = turned[:, : self.wide]
        wire_ref[row : row + self.rest, lane : lane + self.rest] = turned[:, self.wide :]

    def parts(self, wire_ref, t):
        row, lane = self.corners[t]
        start, padded = t * self.each + self.below, up(self.rest, 8)
        head, tail = slice(0, self.wide), slice(self.wide, self.ops)
        side = wire_ref[start : start + padded].T[:, : self.rest]
        corner = wire_ref[row : row + padded, lane : lane + LANES].T[: self.rest, : self.rest]
        main = wire_ref[t * self.each : t * self.each + self.ops]
        return [(slice(0, self.ops), head, main), (head, tail, side), (tail, tail, corner)]


def near_send(det, own, partner, to_mine, after=()):
    states, ops, depth = own.shape
    half, tiles = states // 2, (states // 2) ** 2
    packing = Packing(tiles, ops)

    def body(x_ref, own_ref, partner_ref, wire_ref):
        main = contract_last(own_ref[0], partner_ref[0, : packing.wide])
        turned = contract_last(partner_ref[0, packing.wide :], own_ref[0])
        for t in range(tiles):

            @pl.when(pl.program_id(0) == t)
            def _():
                packing.store(wire_ref, t, main, turned)

    def second(x):
        return half * (1 - x[0]) if to_mine else half * x[0]

    return call(
        body,
        (tiles,),
        1,
        [
            pl.BlockSpec((1, ops, depth), lambda t, x: (half * (1 - x[0]) + t // half, 0, 0)),
            pl.BlockSpec((1, ops, depth), lambda t, x: (second(x) + t % half, 0, 0)),
        ],
        [whole(packing.shape)],
        [f32(*packing.shape)],
        after,
    )(det, own, partner)


def near_keep(det, own, partner, after=()):
    states, ops, depth = own.shape
    half = states // 2

    def body(x_ref, own_ref, partner_ref, tile_ref):
        tile_ref[0] = contract_last(own_ref[0], partner_ref[0])

    return call(
        body,
        (half, states),
        1,
        [
            pl.BlockSpec((1, ops, depth), lambda a, b, x: (half * x[0] + a, 0, 0)),
            pl.BlockSpec((1, ops, depth), lambda a, b, x: (b, 0, 0)),
        ],
        [pl.BlockSpec((1, ops, ops), lambda a, b, x: (a * states + b, 0, 0))],
        [f32(half * states, ops, ops)],
        after,
    )(det, own, partner)


def near_share(det, keep, doubled, states, after=()):
    _, ops, _ = keep.shape
    half, tiles = states // 2, (states // 2) ** 2
    packing = Packing(tiles, ops)
    shape = (tiles, up(ops, 8), up(ops, LANES))

    def body(x_ref, keep_ref, wire_ref, tile_ref):
        for t in range(tiles):
            kept = t // half * states + half * x_ref[0] + t % half
            for rows, columns, values in packing.parts(wire_ref, t):
                tile_ref[t, rows, columns] = keep_ref[kept, rows, columns] + values

    return call(
        body, (1,), 1, [whole(keep.shape), whole(packing.shape)], [whole(shape)], [f32(*shape)], after
    )(det, keep, doubled)


def near_sum(place_in, keep, crossed, share, given, states, after=()):
    tiles, ops, _ = keep.shape
    half = states // 2
    packing = Packing(half * half, ops)

    def body(s_ref, keep_ref, wire_ref, share_ref, given_ref, out_ref):
        x, core = s_ref[0], s_ref[1]
        for a in range(half):
            for b in range(states):
                t, one, turned = a * states + b, a * half + b % half, b % half * half + a

                @pl.when(b // half != x)
                def _():
                    for rows, columns, values in packing.parts(wire_ref, one):
                        out_ref[0, rows, t, columns] = keep_ref[t, rows, columns] + values

                @pl.when((b // half == x) & (core == 0))
                def _():
                    out_ref[0, :, t] = share_ref[one, :ops, :ops]

                @pl.when((b // half == x) & (core == 1))
                def _():
                    out_ref[0, :, t] = given_ref[turned].T[:ops, :ops]

    return call(
        body,
        (1,),
        1,
        [whole(keep.shape), whole(packing.shape), whole(share.shape), whole(given.shape)],
        [pl.BlockSpec((1, ops, tiles, ops), lambda i, s: (1, 0, 0, 0), pipeline_mode=pl.Buffered(1))],
        [f32(2, ops, tiles, ops)],
        after,
    )(place_in, keep, crossed, share, given)


def far_terms(det, own, got, start, width, turned, mine, after=()):
    states, ops, depth = own.shape
    half = states // 2
    rows = ops if turned else width
    tile = (up(ops, 8), width) if turned else (up(width, 8), ops)

    def body(x_ref, own_ref, got_ref, out_ref):
        pair = (own_ref[0], got_ref[...]) if turned else (got_ref[...], own_ref[0])
        every = contract_last(*pair)
        for u in range(states):
            part = slice(u * width, (u + 1) * width)
            out_ref[u, :rows] = every[:, part] if turned else every[part]

    def state(b, x):
        return ((half * x[0] if mine else half * (1 - x[0])) + b, 0, 0)

    return call(
        body,
        (half,),
        1,
        [
            pl.BlockSpec((1, ops, depth), state),
            pl.BlockSpec((pl.Element(states * width), pl.Element(depth)), lambda b, x: (start, 0), pipeline_mode=pl.Buffered(1)),
        ],
        [pl.BlockSpec((states, *tile), lambda b, x: (b, 0, 0))],
        [f32(half * states, *tile)],
        after,
    )(det, own, got)


def far_sum(det, keep, came, states, rows, turned, after=()):
    tiles, padded, lanes = keep.shape
    half = states // 2
    shape = (half * half, up(rows + 1, 8), lanes)

    def body(x_ref, keep_ref, came_ref, own_ref, straight_ref, across_ref):
        x = x_ref[0]
        top = jnp.zeros((rows, lanes), jnp.float32)
        for t in range(tiles):
            tile = keep_ref[t, :rows] + came_ref[t, :rows]
            own_ref[t] = tile
            top = jnp.maximum(top, jnp.abs(tile))
        exponent = jnp.floor(jnp.log2(jnp.maximum(jnp.max(top, keepdims=True), SMALLEST)))
        scale = jnp.exp2(LIFT - exponent)
        below = jnp.broadcast_to(exponent, (shape[1] - rows, lanes))
        for to_ref, first in ((straight_ref, half * x), (across_ref, half * (1 - x))):
            for a in range(half):
                for b in range(half):
                    to_ref[a * half + b] = jnp.concatenate(
                        [powered(own_ref[b * states + first + a] * scale), below]
                    ).astype(jnp.bfloat16)

    return call(
        body,
        (1,),
        1,
        [whole((tiles, padded, lanes))] * 2,
        [whole((tiles, rows, lanes)), whole(shape), whole(shape)],
        [f32(tiles, rows, lanes)] + [jax.ShapeDtypeStruct(shape, jnp.bfloat16)] * 2,
        after,
    )(det, keep, came)


def powered(value):
    square = value * value
    fourth = square * square
    return value * jnp.abs(value) * (fourth * fourth)


def decoded(code, rows):
    code = code.astype(jnp.float32)
    value, exponent = code[:rows], code[rows : rows + 1]
    root = jnp.exp2(jnp.log2(jnp.abs(value)) * (1 / POWER)) * jnp.exp2(exponent - LIFT)
    return jnp.where(value < 0, -root, root)


def place(place_in, out, owned, came, states, after=()):
    _, ops, tiles, _ = out.shape
    full, half = len(came), states // 2
    wide = full * LANES
    code = came[0][0].shape

    def body(s_ref, out_in, *refs):
        owned_refs, came_refs, out_ref = refs[: full + 1], refs[full + 1 : -1], refs[-1]
        x = s_ref[0]

        @pl.when(s_ref[1] == 1)
        def _():
            for t in range(tiles):
                for k in range(full):
                    out_ref[0, :, t, k * LANES : (k + 1) * LANES] = owned_refs[k][t]
                out_ref[0, :, t, wide:] = owned_refs[full][t].T

        for k in range(full):
            straight, across = came_refs[2 * k : 2 * k + 2]

            @pl.when((s_ref[1] == 0) & (pl.program_id(0) == k))
            def _():
                for a in range(half):
                    for v in range(states):
                        one = a * half + v % half
                        block = jnp.where(v // half == x, straight[one], across[one])
                        out_ref[0, :, a * states + v] = decoded(block, ops).T

    return call(
        body,
        (pl.cdiv(ops, LANES),),
        1,
        [pl.BlockSpec(memory_space=pl.ANY)]
        + [pl.BlockSpec((tiles, LANES, LANES), lambda i, s: (0, i, 0))] * full
        + [pl.BlockSpec((tiles, ops - wide, LANES), lambda i, s: (0, 0, i))]
        + [whole(code)] * (2 * full),
        [pl.BlockSpec((1, LANES, tiles, ops), lambda i, s: (0, i, 0, 0))],
        [f32(*out.shape)],
        after,
        {1: 0},
    )(place_in, out, *owned, *[c for pair in came for c in pair])


def finish(place_in, out, straight, across, states):
    _, ops, tiles, _ = out.shape
    rest, half = ops % LANES, states // 2

    def body(s_ref, out_in, straight_ref, across_ref, out_ref, rows_ref, sem):
        x = s_ref[0]

        @pl.when(s_ref[1] == 0)
        def _():
            for a in range(half):
                for v in range(states):
                    one = a * half + v % half
                    block = jnp.where(v // half == x, straight_ref[one], across_ref[one])
                    rows_ref[:, a * states + v] = decoded(block, rest)
            copy = pltpu.make_async_copy(rows_ref, out_ref.at[0, pl.ds(ops - rest, rest)], sem)
            copy.start()
            copy.wait()

    return pl.pallas_call(
        body,
        in_specs=[
            pl.BlockSpec(memory_space=pltpu.SMEM),
            pl.BlockSpec(memory_space=pl.ANY),
            pl.BlockSpec(memory_space=pltpu.VMEM),
            pl.BlockSpec(memory_space=pltpu.VMEM),
        ],
        out_specs=pl.BlockSpec(memory_space=pl.ANY),
        out_shape=f32(*out.shape),
        input_output_aliases={1: 0},
        scratch_shapes=[pltpu.VMEM((rest, tiles, ops), jnp.float32), pltpu.SemaphoreType.DMA],
    )(place_in, out, straight, across)


def paired(amplitudes):
    blocks = lax.axis_size("state")
    far = blocks.bit_length() - 2
    states, depth, ops = amplitudes.shape
    full = ops // LANES
    wide = full * LANES
    both = ("state", "det")
    senders = [s for s in range(blocks) if (s & 1) == (s >> far & 1)]
    receivers = [s for s in range(blocks) if s not in senders]
    over = [(2 * s + x, 2 * (s ^ 1 << far) + x) for s in senders for x in range(2)]
    straight = [(b, a) for a, b in over]
    diagonal = [(b, a ^ 1) for a, b in over]
    across = [(2 * s + x, 2 * s + 1 - x) for s in receivers for x in range(2)]
    first_across = [(2 * s + x, 2 * s + 1 - x) for s in range(0, blocks, 2) for x in range(2)]
    to_second = [(2 * s + x, 2 * (s + 1) + x) for s in range(0, blocks, 2) for x in range(2)]

    state = lax.axis_index("state")
    x = lax.axis_index("det").astype(jnp.int32)
    det = x[None]
    receiver = ((state & 1) ^ (state >> far & 1)).astype(jnp.int32)
    core = (state & 1).astype(jnp.int32)

    partner = lax.ppermute(amplitudes, "state", [(s, s ^ 1) for s in range(blocks)])
    first = amplitudes[:, :, :LANES].transpose(0, 2, 1)
    first, later = lax.optimization_barrier((first.reshape(states * LANES, depth), amplitudes))
    got = [lax.ppermute(first, both, over)]
    own = later.transpose(0, 2, 1)
    partner, own = lax.optimization_barrier((partner, own))
    partner = partner.transpose(0, 2, 1)

    crossed, token = near_send(det, own, partner, False, (first,))
    crossed = lax.ppermute(crossed, "det", [(0, 1), (1, 0)])
    doubled, token = near_send(det, own, partner, True, (token,))
    doubled = lax.ppermute(doubled, both, first_across)
    whole_own, token = lax.optimization_barrier((own, token))
    widths = [LANES] * full + [ops - wide]
    later = [
        whole_own[:, k * LANES : k * LANES + w].reshape(states * w, depth) for k, w in enumerate(widths) if k
    ]
    later, token = lax.optimization_barrier((jnp.concatenate(later), token))
    got.append(lax.ppermute(later, both, over))
    keep, token = near_keep(det, own, partner, (token,))
    def terms(k, mine, *done):
        start = states * LANES * (k - 1) if k else 0
        return far_terms(det, own, got[min(k, 1)], start, widths[k], k < full, mine, done)

    def finished(k, token):
        rows = ops if k < full else widths[k]
        mine, *pair, token = far_sum(det, kepts[k], came[k], states, rows, k < full, (token,))
        codes.append([lax.ppermute(v, both, to) for v, to in zip(pair, (straight, diagonal))])
        owned.append(mine)
        return token

    owned, codes, kepts, came = [], [], [], []
    kept, token = terms(0, True, token)
    kepts.append(kept)
    share, token = near_share(det, keep, doubled, states, (token, crossed))
    given = lax.ppermute(share, both, to_second)
    for k in range(full + 1):
        send, token = terms(k, False, token)
        came.append(lax.ppermute(send, both, across))
        if k == 0:
            out, token = near_sum(jnp.stack([x, core]), keep, crossed, share, given, states, (token,))
    token = finished(0, token)
    for k in range(1, full + 1):
        kept, token = terms(k, True, token)
        kepts.append(kept)
    for k in range(1, full + 1):
        token = finished(k, token)

    at = jnp.stack([x, receiver])
    out, token = place(at, out, owned, codes[:full], states, (token,))
    *last, out = lax.optimization_barrier((*codes[full], out))
    return finish(at, out, *last, states).transpose(0, 2, 1, 3)


def partner_2(value, axis, stride):
    mask = 2**stride
    pairs = [(source, source ^ mask) for source in range(lax.axis_size(axis))]
    return lax.ppermute(value, axis, pairs)


def pair_terms(own_block, partner, count):
    operators = own_block.shape[2]
    terms = jnp.einsum("adp,bdq->abpq", own_block, partner, preferred_element_type=jnp.float32)
    return terms.reshape(count, operators, operators)


def exchanged(amplitudes):
    blocks = lax.axis_size("state")
    far_bit = blocks.bit_length() - 2
    states = amplitudes.shape[0]
    gathered = []
    for bit in (far_bit, 0):
        partner = partner_2(amplitudes, "state", bit)
        terms = pair_terms(amplitudes, partner, states * states)
        gathered.append(lax.psum_scatter(terms, "det", scatter_dimension=0, tiled=True))
    return jnp.stack(gathered)


def on_device(amplitudes):
    states, _, ops = amplitudes.shape
    two = lax.axis_size("det") == 2 and lax.axis_size("state") >= 4
    if two and states % 2 == 0 and ops > LANES and ops % LANES % 8:
        return paired(amplitudes)
    return exchanged(amplitudes)


def solution(mesh):
    return jax.shard_map(
        on_device,
        mesh=mesh,
        in_specs=(P("state", "det", None),),
        out_specs=P(None, ("state", "det"), None, None),
        check_vma=False,
    )
```

```python
import functools

import jax
import jax.numpy as jnp
from jax import lax
from jax.experimental import pallas as pl
from jax.experimental.pallas import tpu as pltpu
from jax.sharding import PartitionSpec as P

LANES = 128
VMEM_LIMIT = 20 * 2**20
POWER, LIFT = 10, 11
SMALLEST = 2.0**-110


def contract_last(left, right):
    return lax.dot_general(left, right, (((1,), (1,)), ((), ())), preferred_element_type=jnp.float32)


def call(body, grid, scalars, in_specs, out_specs, out_shape, after=(), aliases={}):
    idle = len(after)

    def waiting(*refs):
        first = scalars + len(in_specs)
        body(*refs[:first], *refs[first + idle : -1])
        refs[-1][...] = jnp.zeros_like(refs[-1])

    token = (8, LANES)
    kernel = pl.pallas_call(
        waiting,
        grid_spec=pltpu.PrefetchScalarGridSpec(
            num_scalar_prefetch=scalars,
            grid=grid,
            in_specs=in_specs + [pl.BlockSpec(memory_space=pl.ANY)] * idle,
            out_specs=[*out_specs, whole(token)],
        ),
        out_shape=[*out_shape, f32(*token)],
        input_output_aliases=aliases,
        compiler_params=pltpu.CompilerParams(vmem_limit_bytes=VMEM_LIMIT),
    )
    return lambda *operands: kernel(*operands, *after)


def f32(*shape):
    return jax.ShapeDtypeStruct(shape, jnp.float32)


def up(size, unit):
    return -(-size // unit) * unit


def whole(shape):
    return pl.BlockSpec(shape, lambda *_: (0,) * len(shape), pipeline_mode=pl.Buffered(1))


class Packing:
    def __init__(self, tiles, ops):
        self.ops, self.wide = ops, ops // LANES * LANES
        self.rest, self.below = ops - self.wide, up(ops, 8)
        self.each = self.below + up(self.rest, 8)
        beside = self.wide // LANES
        self.corners = [
            (tiles * self.each + t // beside * up(self.rest, 8), t % beside * LANES) for t in range(tiles)
        ]
        self.shape = (tiles * self.each + pl.cdiv(tiles, beside) * up(self.rest, 8), self.wide)

    def store(self, wire_ref, t, main, turned):
        row, lane = self.corners[t]
        wire_ref[t * self.each : t * self.each + self.ops] = main
        start = t * self.each + self.below
        wire_ref[start : start + self.rest] = turned[:, : self.wide]
        wire_ref[row : row + self.rest, lane : lane + self.rest] = turned[:, self.wide :]

    def parts(self, wire_ref, t):
        row, lane = self.corners[t]
        start, padded = t * self.each + self.below, up(self.rest, 8)
        head, tail = slice(0, self.wide), slice(self.wide, self.ops)
        side = wire_ref[start : start + padded].T[:, : self.rest]
        corner = wire_ref[row : row + padded, lane : lane + LANES].T[: self.rest, : self.rest]
        main = wire_ref[t * self.each : t * self.each + self.ops]
        return [(slice(0, self.ops), head, main), (head, tail, side), (tail, tail, corner)]


def near_send(det, own, partner, to_mine, after=()):
    states, ops, depth = own.shape
    half, tiles = states // 2, (states // 2) ** 2
    packing = Packing(tiles, ops)

    def body(x_ref, own_ref, partner_ref, wire_ref):
        main = contract_last(own_ref[0], partner_ref[0, : packing.wide])
        turned = contract_last(partner_ref[0, packing.wide :], own_ref[0])
        for t in range(tiles):

            @pl.when(pl.program_id(0) == t)
            def _():
                packing.store(wire_ref, t, main, turned)

    def second(x):
        return half * (1 - x[0]) if to_mine else half * x[0]

    return call(
        body,
        (tiles,),
        1,
        [
            pl.BlockSpec((1, ops, depth), lambda t, x: (half * (1 - x[0]) + t // half, 0, 0)),
            pl.BlockSpec((1, ops, depth), lambda t, x: (second(x) + t % half, 0, 0)),
        ],
        [whole(packing.shape)],
        [f32(*packing.shape)],
        after,
    )(det, own, partner)


def near_keep(det, own, partner, after=()):
    states, ops, depth = own.shape
    half = states // 2

    def body(x_ref, own_ref, partner_ref, tile_ref):
        tile_ref[0] = contract_last(own_ref[0], partner_ref[0])

    return call(
        body,
        (half, states),
        1,
        [
            pl.BlockSpec((1, ops, depth), lambda a, b, x: (half * x[0] + a, 0, 0)),
            pl.BlockSpec((1, ops, depth), lambda a, b, x: (b, 0, 0)),
        ],
        [pl.BlockSpec((1, ops, ops), lambda a, b, x: (a * states + b, 0, 0))],
        [f32(half * states, ops, ops)],
        after,
    )(det, own, partner)


def near_share(det, keep, doubled, states, after=()):
    _, ops, _ = keep.shape
    half, tiles = states // 2, (states // 2) ** 2
    packing = Packing(tiles, ops)
    shape = (tiles, up(ops, 8), up(ops, LANES))

    def body(x_ref, keep_ref, wire_ref, tile_ref):
        for t in range(tiles):
            kept = t // half * states + half * x_ref[0] + t % half
            for rows, columns, values in packing.parts(wire_ref, t):
                tile_ref[t, rows, columns] = keep_ref[kept, rows, columns] + values

    return call(
        body, (1,), 1, [whole(keep.shape), whole(packing.shape)], [whole(shape)], [f32(*shape)], after
    )(det, keep, doubled)


def near_sum(place_in, keep, crossed, share, given, states, after=()):
    tiles, ops, _ = keep.shape
    half = states // 2
    packing = Packing(half * half, ops)

    def body(s_ref, keep_ref, wire_ref, share_ref, given_ref, out_ref):
        x, core = s_ref[0], s_ref[1]
        for a in range(half):
            for b in range(states):
                t, one, turned = a * states + b, a * half + b % half, b % half * half + a

                @pl.when(b // half != x)
                def _():
                    for rows, columns, values in packing.parts(wire_ref, one):
                        out_ref[0, rows, t, columns] = keep_ref[t, rows, columns] + values

                @pl.when((b // half == x) & (core == 0))
                def _():
                    out_ref[0, :, t] = share_ref[one, :ops, :ops]

                @pl.when((b // half == x) & (core == 1))
                def _():
                    out_ref[0, :, t] = given_ref[turned].T[:ops, :ops]

    return call(
        body,
        (1,),
        1,
        [whole(keep.shape), whole(packing.shape), whole(share.shape), whole(given.shape)],
        [pl.BlockSpec((1, ops, tiles, ops), lambda i, s: (1, 0, 0, 0), pipeline_mode=pl.Buffered(1))],
        [f32(2, ops, tiles, ops)],
        after,
    )(place_in, keep, crossed, share, given)


def far_terms(det, own, got, start, width, turned, mine, after=()):
    states, ops, depth = own.shape
    half = states // 2
    rows = ops if turned else width
    tile = (up(ops, 8), width) if turned else (up(width, 8), ops)

    def first(x):
        return half * x if mine else half * (1 - x)

    def body(x_ref, own_ref, got_ref, out_ref):
        if turned:
            both = contract_last(own_ref[0], got_ref[...])
            parts = [both[:, a * width : (a + 1) * width] for a in range(half)]
        else:
            every = contract_last(got_ref[...], own_ref[0])
            parts = [every[u * width : (u + 1) * width] for u in range(states)]
            parts = [jnp.where(first(x_ref[0]) == 0, parts[a], parts[half + a]) for a in range(half)]
        for a in range(half):
            out_ref[a, 0, :rows] = parts[a]

    picked = half if turned else states

    def rows_in(v, x):
        return (start + first(x[0]) * width if turned else start, 0)

    return call(
        body,
        (states,),
        1,
        [
            pl.BlockSpec((1, ops, depth), lambda v, x: (v, 0, 0)),
            pl.BlockSpec(
                (pl.Element(picked * width), pl.Element(depth)), rows_in, pipeline_mode=pl.Buffered(1)
            ),
        ],
        [pl.BlockSpec((half, 1, *tile), lambda v, x: (0, v, 0, 0))],
        [f32(half, states, *tile)],
        after,
    )(det, own, got)


def far_sum(det, keep, came, rows, turned, others=None, after=()):
    half, states, padded, lanes = keep.shape
    earlier = len(others or ())
    shape = (up(rows + 1, 8), lanes)

    def body(x_ref, keep_ref, came_ref, *refs):
        x = x_ref[0]
        other_refs, (tile_ref, code_ref), cross_refs = refs[:earlier], refs[earlier:][:2], refs[earlier + 2 :]
        top = jnp.zeros((rows, lanes), jnp.float32)
        for a in range(half):
            for v in range(states):
                tile = keep_ref[a, v, :rows] + came_ref[a, v, :rows]
                tile_ref[a, v] = tile
                top = jnp.maximum(top, jnp.abs(tile))

        def coder(top):
            exponent = jnp.floor(jnp.log2(jnp.maximum(jnp.max(top, keepdims=True), SMALLEST)))
            scale = jnp.exp2(LIFT - exponent)
            below = jnp.broadcast_to(exponent, (shape[0] - rows, lanes))
            return lambda tile: jnp.concatenate([powered(tile * scale), below]).astype(jnp.bfloat16)

        code = coder(top)
        for a in range(half):
            for v in range(states):
                code_ref[a, v] = code(tile_ref[a, v])
        for cross_ref in cross_refs:
            for a in range(half):
                for b in range(half):
                    cross_ref[earlier, a, b] = code_ref[a, half * (1 - x) + b]
            for k, other_ref in enumerate(other_refs):
                top = jnp.zeros((rows, lanes), jnp.float32)
                for a in range(half):
                    for v in range(states):
                        top = jnp.maximum(top, jnp.abs(other_ref[a, v]))
                code = coder(top)
                for a in range(half):
                    for b in range(half):
                        cross_ref[k, a, b] = code(other_ref[a, half * (1 - x) + b])

    shapes = [(half, states, rows, lanes), (half, states, *shape)]
    if others is not None:
        shapes.append((earlier + 1, half, half, *shape))
    kinds = [jnp.float32] + [jnp.bfloat16] * (len(shapes) - 1)
    return call(
        body,
        (1,),
        1,
        [whole(keep.shape)] * 2 + [whole(shapes[0])] * earlier,
        [whole(s) for s in shapes],
        [jax.ShapeDtypeStruct(s, kind) for s, kind in zip(shapes, kinds)],
        after,
    )(det, keep, came, *(others or ()))


def powered(value):
    square = value * value
    fourth = square * square
    return value * jnp.abs(value) * (fourth * fourth)


def rooted(code, exponent):
    code = code.astype(jnp.float32)
    root = jnp.exp2(jnp.log2(jnp.abs(code)) * (1 / POWER)) * jnp.exp2(exponent - LIFT)
    return jnp.where(code < 0, -root, root)


def decoded(code, rows):
    return rooted(code[:rows], code[rows:].astype(jnp.float32)[:1])


def place(place_in, out, finished, crossed, came, after=()):
    _, ops, tiles, _ = out.shape
    full = len(came)
    half, states, _, _ = finished[0].shape
    wide = full * LANES
    turned, last = crossed

    def body(s_ref, out_in, *refs):
        finished_refs, came_refs, out_ref = refs[: full + 1], refs[full + 4 : -1], refs[-1]
        turned_ref, under_ref, last_ref = refs[full + 1 :][:3]
        x = s_ref[0]

        @pl.when(s_ref[1] == 1)
        def _():
            for b in range(half):
                for u in range(states):
                    a, t = u % half, b * states + u

                    @pl.when(u // half == x)
                    def _():
                        for k in range(full):
                            out_ref[0, :, t, k * LANES : (k + 1) * LANES] = finished_refs[k][a, half * x + b]
                        out_ref[0, :, t, wide:] = finished_refs[full][a, half * x + b].T

                    @pl.when(u // half != x)
                    def _():
                        for k in range(full):
                            exponent = under_ref[k, a, b].astype(jnp.float32)[ops % 16 : ops % 16 + 1]
                            out_ref[0, :, t, k * LANES : (k + 1) * LANES] = rooted(turned_ref[k, a, b], exponent)
                        exponent = last_ref[a, b, ops - wide :, :1].astype(jnp.float32)[:1]
                        out_ref[0, :, t, wide:] = rooted(last_ref[a, b, : ops - wide], exponent).T

        for k in range(full):

            @pl.when((s_ref[1] == 0) & (pl.program_id(0) == k))
            def _():
                for a in range(half):
                    for v in range(states):
                        out_ref[0, :, a * states + v] = decoded(came_refs[k][a, v], ops).T

    steps = pl.cdiv(ops, LANES)
    return call(
        body,
        (steps,),
        1,
        [pl.BlockSpec(memory_space=pl.ANY)]
        + [pl.BlockSpec((half, states, LANES, LANES), lambda i, s: (0, 0, i, 0))] * full
        + [pl.BlockSpec((half, states, ops - wide, LANES), lambda i, s: (0, 0, 0, i))]
        + [pl.BlockSpec((full, half, half, LANES, LANES), lambda i, s: (0, 0, 0, i, 0))]
        + [pl.BlockSpec((full, half, half, 16, LANES), lambda i, s: (0, 0, 0, ops // 16, 0))]
        + [pl.BlockSpec((half, half, last.shape[2], LANES), lambda i, s: (0, 0, 0, i))]
        + [whole(c.shape) for c in came],
        [pl.BlockSpec((1, LANES, tiles, ops), lambda i, s: (0, i, 0, 0))],
        [f32(*out.shape)],
        after,
        {1: 0},
    )(place_in, out, *finished, turned, turned, last, *came)


def finish(place_in, out, last):
    _, ops, tiles, _ = out.shape
    half, states, _, _ = last.shape
    rest = ops % LANES

    def body(s_ref, out_in, last_ref, out_ref, rows_ref, sem):
        @pl.when(s_ref[1] == 0)
        def _():
            for a in range(half):
                for v in range(states):
                    rows_ref[:, a * states + v] = decoded(last_ref[a, v], rest)
            copy = pltpu.make_async_copy(rows_ref, out_ref.at[0, pl.ds(ops - rest, rest)], sem)
            copy.start()
            copy.wait()

    return pl.pallas_call(
        body,
        in_specs=[
            pl.BlockSpec(memory_space=pltpu.SMEM),
            pl.BlockSpec(memory_space=pl.ANY),
            pl.BlockSpec(memory_space=pltpu.VMEM),
        ],
        out_specs=pl.BlockSpec(memory_space=pl.ANY),
        out_shape=f32(*out.shape),
        input_output_aliases={1: 0},
        scratch_shapes=[pltpu.VMEM((rest, tiles, ops), jnp.float32), pltpu.SemaphoreType.DMA],
    )(place_in, out, last)


def paired(amplitudes):
    blocks = lax.axis_size("state")
    far = blocks.bit_length() - 2
    states, depth, ops = amplitudes.shape
    full = ops // LANES
    wide = full * LANES
    both = ("state", "det")
    senders = [s for s in range(blocks) if (s & 1) == (s >> far & 1)]
    receivers = [s for s in range(blocks) if s not in senders]
    over = [(2 * s + x, 2 * (s ^ 1 << far) + x) for s in senders for x in range(2)]
    back = [(b, a) for a, b in over]
    across = [(2 * s + x, 2 * s + 1 - x) for s in receivers for x in range(2)]
    first_across = [(2 * s + x, 2 * s + 1 - x) for s in range(0, blocks, 2) for x in range(2)]
    to_second = [(2 * s + x, 2 * (s + 1) + x) for s in range(0, blocks, 2) for x in range(2)]

    state = lax.axis_index("state")
    x = lax.axis_index("det").astype(jnp.int32)
    det = x[None]
    receiver = ((state & 1) ^ (state >> far & 1)).astype(jnp.int32)
    core = (state & 1).astype(jnp.int32)

    partner = lax.ppermute(amplitudes, "state", [(s, s ^ 1) for s in range(blocks)])
    first = amplitudes[:, :, :LANES].transpose(0, 2, 1)
    first, later = lax.optimization_barrier((first.reshape(states * LANES, depth), amplitudes))
    got = [lax.ppermute(first, both, over)]
    own = later.transpose(0, 2, 1)
    partner, own = lax.optimization_barrier((partner, own))
    partner = partner.transpose(0, 2, 1)

    crossed, token = near_send(det, own, partner, False, (first,))
    crossed = lax.ppermute(crossed, "det", [(0, 1), (1, 0)])
    doubled, token = near_send(det, own, partner, True, (token,))
    doubled = lax.ppermute(doubled, both, first_across)
    whole_own, token = lax.optimization_barrier((own, token))
    widths = [LANES] * full + [ops - wide]
    later = [
        whole_own[:, k * LANES : k * LANES + w].reshape(states * w, depth) for k, w in enumerate(widths) if k
    ]
    later, token = lax.optimization_barrier((jnp.concatenate(later), token))
    got.append(lax.ppermute(later, both, over))
    keep, token = near_keep(det, own, partner, (token,))
    def terms(k, mine, *done):
        start = states * LANES * (k - 1) if k else 0
        return far_terms(det, own, got[min(k, 1)], start, widths[k], k < full, mine, done)

    finished, codes, crossing, kepts, came = [], [], [], [], []

    def sum_up(k, token):
        rows = ops if k < full else widths[k]
        others = finished[:k] if k == full - 1 else [] if k == full else None
        tiles, code, *cross, token = far_sum(det, kepts[k], came[k], rows, k < full, others, (token,))
        codes.append(lax.ppermute(code, both, back))
        crossing.extend(lax.ppermute(c, both, across) for c in cross)
        finished.append(tiles)
        return token

    kept, token = terms(0, True, token)
    kepts.append(kept)
    share, token = near_share(det, keep, doubled, states, (token, crossed))
    given = lax.ppermute(share, both, to_second)
    for k in range(full + 1):
        send, token = terms(k, False, token)
        came.append(lax.ppermute(send, both, across))
        if k == 0:
            out, token = near_sum(jnp.stack([x, core]), keep, crossed, share, given, states, (token,))
    token = sum_up(0, token)
    for k in range(1, full + 1):
        kept, token = terms(k, True, token)
        kepts.append(kept)
    for k in range(1, full + 1):
        token = sum_up(k, token)

    at = jnp.stack([x, receiver])
    crossing[1] = crossing[1].reshape(crossing[1].shape[1:])
    out, token = place(at, out, finished, crossing, codes[:full], (token,))
    last, out = lax.optimization_barrier((codes[full], out))
    return finish(at, out, last).transpose(0, 2, 1, 3)


def partner_2(value, axis, stride):
    mask = 2**stride
    pairs = [(source, source ^ mask) for source in range(lax.axis_size(axis))]
    return lax.ppermute(value, axis, pairs)


def pair_terms(own_block, partner, count):
    operators = own_block.shape[2]
    terms = jnp.einsum("adp,bdq->abpq", own_block, partner, preferred_element_type=jnp.float32)
    return terms.reshape(count, operators, operators)


def exchanged(amplitudes):
    blocks = lax.axis_size("state")
    far_bit = blocks.bit_length() - 2
    states = amplitudes.shape[0]
    gathered = []
    for bit in (far_bit, 0):
        partner = partner_2(amplitudes, "state", bit)
        terms = pair_terms(amplitudes, partner, states * states)
        gathered.append(lax.psum_scatter(terms, "det", scatter_dimension=0, tiled=True))
    return jnp.stack(gathered)


def on_device(amplitudes):
    states, _, ops = amplitudes.shape
    two = lax.axis_size("det") == 2 and lax.axis_size("state") >= 4
    if two and states % 2 == 0 and ops > LANES and ops % LANES % 8:
        return paired(amplitudes)
    return exchanged(amplitudes)


def solution(mesh):
    return jax.shard_map(
        on_device,
        mesh=mesh,
        in_specs=(P("state", "det", None),),
        out_specs=P(None, ("state", "det"), None, None),
        check_vma=False,
    )
```

```python
import functools

import jax
import jax.numpy as jnp
from jax import lax
from jax.experimental import pallas as pl
from jax.experimental.pallas import tpu as pltpu
from jax.sharding import PartitionSpec as P

LANES = 128
VMEM_LIMIT = 20 * 2**20
POWER, LIFT = 10, 11
SMALLEST = 2.0**-110


def contract_last(left, right):
    return lax.dot_general(left, right, (((1,), (1,)), ((), ())), preferred_element_type=jnp.float32)


def call(body, grid, scalars, in_specs, out_specs, out_shape, after=(), aliases={}, scratch=()):
    idle = len(after)

    def waiting(*refs):
        first = scalars + len(in_specs)
        last = first + idle + len(out_specs)
        body(*refs[:first], *refs[first + idle : last], *refs[last + 1 :])
        refs[last][...] = jnp.zeros_like(refs[last])

    token = (8, LANES)
    kernel = pl.pallas_call(
        waiting,
        grid_spec=pltpu.PrefetchScalarGridSpec(
            num_scalar_prefetch=scalars,
            grid=grid,
            in_specs=in_specs + [pl.BlockSpec(memory_space=pl.ANY)] * idle,
            out_specs=[*out_specs, whole(token)],
            scratch_shapes=scratch,
        ),
        out_shape=[*out_shape, f32(*token)],
        input_output_aliases=aliases,
        compiler_params=pltpu.CompilerParams(vmem_limit_bytes=VMEM_LIMIT),
    )
    return lambda *operands: kernel(*operands, *after)


def f32(*shape):
    return jax.ShapeDtypeStruct(shape, jnp.float32)


def up(size, unit):
    return -(-size // unit) * unit


def whole(shape):
    return pl.BlockSpec(shape, lambda *_: (0,) * len(shape), pipeline_mode=pl.Buffered(1))


class Packing:
    def __init__(self, tiles, ops):
        self.ops, self.wide = ops, ops // LANES * LANES
        self.rest, self.below = ops - self.wide, up(ops, 8)
        self.each = self.below + up(self.rest, 8)
        beside = self.wide // LANES
        self.corners = [
            (tiles * self.each + t // beside * up(self.rest, 8), t % beside * LANES) for t in range(tiles)
        ]
        self.shape = (tiles * self.each + pl.cdiv(tiles, beside) * up(self.rest, 8), self.wide)

    def store(self, wire_ref, t, main, turned):
        row, lane = self.corners[t]
        wire_ref[t * self.each : t * self.each + self.ops] = main
        start = t * self.each + self.below
        wire_ref[start : start + self.rest] = turned[:, : self.wide]
        wire_ref[row : row + self.rest, lane : lane + self.rest] = turned[:, self.wide :]

    def parts(self, wire_ref, t):
        row, lane = self.corners[t]
        start, padded = t * self.each + self.below, up(self.rest, 8)
        head, tail = slice(0, self.wide), slice(self.wide, self.ops)
        side = wire_ref[start : start + padded].T[:, : self.rest]
        corner = wire_ref[row : row + padded, lane : lane + LANES].T[: self.rest, : self.rest]
        main = wire_ref[t * self.each : t * self.each + self.ops]
        return [(slice(0, self.ops), head, main), (head, tail, side), (tail, tail, corner)]


def near_send(det, own, partner, to_mine, after=()):
    states, ops, depth = own.shape
    half, tiles = states // 2, (states // 2) ** 2
    packing = Packing(tiles, ops)

    def body(x_ref, own_ref, partner_ref, wire_ref):
        main = contract_last(own_ref[0], partner_ref[0, : packing.wide])
        turned = contract_last(partner_ref[0, packing.wide :], own_ref[0])
        for t in range(tiles):

            @pl.when(pl.program_id(0) == t)
            def _():
                packing.store(wire_ref, t, main, turned)

    def second(x):
        return half * (1 - x[0]) if to_mine else half * x[0]

    return call(
        body,
        (tiles,),
        1,
        [
            pl.BlockSpec((1, ops, depth), lambda t, x: (half * (1 - x[0]) + t // half, 0, 0)),
            pl.BlockSpec((1, ops, depth), lambda t, x: (second(x) + t % half, 0, 0)),
        ],
        [whole(packing.shape)],
        [f32(*packing.shape)],
        after,
    )(det, own, partner)


def near_keep(det, own, partner, after=()):
    states, ops, depth = own.shape
    half = states // 2

    def body(x_ref, own_ref, partner_ref, tile_ref):
        tile_ref[0] = contract_last(own_ref[0], partner_ref[0])

    return call(
        body,
        (half, states),
        1,
        [
            pl.BlockSpec((1, ops, depth), lambda a, b, x: (half * x[0] + a, 0, 0)),
            pl.BlockSpec((1, ops, depth), lambda a, b, x: (b, 0, 0)),
        ],
        [pl.BlockSpec((1, ops, ops), lambda a, b, x: (a * states + b, 0, 0))],
        [f32(half * states, ops, ops)],
        after,
    )(det, own, partner)


def near_share(det, keep, doubled, states, after=()):
    _, ops, _ = keep.shape
    half, tiles = states // 2, (states // 2) ** 2
    packing = Packing(tiles, ops)
    shape = (tiles, up(ops, 8), up(ops, LANES))

    def body(x_ref, keep_ref, wire_ref, tile_ref):
        for t in range(tiles):
            kept = t // half * states + half * x_ref[0] + t % half
            for rows, columns, values in packing.parts(wire_ref, t):
                tile_ref[t, rows, columns] = keep_ref[kept, rows, columns] + values

    return call(
        body, (1,), 1, [whole(keep.shape), whole(packing.shape)], [whole(shape)], [f32(*shape)], after
    )(det, keep, doubled)


def near_sum(place_in, keep, crossed, share, given, states, after=()):
    tiles, ops, _ = keep.shape
    half = states // 2
    packing = Packing(half * half, ops)

    def body(s_ref, keep_ref, wire_ref, share_ref, given_ref, out_ref):
        x, core = s_ref[0], s_ref[1]
        for a in range(half):
            for b in range(states):
                t, one, turned = a * states + b, a * half + b % half, b % half * half + a

                @pl.when(b // half != x)
                def _():
                    for rows, columns, values in packing.parts(wire_ref, one):
                        out_ref[0, rows, t, columns] = keep_ref[t, rows, columns] + values

                @pl.when((b // half == x) & (core == 0))
                def _():
                    out_ref[0, :, t] = share_ref[one, :ops, :ops]

                @pl.when((b // half == x) & (core == 1))
                def _():
                    out_ref[0, :, t] = given_ref[turned].T[:ops, :ops]

    return call(
        body,
        (1,),
        1,
        [whole(keep.shape), whole(packing.shape), whole(share.shape), whole(given.shape)],
        [pl.BlockSpec((1, ops, tiles, ops), lambda i, s: (1, 0, 0, 0), pipeline_mode=pl.Buffered(1))],
        [f32(2, ops, tiles, ops)],
        after,
    )(place_in, keep, crossed, share, given)


def far_terms(det, own, got, start, width, turned, mine, after=()):
    states, ops, depth = own.shape
    half = states // 2
    rows = ops if turned else width
    tile = (up(ops, 8), width) if turned else (up(width, 8), ops)

    def first(x):
        return half * x if mine else half * (1 - x)

    def body(x_ref, own_ref, got_ref, out_ref):
        if turned:
            both = contract_last(own_ref[0], got_ref[...])
            parts = [both[:, a * width : (a + 1) * width] for a in range(half)]
        else:
            every = contract_last(got_ref[...], own_ref[0])
            parts = [every[u * width : (u + 1) * width] for u in range(states)]
            parts = [jnp.where(first(x_ref[0]) == 0, parts[a], parts[half + a]) for a in range(half)]
        for a in range(half):
            out_ref[a, 0, :rows] = parts[a]

    picked = half if turned else states

    def rows_in(v, x):
        return (start + first(x[0]) * width if turned else start, 0)

    return call(
        body,
        (states,),
        1,
        [
            pl.BlockSpec((1, ops, depth), lambda v, x: (v, 0, 0)),
            pl.BlockSpec(
                (pl.Element(picked * width), pl.Element(depth)), rows_in, pipeline_mode=pl.Buffered(1)
            ),
        ],
        [pl.BlockSpec((half, 1, *tile), lambda v, x: (0, v, 0, 0))],
        [f32(half, states, *tile)],
        after,
    )(det, own, got)


def far_sum(det, keep, came, rows, turned, after=()):
    half, states, _, lanes = keep.shape
    shape = (up(rows + 1, 8), lanes)

    def body(x_ref, keep_ref, came_ref, tile_ref, code_ref, cross_ref):
        x = x_ref[0]
        top = jnp.zeros((rows, lanes), jnp.float32)
        for a in range(half):
            for v in range(states):
                top = jnp.maximum(top, jnp.abs(keep_ref[a, v, :rows] + came_ref[a, v, :rows]))
        exponent = jnp.floor(jnp.log2(jnp.maximum(jnp.max(top, keepdims=True), SMALLEST)))
        scale = jnp.exp2(LIFT - exponent)
        below = jnp.broadcast_to(exponent, (shape[0] - rows, lanes))
        for a in range(half):
            for v in range(states):
                tile = keep_ref[a, v, :rows] + came_ref[a, v, :rows]
                code_ref[a, v] = jnp.concatenate([powered(tile * scale), below]).astype(jnp.bfloat16)
            for b in range(half):
                v = half * x + b
                tile_ref[a, b] = keep_ref[a, v, :rows] + came_ref[a, v, :rows]
                cross_ref[a, b] = code_ref[a, half * (1 - x) + b]

    shapes = [(half, half, rows, lanes), (half, states, *shape), (half, half, *shape)]
    kinds = [jnp.float32, jnp.bfloat16, jnp.bfloat16]
    return call(
        body,
        (1,),
        1,
        [whole(keep.shape)] * 2,
        [whole(s) for s in shapes],
        [jax.ShapeDtypeStruct(s, kind) for s, kind in zip(shapes, kinds)],
        after,
    )(det, keep, came)


def powered(value):
    square = value * value
    fourth = square * square
    return value * jnp.abs(value) * (fourth * fourth)


def decoded(code, rows):
    code = code.astype(jnp.float32)
    value, exponent = code[:rows], code[rows : rows + 1]
    root = jnp.exp2(jnp.log2(jnp.abs(value)) * (1 / POWER)) * jnp.exp2(exponent - LIFT)
    return jnp.where(value < 0, -root, root)


def into_place(role, place_in, out, pieces, after=()):
    tiles = out.shape[2]
    sources = [v for piece in pieces for v in piece[2]]
    count = len(sources)

    def body(s_ref, out_in, *refs):
        out_ref, held, made, sems = refs[count], refs[count + 1 : 2 * count + 1], refs[2 * count + 1 : -1], refs[-1]

        @pl.when(s_ref[1] == role)
        def _():
            loads = [pltpu.make_async_copy(refs[k], held[k], sems.at[k]) for k in range(count)]
            for load in loads:
                load.start()
            stores, first = [], 0
            for k, (rows, lanes, own, fill) in enumerate(pieces):
                for load in loads[first : first + len(own)]:
                    load.wait()
                fill(s_ref[0], held[first : first + len(own)], made[k])
                first += len(own)
                target = out_ref.at[0, pl.ds(*rows), :, pl.ds(*lanes)]
                stores.append(pltpu.make_async_copy(made[k], target, sems.at[count + k]))
                stores[k].start()
            for store in stores:
                store.wait()

    return call(
        body,
        (1,),
        1,
        [pl.BlockSpec(memory_space=pl.ANY)] * (1 + count),
        [pl.BlockSpec(memory_space=pl.ANY)],
        [f32(*out.shape)],
        after,
        {1: 0},
        [pltpu.VMEM(v.shape, v.dtype) for v in sources]
        + [pltpu.VMEM((rows[1], tiles, lanes[1]), jnp.float32) for rows, lanes, *_ in pieces]
        + [pltpu.SemaphoreType.DMA((count + len(pieces),))],
    )(place_in, out, *sources)


def returned_piece(code, start, width, ops):
    half, states, _, _ = code.shape
    turned = code.shape[3] == width

    def fill(x, refs, ref):
        for a in range(half):
            for v in range(states):
                one = refs[0][a, v]
                ref[:, a * states + v] = decoded(one, ops).T if turned else decoded(one, width)

    return (start, width), (0, ops), (code,), fill


def finished_piece(tiles, cross, start, width, ops):
    half, _, rows, _ = tiles.shape
    turned = rows == ops

    def fill(x, refs, ref):
        for b in range(half):
            for u in range(2 * half):
                a, t = u % half, 2 * half * b + u

                @pl.when(u // half == x)
                def _():
                    ref[:, t] = refs[0][a, b] if turned else refs[0][a, b].T

                @pl.when(u // half != x)
                def _():
                    one = decoded(refs[1][a, b], rows)
                    ref[:, t] = one if turned else one.T

    return (0, ops), (start, width), (tiles, cross), fill


def paired(amplitudes):
    blocks = lax.axis_size("state")
    far = blocks.bit_length() - 2
    states, depth, ops = amplitudes.shape
    full = ops // LANES
    wide = full * LANES
    both = ("state", "det")
    senders = [s for s in range(blocks) if (s & 1) == (s >> far & 1)]
    receivers = [s for s in range(blocks) if s not in senders]
    over = [(2 * s + x, 2 * (s ^ 1 << far) + x) for s in senders for x in range(2)]
    back = [(b, a) for a, b in over]
    across = [(2 * s + x, 2 * s + 1 - x) for s in receivers for x in range(2)]
    first_across = [(2 * s + x, 2 * s + 1 - x) for s in range(0, blocks, 2) for x in range(2)]
    to_second = [(2 * s + x, 2 * (s + 1) + x) for s in range(0, blocks, 2) for x in range(2)]

    state = lax.axis_index("state")
    x = lax.axis_index("det").astype(jnp.int32)
    det = x[None]
    receiver = ((state & 1) ^ (state >> far & 1)).astype(jnp.int32)
    core = (state & 1).astype(jnp.int32)

    partner = lax.ppermute(amplitudes, "state", [(s, s ^ 1) for s in range(blocks)])
    first = amplitudes[:, :, :LANES].transpose(0, 2, 1)
    first, later = lax.optimization_barrier((first.reshape(states * LANES, depth), amplitudes))
    got = [lax.ppermute(first, both, over)]
    own = later.transpose(0, 2, 1)
    partner, own = lax.optimization_barrier((partner, own))
    partner = partner.transpose(0, 2, 1)

    crossed, token = near_send(det, own, partner, False, (first,))
    crossed = lax.ppermute(crossed, "det", [(0, 1), (1, 0)])
    doubled, token = near_send(det, own, partner, True, (token,))
    doubled = lax.ppermute(doubled, both, first_across)
    whole_own, token = lax.optimization_barrier((own, token))
    widths = [LANES] * full + [ops - wide]
    later = [
        whole_own[:, k * LANES : k * LANES + w].reshape(states * w, depth) for k, w in enumerate(widths) if k
    ]
    later, token = lax.optimization_barrier((jnp.concatenate(later), token))
    got.append(lax.ppermute(later, both, over))
    keep, token = near_keep(det, own, partner, (token,))
    def terms(k, mine, *done):
        start = states * LANES * (k - 1) if k else 0
        return far_terms(det, own, got[min(k, 1)], start, widths[k], k < full, mine, done)

    codes, mine, kepts, came = [], [], [], []

    def sum_up(k, token):
        rows = ops if k < full else widths[k]
        tiles, code, cross, token = far_sum(det, kepts[k], came[k], rows, k < full, (token,))
        place = k * LANES, widths[k], ops
        codes.append(returned_piece(lax.ppermute(code, both, back), *place))
        mine.append(finished_piece(tiles, lax.ppermute(cross, both, across), *place))
        return token

    kept, token = terms(0, True, token)
    kepts.append(kept)
    share, token = near_share(det, keep, doubled, states, (token, crossed))
    given = lax.ppermute(share, both, to_second)
    for k in range(full + 1):
        send, token = terms(k, False, token)
        came.append(lax.ppermute(send, both, across))
        if k == 0:
            out, token = near_sum(jnp.stack([x, core]), keep, crossed, share, given, states, (token,))
        if k == 1:
            token = sum_up(0, token)
    for k in range(1, full + 1):
        kept, token = terms(k, True, token)
        kepts.append(kept)
    for k in range(1, full + 1):
        token = sum_up(k, token)

    at = jnp.stack([x, receiver])
    for role, pieces in ((0, codes[:full]), (1, mine[:full]), (1, mine[full:]), (0, codes[full:])):
        out, token = into_place(role, at, out, pieces, (token,))
    return out.transpose(0, 2, 1, 3)


def partner_2(value, axis, stride):
    mask = 2**stride
    pairs = [(source, source ^ mask) for source in range(lax.axis_size(axis))]
    return lax.ppermute(value, axis, pairs)


def pair_terms(own_block, partner, count):
    operators = own_block.shape[2]
    terms = jnp.einsum("adp,bdq->abpq", own_block, partner, preferred_element_type=jnp.float32)
    return terms.reshape(count, operators, operators)


def exchanged(amplitudes):
    blocks = lax.axis_size("state")
    far_bit = blocks.bit_length() - 2
    states = amplitudes.shape[0]
    gathered = []
    for bit in (far_bit, 0):
        partner = partner_2(amplitudes, "state", bit)
        terms = pair_terms(amplitudes, partner, states * states)
        gathered.append(lax.psum_scatter(terms, "det", scatter_dimension=0, tiled=True))
    return jnp.stack(gathered)


def on_device(amplitudes):
    states, _, ops = amplitudes.shape
    two = lax.axis_size("det") == 2 and lax.axis_size("state") >= 4
    if two and states % 2 == 0 and ops > LANES and ops % LANES % 8:
        return paired(amplitudes)
    return exchanged(amplitudes)


def solution(mesh):
    return jax.shard_map(
        on_device,
        mesh=mesh,
        in_specs=(P("state", "det", None),),
        out_specs=P(None, ("state", "det"), None, None),
        check_vma=False,
    )
```

```python
import functools

import jax
import jax.numpy as jnp
from jax import lax
from jax.experimental import pallas as pl
from jax.experimental.pallas import tpu as pltpu
from jax.sharding import PartitionSpec as P

LANES = 128
VMEM_LIMIT = 20 * 2**20
POWER, LIFT = 10, 11
SMALLEST = 2.0**-110
LONG = 10**10


def contract_last(left, right):
    return lax.dot_general(left, right, (((1,), (1,)), ((), ())), preferred_element_type=jnp.float32)


def call(body, grid, scalars, in_specs, out_specs, out_shape, after=(), aliases={}, scratch=(), declared=0):
    idle = len(after)

    def waiting(*refs):
        first = scalars + len(in_specs)
        last = first + idle + len(out_specs)
        body(*refs[:first], *refs[first + idle : last], *refs[last + 1 :])
        refs[last][...] = jnp.zeros_like(refs[last])

    token = (8, LANES)
    kernel = pl.pallas_call(
        waiting,
        grid_spec=pltpu.PrefetchScalarGridSpec(
            num_scalar_prefetch=scalars,
            grid=grid,
            in_specs=in_specs + [pl.BlockSpec(memory_space=pl.ANY)] * idle,
            out_specs=[*out_specs, whole(token)],
            scratch_shapes=scratch,
        ),
        out_shape=[*out_shape, f32(*token)],
        input_output_aliases=aliases,
        compiler_params=pltpu.CompilerParams(vmem_limit_bytes=VMEM_LIMIT),
        cost_estimate=pl.CostEstimate(flops=declared, bytes_accessed=declared // 100, transcendentals=0),
    )
    return lambda *operands: kernel(*operands, *after)


def f32(*shape):
    return jax.ShapeDtypeStruct(shape, jnp.float32)


def up(size, unit):
    return -(-size // unit) * unit


def whole(shape):
    return pl.BlockSpec(shape, lambda *_: (0,) * len(shape), pipeline_mode=pl.Buffered(1))


class Packing:
    def __init__(self, tiles, ops):
        self.ops, self.wide = ops, ops // LANES * LANES
        self.rest, self.below = ops - self.wide, up(ops, 8)
        self.each = self.below + up(self.rest, 8)
        beside = self.wide // LANES
        self.corners = [
            (tiles * self.each + t // beside * up(self.rest, 8), t % beside * LANES) for t in range(tiles)
        ]
        self.shape = (tiles * self.each + pl.cdiv(tiles, beside) * up(self.rest, 8), self.wide)

    def store(self, wire_ref, t, main, turned):
        row, lane = self.corners[t]
        wire_ref[t * self.each : t * self.each + self.ops] = main
        start = t * self.each + self.below
        wire_ref[start : start + self.rest] = turned[:, : self.wide]
        wire_ref[row : row + self.rest, lane : lane + self.rest] = turned[:, self.wide :]

    def parts(self, wire_ref, t):
        row, lane = self.corners[t]
        start, padded = t * self.each + self.below, up(self.rest, 8)
        head, tail = slice(0, self.wide), slice(self.wide, self.ops)
        side = wire_ref[start : start + padded].T[:, : self.rest]
        corner = wire_ref[row : row + padded, lane : lane + LANES].T[: self.rest, : self.rest]
        main = wire_ref[t * self.each : t * self.each + self.ops]
        return [(slice(0, self.ops), head, main), (head, tail, side), (tail, tail, corner)]


def near_send(det, own, partner, to_mine, after=()):
    states, ops, depth = own.shape
    half, tiles = states // 2, (states // 2) ** 2
    packing = Packing(tiles, ops)

    def body(x_ref, own_ref, partner_ref, wire_ref):
        main = contract_last(own_ref[0], partner_ref[0, : packing.wide])
        turned = contract_last(partner_ref[0, packing.wide :], own_ref[0])
        for t in range(tiles):

            @pl.when(pl.program_id(0) == t)
            def _():
                packing.store(wire_ref, t, main, turned)

    def second(x):
        return half * (1 - x[0]) if to_mine else half * x[0]

    return call(
        body,
        (tiles,),
        1,
        [
            pl.BlockSpec((1, ops, depth), lambda t, x: (half * (1 - x[0]) + t // half, 0, 0)),
            pl.BlockSpec((1, ops, depth), lambda t, x: (second(x) + t % half, 0, 0)),
        ],
        [whole(packing.shape)],
        [f32(*packing.shape)],
        after,
    )(det, own, partner)


def near_keep(det, own, partner, after=()):
    states, ops, depth = own.shape
    half = states // 2

    def body(x_ref, own_ref, partner_ref, tile_ref):
        tile_ref[0] = contract_last(own_ref[0], partner_ref[0])

    return call(
        body,
        (half, states),
        1,
        [
            pl.BlockSpec((1, ops, depth), lambda a, b, x: (half * x[0] + a, 0, 0)),
            pl.BlockSpec((1, ops, depth), lambda a, b, x: (b, 0, 0)),
        ],
        [pl.BlockSpec((1, ops, ops), lambda a, b, x: (a * states + b, 0, 0))],
        [f32(half * states, ops, ops)],
        after,
    )(det, own, partner)


def near_share(det, keep, doubled, states, after=()):
    _, ops, _ = keep.shape
    half, tiles = states // 2, (states // 2) ** 2
    packing = Packing(tiles, ops)
    shape = (tiles, up(ops, 8), up(ops, LANES))

    def body(x_ref, keep_ref, wire_ref, tile_ref):
        for t in range(tiles):
            kept = t // half * states + half * x_ref[0] + t % half
            for rows, columns, values in packing.parts(wire_ref, t):
                tile_ref[t, rows, columns] = keep_ref[kept, rows, columns] + values

    return call(
        body, (1,), 1, [whole(keep.shape), whole(packing.shape)], [whole(shape)], [f32(*shape)], after
    )(det, keep, doubled)


def near_sum(place_in, keep, crossed, share, given, states, after=()):
    tiles, ops, _ = keep.shape
    half = states // 2
    packing = Packing(half * half, ops)

    def body(s_ref, keep_ref, wire_ref, share_ref, given_ref, out_ref):
        x, core = s_ref[0], s_ref[1]
        for a in range(half):
            for b in range(states):
                t, one, turned = a * states + b, a * half + b % half, b % half * half + a

                @pl.when(b // half != x)
                def _():
                    for rows, columns, values in packing.parts(wire_ref, one):
                        out_ref[0, rows, t, columns] = keep_ref[t, rows, columns] + values

                @pl.when((b // half == x) & (core == 0))
                def _():
                    out_ref[0, :, t] = share_ref[one, :ops, :ops]

                @pl.when((b // half == x) & (core == 1))
                def _():
                    out_ref[0, :, t] = given_ref[turned].T[:ops, :ops]

    return call(
        body,
        (1,),
        1,
        [whole(keep.shape), whole(packing.shape), whole(share.shape), whole(given.shape)],
        [pl.BlockSpec((1, ops, tiles, ops), lambda i, s: (1, 0, 0, 0), pipeline_mode=pl.Buffered(1))],
        [f32(2, ops, tiles, ops)],
        after,
    )(place_in, keep, crossed, share, given)


def far_terms(det, own, got, start, width, turned, mine, after=()):
    states, ops, depth = own.shape
    half = states // 2
    rows = ops if turned else width
    tile = (up(ops, 8), width) if turned else (up(width, 8), ops)

    def first(x):
        return half * x if mine else half * (1 - x)

    def body(x_ref, own_ref, got_ref, out_ref):
        if turned:
            both = contract_last(own_ref[0], got_ref[...])
            parts = [both[:, a * width : (a + 1) * width] for a in range(half)]
        else:
            every = contract_last(got_ref[...], own_ref[0])
            parts = [every[u * width : (u + 1) * width] for u in range(states)]
            parts = [jnp.where(first(x_ref[0]) == 0, parts[a], parts[half + a]) for a in range(half)]
        for a in range(half):
            out_ref[a, 0, :rows] = parts[a]

    picked = half if turned else states

    def rows_in(v, x):
        return (start + first(x[0]) * width if turned else start, 0)

    return call(
        body,
        (states,),
        1,
        [
            pl.BlockSpec((1, ops, depth), lambda v, x: (v, 0, 0)),
            pl.BlockSpec(
                (pl.Element(picked * width), pl.Element(depth)), rows_in, pipeline_mode=pl.Buffered(1)
            ),
        ],
        [pl.BlockSpec((half, 1, *tile), lambda v, x: (0, v, 0, 0))],
        [f32(half, states, *tile)],
        after,
    )(det, own, got)


def far_sum(det, keep, came, rows, turned, after=(), declared=0):
    half, states, _, lanes = keep.shape
    shape = (up(rows + 1, 8), lanes)

    def body(x_ref, keep_ref, came_ref, tile_ref, code_ref):
        x = x_ref[0]
        top = jnp.zeros((rows, lanes), jnp.float32)
        for a in range(half):
            for v in range(states):
                top = jnp.maximum(top, jnp.abs(keep_ref[a, v, :rows] + came_ref[a, v, :rows]))
        exponent = jnp.floor(jnp.log2(jnp.maximum(jnp.max(top, keepdims=True), SMALLEST)))
        scale = jnp.exp2(LIFT - exponent)
        below = jnp.broadcast_to(exponent, (shape[0] - rows, lanes))
        for a in range(half):
            for v in range(states):
                tile = keep_ref[a, v, :rows] + came_ref[a, v, :rows]
                code_ref[a, v] = jnp.concatenate([powered(tile * scale), below]).astype(jnp.bfloat16)
            for b in range(half):
                v = half * x + b
                tile_ref[a, b] = keep_ref[a, v, :rows] + came_ref[a, v, :rows]

    shapes = [(half, half, rows, lanes), (half, states, *shape)]
    kinds = [jnp.float32, jnp.bfloat16]
    return call(
        body,
        (1,),
        1,
        [whole(keep.shape)] * 2,
        [whole(s) for s in shapes],
        [jax.ShapeDtypeStruct(s, kind) for s, kind in zip(shapes, kinds)],
        after,
        declared=declared,
    )(det, keep, came)


def crossing_codes(det, codes, after=()):
    half, states, *tile = codes[0].shape
    shape = (len(codes), half, half, *tile)

    def body(x_ref, *refs):
        for k in range(len(codes)):
            refs[-1][k] = refs[k][...]

    return call(
        body,
        (1,),
        1,
        [pl.BlockSpec((half, half, *tile), lambda i, x: (0, 1 - x[0], 0, 0))] * len(codes),
        [whole(shape)],
        [jax.ShapeDtypeStruct(shape, jnp.bfloat16)],
        after,
    )(det, *codes)


def powered(value):
    square = value * value
    fourth = square * square
    return value * jnp.abs(value) * (fourth * fourth)


def decoded(code, rows):
    code = code.astype(jnp.float32)
    value, exponent = code[:rows], code[rows : rows + 1]
    root = jnp.exp2(jnp.log2(jnp.abs(value)) * (1 / POWER)) * jnp.exp2(exponent - LIFT)
    return jnp.where(value < 0, -root, root)


def into_place(role, place_in, out, pieces, after=(), declared=0):
    tiles = out.shape[2]
    sources = [v for piece in pieces for v, _ in piece[2]]
    picks = [pick for piece in pieces for _, pick in piece[2]]
    count = len(sources)

    def body(s_ref, out_in, *refs):
        out_ref, held, made, sems = refs[count], refs[count + 1 : 2 * count + 1], refs[2 * count + 1 : -1], refs[-1]

        @pl.when(s_ref[1] == role)
        def _():
            loads = [pltpu.make_async_copy(refs[k].at[picks[k]], held[k], sems.at[k]) for k in range(count)]
            for load in loads:
                load.start()
            stores, first = [], 0
            for k, (rows, lanes, own, fill) in enumerate(pieces):
                for load in loads[first : first + len(own)]:
                    load.wait()
                fill(s_ref[0], held[first : first + len(own)], made[k])
                first += len(own)
                target = out_ref.at[0, pl.ds(*rows), :, pl.ds(*lanes)]
                stores.append(pltpu.make_async_copy(made[k], target, sems.at[count + k]))
                stores[k].start()
            for store in stores:
                store.wait()

    return call(
        body,
        (1,),
        1,
        [pl.BlockSpec(memory_space=pl.ANY)] * (1 + count),
        [pl.BlockSpec(memory_space=pl.ANY)],
        [f32(*out.shape)],
        after,
        {1: 0},
        [pltpu.VMEM(v.shape[1:], v.dtype) for v in sources]
        + [pltpu.VMEM((rows[1], tiles, lanes[1]), jnp.float32) for rows, lanes, *_ in pieces]
        + [pltpu.SemaphoreType.DMA((count + len(pieces),))],
        declared,
    )(place_in, out, *sources)


def returned_piece(code, start, width, ops):
    half, states, _, _ = code.shape
    turned = code.shape[3] == width

    def fill(x, refs, ref):
        for a in range(half):
            for v in range(states):
                one = refs[a][v]
                ref[:, a * states + v] = decoded(one, ops).T if turned else decoded(one, width)

    return (start, width), (0, ops), [(code, a) for a in range(half)], fill


def finished_piece(tiles, cross, chunk, start, width, ops):
    half, _, rows, _ = tiles.shape
    turned = rows == ops

    def fill(x, refs, ref):
        for b in range(half):
            for u in range(2 * half):
                a, t = u % half, 2 * half * b + u

                @pl.when(u // half == x)
                def _():
                    ref[:, t] = refs[a][b] if turned else refs[a][b].T

                @pl.when(u // half != x)
                def _():
                    one = decoded(refs[half][a, b], rows)
                    ref[:, t] = one if turned else one.T

    return (0, ops), (start, width), [(tiles, a) for a in range(half)] + [(cross, chunk)], fill


def paired(amplitudes):
    blocks = lax.axis_size("state")
    far = blocks.bit_length() - 2
    states, depth, ops = amplitudes.shape
    full = ops // LANES
    wide = full * LANES
    both = ("state", "det")
    senders = [s for s in range(blocks) if (s & 1) == (s >> far & 1)]
    receivers = [s for s in range(blocks) if s not in senders]
    over = [(2 * s + x, 2 * (s ^ 1 << far) + x) for s in senders for x in range(2)]
    back = [(b, a) for a, b in over]
    across = [(2 * s + x, 2 * s + 1 - x) for s in receivers for x in range(2)]
    first_across = [(2 * s + x, 2 * s + 1 - x) for s in range(0, blocks, 2) for x in range(2)]
    to_second = [(2 * s + x, 2 * (s + 1) + x) for s in range(0, blocks, 2) for x in range(2)]

    state = lax.axis_index("state")
    x = lax.axis_index("det").astype(jnp.int32)
    det = x[None]
    receiver = ((state & 1) ^ (state >> far & 1)).astype(jnp.int32)
    core = (state & 1).astype(jnp.int32)

    partner = lax.ppermute(amplitudes, "state", [(s, s ^ 1) for s in range(blocks)])
    first = amplitudes[:, :, :LANES].transpose(0, 2, 1)
    first, later = lax.optimization_barrier((first.reshape(states * LANES, depth), amplitudes))
    got = [lax.ppermute(first, both, over)]
    own = later.transpose(0, 2, 1)
    partner, own = lax.optimization_barrier((partner, own))
    partner = partner.transpose(0, 2, 1)

    crossed, token = near_send(det, own, partner, False, (first,))
    crossed = lax.ppermute(crossed, "det", [(0, 1), (1, 0)])
    doubled, token = near_send(det, own, partner, True, (token,))
    doubled = lax.ppermute(doubled, both, first_across)
    whole_own, token = lax.optimization_barrier((own, token))
    widths = [LANES] * full + [ops - wide]
    chunk = [whole_own[:, k * LANES : k * LANES + w].reshape(states * w, depth) for k, w in enumerate(widths)]
    last, token = lax.optimization_barrier((chunk[full], token))
    got.append(lax.ppermute(last, both, over))
    later, token = lax.optimization_barrier((jnp.concatenate(chunk[1:full]), token))
    got.append(lax.ppermute(later, both, over))
    keep, token = near_keep(det, own, partner, (token,))
    def terms(k, mine, *done):
        wire, start = (0, 0) if k == 0 else (1, 0) if k == full else (2, states * LANES * (k - 1))
        return far_terms(det, own, got[wire], start, widths[k], k < full, mine, done)

    kepts, came, tiles, codes, mine, theirs = {}, {}, {}, {}, {}, {}

    def place_of(k):
        return k * LANES, widths[k], ops

    def keep_terms(k, token):
        kepts[k], token = terms(k, True, token)
        return token

    def send_terms(k, token):
        send, token = terms(k, False, token)
        came[k] = lax.ppermute(send, both, across)
        return token

    def sum_up(k, token):
        rows = ops if k < full else widths[k]
        declared = LONG if k == early[-1] else 0
        tiles[k], codes[k], token = far_sum(det, kepts[k], came[k], rows, k < full, (token,), declared)
        theirs[k] = returned_piece(lax.ppermute(codes[k], both, back), *place_of(k))
        return token

    def cross(ks, token):
        wire, token = crossing_codes(det, [codes[k] for k in ks], (token,))
        wire = lax.ppermute(wire, both, across)
        for n, k in enumerate(ks):
            mine[k] = finished_piece(tiles[k], wire, n, *place_of(k))
        return token

    early, late = [0, full], list(range(1, full))
    for k in early:
        token = keep_terms(k, token)
    share, token = near_share(det, keep, doubled, states, (token, crossed))
    given = lax.ppermute(share, both, to_second)
    for k in early:
        token = send_terms(k, token)
    out, token = near_sum(jnp.stack([x, core]), keep, crossed, share, given, states, (token,))
    for k in late:
        token = send_terms(k, token)
    for k in early:
        token = sum_up(k, token)
    token = cross([full], token)
    for k in late:
        token = keep_terms(k, token)
    for k in late:
        token = sum_up(k, token)
    turned = list(range(full))
    token = cross(turned, token)

    at = jnp.stack([x, receiver])
    for role, kind, ks in ((0, theirs, early), (1, mine, [full]), (1, mine, turned), (0, theirs, late)):
        declared = LONG if role == 1 else 0
        out, token = into_place(role, at, out, [kind[k] for k in ks], (token,), declared)
    return out.transpose(0, 2, 1, 3)


def partner_2(value, axis, stride):
    mask = 2**stride
    pairs = [(source, source ^ mask) for source in range(lax.axis_size(axis))]
    return lax.ppermute(value, axis, pairs)


def pair_terms(own_block, partner, count):
    operators = own_block.shape[2]
    terms = jnp.einsum("adp,bdq->abpq", own_block, partner, preferred_element_type=jnp.float32)
    return terms.reshape(count, operators, operators)


def exchanged(amplitudes):
    blocks = lax.axis_size("state")
    far_bit = blocks.bit_length() - 2
    states = amplitudes.shape[0]
    gathered = []
    for bit in (far_bit, 0):
        partner = partner_2(amplitudes, "state", bit)
        terms = pair_terms(amplitudes, partner, states * states)
        gathered.append(lax.psum_scatter(terms, "det", scatter_dimension=0, tiled=True))
    return jnp.stack(gathered)


def on_device(amplitudes):
    states, _, ops = amplitudes.shape
    two = lax.axis_size("det") == 2 and lax.axis_size("state") >= 4
    if two and states % 2 == 0 and ops > 2 * LANES and ops % LANES % 8:
        return paired(amplitudes)
    return exchanged(amplitudes)


def solution(mesh):
    return jax.shard_map(
        on_device,
        mesh=mesh,
        in_specs=(P("state", "det", None),),
        out_specs=P(None, ("state", "det"), None, None),
        check_vma=False,
    )
```

```python
import functools

import jax
import jax.numpy as jnp
from jax import lax
from jax.experimental import pallas as pl
from jax.experimental.pallas import tpu as pltpu
from jax.sharding import PartitionSpec as P

LANES = 128
VMEM_LIMIT = 20 * 2**20
POWER, LIFT = 10, 11
SMALLEST = 2.0**-110
LONG = 10**10


def contract_last(left, right):
    return lax.dot_general(left, right, (((1,), (1,)), ((), ())), preferred_element_type=jnp.float32)


def call(body, grid, scalars, in_specs, out_specs, out_shape, after=(), aliases={}, scratch=(), declared=0):
    idle = len(after)

    def waiting(*refs):
        first = scalars + len(in_specs)
        last = first + idle + len(out_specs)
        body(*refs[:first], *refs[first + idle : last], *refs[last + 1 :])
        refs[last][...] = jnp.zeros_like(refs[last])

    token = (8, LANES)
    kernel = pl.pallas_call(
        waiting,
        grid_spec=pltpu.PrefetchScalarGridSpec(
            num_scalar_prefetch=scalars,
            grid=grid,
            in_specs=in_specs + [pl.BlockSpec(memory_space=pl.ANY)] * idle,
            out_specs=[*out_specs, whole(token)],
            scratch_shapes=scratch,
        ),
        out_shape=[*out_shape, f32(*token)],
        input_output_aliases=aliases,
        compiler_params=pltpu.CompilerParams(vmem_limit_bytes=VMEM_LIMIT),
        cost_estimate=pl.CostEstimate(flops=declared, bytes_accessed=declared // 100, transcendentals=0),
    )
    return lambda *operands: kernel(*operands, *after)


def f32(*shape):
    return jax.ShapeDtypeStruct(shape, jnp.float32)


def up(size, unit):
    return -(-size // unit) * unit


def whole(shape):
    return pl.BlockSpec(shape, lambda *_: (0,) * len(shape), pipeline_mode=pl.Buffered(1))


class Packing:
    def __init__(self, tiles, ops):
        self.ops, self.wide = ops, ops // LANES * LANES
        self.rest, self.below = ops - self.wide, up(ops, 8)
        self.each = self.below + up(self.rest, 8)
        beside = self.wide // LANES
        self.corners = [
            (tiles * self.each + t // beside * up(self.rest, 8), t % beside * LANES) for t in range(tiles)
        ]
        self.shape = (tiles * self.each + pl.cdiv(tiles, beside) * up(self.rest, 8), self.wide)

    def store(self, wire_ref, t, main, turned):
        row, lane = self.corners[t]
        wire_ref[t * self.each : t * self.each + self.ops] = main
        start = t * self.each + self.below
        wire_ref[start : start + self.rest] = turned[:, : self.wide]
        wire_ref[row : row + self.rest, lane : lane + self.rest] = turned[:, self.wide :]

    def rows(self, wire_ref, t, start, rows):
        row, lane = self.corners[t]
        under, padded = t * self.each + self.below, up(self.rest, 8)
        if start < self.wide:
            side = wire_ref[under : under + padded, start : start + rows].T[:, : self.rest]
        else:
            side = wire_ref[row : row + padded, lane : lane + LANES].T[:rows, : self.rest]
        return jnp.concatenate([wire_ref[t * self.each + start : t * self.each + start + rows], side], axis=1)

    def parts(self, wire_ref, t):
        row, lane = self.corners[t]
        start, padded = t * self.each + self.below, up(self.rest, 8)
        head, tail = slice(0, self.wide), slice(self.wide, self.ops)
        side = wire_ref[start : start + padded].T[:, : self.rest]
        corner = wire_ref[row : row + padded, lane : lane + LANES].T[: self.rest, : self.rest]
        main = wire_ref[t * self.each : t * self.each + self.ops]
        return [(slice(0, self.ops), head, main), (head, tail, side), (tail, tail, corner)]


def near_send(det, own, partner, to_mine, after=()):
    states, ops, depth = own.shape
    half, tiles = states // 2, (states // 2) ** 2
    packing = Packing(tiles, ops)

    def body(x_ref, own_ref, partner_ref, wire_ref):
        main = contract_last(own_ref[0], partner_ref[0, : packing.wide])
        turned = contract_last(partner_ref[0, packing.wide :], own_ref[0])
        for t in range(tiles):

            @pl.when(pl.program_id(0) == t)
            def _():
                packing.store(wire_ref, t, main, turned)

    def second(x):
        return half * (1 - x[0]) if to_mine else half * x[0]

    return call(
        body,
        (tiles,),
        1,
        [
            pl.BlockSpec((1, ops, depth), lambda t, x: (half * (1 - x[0]) + t // half, 0, 0)),
            pl.BlockSpec((1, ops, depth), lambda t, x: (second(x) + t % half, 0, 0)),
        ],
        [whole(packing.shape)],
        [f32(*packing.shape)],
        after,
    )(det, own, partner)


def near_keep(det, own, partner, after=()):
    states, ops, depth = own.shape
    half = states // 2

    def body(x_ref, own_ref, partner_ref, tile_ref):
        tile_ref[0] = contract_last(own_ref[0], partner_ref[0])

    return call(
        body,
        (half, states),
        1,
        [
            pl.BlockSpec((1, ops, depth), lambda a, b, x: (half * x[0] + a, 0, 0)),
            pl.BlockSpec((1, ops, depth), lambda a, b, x: (b, 0, 0)),
        ],
        [pl.BlockSpec((1, ops, ops), lambda a, b, x: (a * states + b, 0, 0))],
        [f32(half * states, ops, ops)],
        after,
    )(det, own, partner)


def near_share(det, keep, doubled, states, after=()):
    _, ops, _ = keep.shape
    half, tiles = states // 2, (states // 2) ** 2
    packing = Packing(tiles, ops)
    shape = (tiles, up(ops, 8), up(ops, LANES))

    def body(x_ref, keep_ref, wire_ref, tile_ref):
        for t in range(tiles):
            kept = t // half * states + half * x_ref[0] + t % half
            for rows, columns, values in packing.parts(wire_ref, t):
                tile_ref[t, rows, columns] = keep_ref[kept, rows, columns] + values

    return call(
        body, (1,), 1, [whole(keep.shape), whole(packing.shape)], [whole(shape)], [f32(*shape)], after
    )(det, keep, doubled)


def near_sum(place_in, keep, crossed, share, given, states, after=()):
    tiles, ops, _ = keep.shape
    half = states // 2
    packing = Packing(half * half, ops)
    blocks = [(p, min(LANES, ops - p)) for p in range(0, ops, LANES)]

    def body(s_ref, keep_ref, wire_in, share_ref, given_ref, out_ref, kept, wire, mine, *rest):
        made, sems = rest[:-1], rest[-1]
        x, core = s_ref[0], s_ref[1]
        loads = [pltpu.make_async_copy(wire_in, wire, sems.at[0])]
        for a in range(half):
            other = keep_ref.at[pl.ds(a * states + half * (1 - x), half)]
            loads.append(pltpu.make_async_copy(other, kept.at[pl.ds(a * half, half)], sems.at[1 + a]))
        for load in loads:
            load.start()
        for source, which in ((share_ref, 0), (given_ref, 1)):

            @pl.when(core == which)
            def _():
                load = pltpu.make_async_copy(source, mine, sems.at[1 + half])
                load.start()
                load.wait()

        for load in loads:
            load.wait()
        stores = []
        for n, (start, rows) in enumerate(blocks):
            ref = made[n]
            for a in range(half):
                for b in range(states):
                    t, one, turned = a * states + b, a * half + b % half, b % half * half + a

                    @pl.when(b // half != x)
                    def _():
                        ref[:, t] = kept[one, start : start + rows] + packing.rows(wire, one, start, rows)

                    @pl.when((b // half == x) & (core == 0))
                    def _():
                        ref[:, t] = mine[one, start : start + rows, :ops]

                    @pl.when((b // half == x) & (core == 1))
                    def _():
                        ref[:, t] = mine[turned, :, start : start + LANES].T[:rows, :ops]

            target = out_ref.at[1, pl.ds(start, rows)]
            stores.append(pltpu.make_async_copy(ref, target, sems.at[2 + half + n]))
            stores[n].start()
        for store in stores:
            store.wait()

    return call(
        body,
        (1,),
        1,
        [pl.BlockSpec(memory_space=pl.ANY)] * 4,
        [pl.BlockSpec(memory_space=pl.ANY)],
        [f32(2, ops, tiles, ops)],
        after,
        scratch=[
            pltpu.VMEM((half * half, ops, ops), jnp.float32),
            pltpu.VMEM(packing.shape, jnp.float32),
            pltpu.VMEM(share.shape, jnp.float32),
            *[pltpu.VMEM((rows, tiles, ops), jnp.float32) for _, rows in blocks],
            pltpu.SemaphoreType.DMA((2 + half + len(blocks),)),
        ],
    )(place_in, keep, crossed, share, given)


def far_terms(det, own, got, start, width, turned, mine, after=()):
    states, ops, depth = own.shape
    half = states // 2
    rows = ops if turned else width
    tile = (up(ops, 8), width) if turned else (up(width, 8), ops)

    def first(x):
        return half * x if mine else half * (1 - x)

    def body(x_ref, own_ref, got_ref, out_ref):
        if turned:
            both = contract_last(own_ref[0], got_ref[...])
            parts = [both[:, a * width : (a + 1) * width] for a in range(half)]
        else:
            every = contract_last(got_ref[...], own_ref[0])
            parts = [every[u * width : (u + 1) * width] for u in range(states)]
            parts = [jnp.where(first(x_ref[0]) == 0, parts[a], parts[half + a]) for a in range(half)]
        for a in range(half):
            out_ref[a, 0, :rows] = parts[a]

    picked = half if turned else states

    def rows_in(v, x):
        return (start + first(x[0]) * width if turned else start, 0)

    return call(
        body,
        (states,),
        1,
        [
            pl.BlockSpec((1, ops, depth), lambda v, x: (v, 0, 0)),
            pl.BlockSpec(
                (pl.Element(picked * width), pl.Element(depth)), rows_in, pipeline_mode=pl.Buffered(1)
            ),
        ],
        [pl.BlockSpec((half, 1, *tile), lambda v, x: (0, v, 0, 0))],
        [f32(half, states, *tile)],
        after,
    )(det, own, got)


def far_sum(det, keep, came, rows, turned, after=(), declared=0):
    half, states, _, lanes = keep.shape
    shape = (up(rows + 1, 8), lanes)

    def body(x_ref, keep_ref, came_ref, tile_ref, code_ref):
        x = x_ref[0]
        top = jnp.zeros((rows, lanes), jnp.float32)
        for a in range(half):
            for v in range(states):
                top = jnp.maximum(top, jnp.abs(keep_ref[a, v, :rows] + came_ref[a, v, :rows]))
        exponent = jnp.floor(jnp.log2(jnp.maximum(jnp.max(top, keepdims=True), SMALLEST)))
        scale = jnp.exp2(LIFT - exponent)
        below = jnp.broadcast_to(exponent, (shape[0] - rows, lanes))
        for a in range(half):
            for v in range(states):
                tile = keep_ref[a, v, :rows] + came_ref[a, v, :rows]
                code_ref[a, v] = jnp.concatenate([powered(tile * scale), below]).astype(jnp.bfloat16)
            for b in range(half):
                v = half * x + b
                tile_ref[a, b] = keep_ref[a, v, :rows] + came_ref[a, v, :rows]

    shapes = [(half, half, rows, lanes), (half, states, *shape)]
    kinds = [jnp.float32, jnp.bfloat16]
    return call(
        body,
        (1,),
        1,
        [whole(keep.shape)] * 2,
        [whole(s) for s in shapes],
        [jax.ShapeDtypeStruct(s, kind) for s, kind in zip(shapes, kinds)],
        after,
        declared=declared,
    )(det, keep, came)


def crossing_codes(det, codes, after=()):
    half, states, *tile = codes[0].shape
    shape = (len(codes), half, half, *tile)

    def body(x_ref, *refs):
        for k in range(len(codes)):
            refs[-1][k] = refs[k][...]

    return call(
        body,
        (1,),
        1,
        [pl.BlockSpec((half, half, *tile), lambda i, x: (0, 1 - x[0], 0, 0))] * len(codes),
        [whole(shape)],
        [jax.ShapeDtypeStruct(shape, jnp.bfloat16)],
        after,
    )(det, *codes)


def powered(value):
    square = value * value
    fourth = square * square
    return value * jnp.abs(value) * (fourth * fourth)


def decoded(code, rows):
    code = code.astype(jnp.float32)
    value, exponent = code[:rows], code[rows : rows + 1]
    root = jnp.exp2(jnp.log2(jnp.abs(value)) * (1 / POWER)) * jnp.exp2(exponent - LIFT)
    return jnp.where(value < 0, -root, root)


def into_place(role, place_in, out, pieces, after=(), declared=0):
    tiles = out.shape[2]
    sources = [v for piece in pieces for v, _ in piece[2]]
    picks = [pick for piece in pieces for _, pick in piece[2]]
    count = len(sources)

    def body(s_ref, out_in, *refs):
        out_ref, held, made, sems = refs[count], refs[count + 1 : 2 * count + 1], refs[2 * count + 1 : -1], refs[-1]

        @pl.when(s_ref[1] == role)
        def _():
            loads = [pltpu.make_async_copy(refs[k].at[picks[k]], held[k], sems.at[k]) for k in range(count)]
            for load in loads:
                load.start()
            stores, first = [], 0
            for k, (rows, lanes, own, fill) in enumerate(pieces):
                for load in loads[first : first + len(own)]:
                    load.wait()
                fill(s_ref[0], held[first : first + len(own)], made[k])
                first += len(own)
                target = out_ref.at[0, pl.ds(*rows), :, pl.ds(*lanes)]
                stores.append(pltpu.make_async_copy(made[k], target, sems.at[count + k]))
                stores[k].start()
            for store in stores:
                store.wait()

    return call(
        body,
        (1,),
        1,
        [pl.BlockSpec(memory_space=pl.ANY)] * (1 + count),
        [pl.BlockSpec(memory_space=pl.ANY)],
        [f32(*out.shape)],
        after,
        {1: 0},
        [pltpu.VMEM(v.shape[1:], v.dtype) for v in sources]
        + [pltpu.VMEM((rows[1], tiles, lanes[1]), jnp.float32) for rows, lanes, *_ in pieces]
        + [pltpu.SemaphoreType.DMA((count + len(pieces),))],
        declared,
    )(place_in, out, *sources)


def returned_piece(code, start, width, ops):
    half, states, _, _ = code.shape
    turned = code.shape[3] == width

    def fill(x, refs, ref):
        for a in range(half):
            for v in range(states):
                one = refs[a][v]
                ref[:, a * states + v] = decoded(one, ops).T if turned else decoded(one, width)

    return (start, width), (0, ops), [(code, a) for a in range(half)], fill


def finished_piece(tiles, cross, chunk, start, width, ops):
    half, _, rows, _ = tiles.shape
    turned = rows == ops

    def fill(x, refs, ref):
        for b in range(half):
            for u in range(2 * half):
                a, t = u % half, 2 * half * b + u

                @pl.when(u // half == x)
                def _():
                    ref[:, t] = refs[a][b] if turned else refs[a][b].T

                @pl.when(u // half != x)
                def _():
                    one = decoded(refs[half][a, b], rows)
                    ref[:, t] = one if turned else one.T

    return (0, ops), (start, width), [(tiles, a) for a in range(half)] + [(cross, chunk)], fill


def paired(amplitudes):
    blocks = lax.axis_size("state")
    far = blocks.bit_length() - 2
    states, depth, ops = amplitudes.shape
    full = ops // LANES
    wide = full * LANES
    both = ("state", "det")
    senders = [s for s in range(blocks) if (s & 1) == (s >> far & 1)]
    receivers = [s for s in range(blocks) if s not in senders]
    over = [(2 * s + x, 2 * (s ^ 1 << far) + x) for s in senders for x in range(2)]
    back = [(b, a) for a, b in over]
    across = [(2 * s + x, 2 * s + 1 - x) for s in receivers for x in range(2)]
    first_across = [(2 * s + x, 2 * s + 1 - x) for s in range(0, blocks, 2) for x in range(2)]
    to_second = [(2 * s + x, 2 * (s + 1) + x) for s in range(0, blocks, 2) for x in range(2)]

    state = lax.axis_index("state")
    x = lax.axis_index("det").astype(jnp.int32)
    det = x[None]
    receiver = ((state & 1) ^ (state >> far & 1)).astype(jnp.int32)
    core = (state & 1).astype(jnp.int32)

    partner = lax.ppermute(amplitudes, "state", [(s, s ^ 1) for s in range(blocks)])
    first = amplitudes[:, :, :LANES].transpose(0, 2, 1)
    first, later = lax.optimization_barrier((first.reshape(states * LANES, depth), amplitudes))
    got = [lax.ppermute(first, both, over)]
    own = later.transpose(0, 2, 1)
    partner, own = lax.optimization_barrier((partner, own))
    partner = partner.transpose(0, 2, 1)

    crossed, token = near_send(det, own, partner, False, (first,))
    crossed = lax.ppermute(crossed, "det", [(0, 1), (1, 0)])
    doubled, token = near_send(det, own, partner, True, (token,))
    doubled = lax.ppermute(doubled, both, first_across)
    whole_own, token = lax.optimization_barrier((own, token))
    widths = [LANES] * full + [ops - wide]
    chunk = [whole_own[:, k * LANES : k * LANES + w].reshape(states * w, depth) for k, w in enumerate(widths)]
    later, token = lax.optimization_barrier((jnp.concatenate(chunk[1:full]), token))
    got.append(lax.ppermute(later, both, over))
    last, token = lax.optimization_barrier((chunk[full], token))
    got.append(lax.ppermute(last, both, over))
    keep, token = near_keep(det, own, partner, (token,))
    def terms(k, mine, *done):
        wire, start = (0, 0) if k == 0 else (2, 0) if k == full else (1, states * LANES * (k - 1))
        return far_terms(det, own, got[wire], start, widths[k], k < full, mine, done)

    kepts, came, tiles, codes, mine, theirs = {}, {}, {}, {}, {}, {}

    def place_of(k):
        return k * LANES, widths[k], ops

    def keep_terms(k, *token):
        kepts[k], token = terms(k, True, *token)
        return token

    def send_terms(k, token):
        send, token = terms(k, False, token)
        came[k] = lax.ppermute(send, both, across)
        return token

    def sum_up(k, *token):
        rows = ops if k < full else widths[k]
        declared = LONG if k in early else 0
        tiles[k], codes[k], token = far_sum(det, kepts[k], came[k], rows, k < full, token, declared)
        theirs[k] = returned_piece(lax.ppermute(codes[k], both, back), *place_of(k))
        return token

    def cross(ks, token):
        wire, token = crossing_codes(det, [codes[k] for k in ks], (token,))
        wire = lax.ppermute(wire, both, across)
        for n, k in enumerate(ks):
            mine[k] = finished_piece(tiles[k], wire, n, *place_of(k))
        return token

    early, late = list(range(full)), [full]
    for k in early:
        token = keep_terms(k, send_terms(k, token))
        if k == 0:
            share, token = near_share(det, keep, doubled, states, (token, crossed))
            given = lax.ppermute(share, both, to_second)
    token = send_terms(full, token)
    for k in early:
        token = sum_up(k, token)
    turned = list(range(full))
    token = cross(turned, token)
    token = keep_terms(full, token, given)
    token = sum_up(full, token)
    token = cross([full], token)
    out, token = near_sum(jnp.stack([x, core]), keep, crossed, share, given, states, (token,))

    at = jnp.stack([x, receiver])
    for role, kind, ks in ((0, theirs, early), (1, mine, early), (1, mine, late), (0, theirs, late)):
        declared = LONG if role == 1 else 0
        out, token = into_place(role, at, out, [kind[k] for k in ks], (token,), declared)
    return out.transpose(0, 2, 1, 3)


def partner_2(value, axis, stride):
    mask = 2**stride
    pairs = [(source, source ^ mask) for source in range(lax.axis_size(axis))]
    return lax.ppermute(value, axis, pairs)


def pair_terms(own_block, partner, count):
    operators = own_block.shape[2]
    terms = jnp.einsum("adp,bdq->abpq", own_block, partner, preferred_element_type=jnp.float32)
    return terms.reshape(count, operators, operators)


def exchanged(amplitudes):
    blocks = lax.axis_size("state")
    far_bit = blocks.bit_length() - 2
    states = amplitudes.shape[0]
    gathered = []
    for bit in (far_bit, 0):
        partner = partner_2(amplitudes, "state", bit)
        terms = pair_terms(amplitudes, partner, states * states)
        gathered.append(lax.psum_scatter(terms, "det", scatter_dimension=0, tiled=True))
    return jnp.stack(gathered)


def on_device(amplitudes):
    states, _, ops = amplitudes.shape
    two = lax.axis_size("det") == 2 and lax.axis_size("state") >= 4
    if two and states % 2 == 0 and ops > 2 * LANES and ops % LANES % 8:
        return paired(amplitudes)
    return exchanged(amplitudes)


def solution(mesh):
    return jax.shard_map(
        on_device,
        mesh=mesh,
        in_specs=(P("state", "det", None),),
        out_specs=P(None, ("state", "det"), None, None),
        check_vma=False,
    )
```

```python
import functools

import jax
import jax.numpy as jnp
from jax import lax
from jax.experimental import pallas as pl
from jax.experimental.pallas import tpu as pltpu
from jax.sharding import PartitionSpec as P

LANES = 128
VMEM_LIMIT = 20 * 2**20
POWER, LIFT = 10, 11
SMALLEST = 2.0**-110
LONG = 10**10


def contract_last(left, right):
    return lax.dot_general(left, right, (((1,), (1,)), ((), ())), preferred_element_type=jnp.float32)


def call(body, grid, scalars, in_specs, out_specs, out_shape, after=(), aliases={}, scratch=(), declared=0):
    idle = len(after)

    def waiting(*refs):
        first = scalars + len(in_specs)
        last = first + idle + len(out_specs)
        body(*refs[:first], *refs[first + idle : last], *refs[last + 1 :])
        refs[last][...] = jnp.zeros_like(refs[last])

    token = (8, LANES)
    kernel = pl.pallas_call(
        waiting,
        grid_spec=pltpu.PrefetchScalarGridSpec(
            num_scalar_prefetch=scalars,
            grid=grid,
            in_specs=in_specs + [pl.BlockSpec(memory_space=pl.ANY)] * idle,
            out_specs=[*out_specs, whole(token)],
            scratch_shapes=scratch,
        ),
        out_shape=[*out_shape, f32(*token)],
        input_output_aliases=aliases,
        compiler_params=pltpu.CompilerParams(vmem_limit_bytes=VMEM_LIMIT),
        cost_estimate=pl.CostEstimate(flops=declared, bytes_accessed=declared // 100, transcendentals=0),
    )
    return lambda *operands: kernel(*operands, *after)


def f32(*shape):
    return jax.ShapeDtypeStruct(shape, jnp.float32)


def up(size, unit):
    return -(-size // unit) * unit


def whole(shape):
    return pl.BlockSpec(shape, lambda *_: (0,) * len(shape), pipeline_mode=pl.Buffered(1))


class Packing:
    def __init__(self, tiles, ops):
        self.ops, self.wide = ops, ops // LANES * LANES
        self.rest, self.below = ops - self.wide, up(ops, 8)
        self.each = self.below + up(self.rest, 8)
        beside = self.wide // LANES
        self.corners = [
            (tiles * self.each + t // beside * up(self.rest, 8), t % beside * LANES) for t in range(tiles)
        ]
        self.shape = (tiles * self.each + pl.cdiv(tiles, beside) * up(self.rest, 8), self.wide)

    def store(self, wire_ref, t, main, turned):
        row, lane = self.corners[t]
        wire_ref[t * self.each : t * self.each + self.ops] = main
        start = t * self.each + self.below
        wire_ref[start : start + self.rest] = turned[:, : self.wide]
        wire_ref[row : row + self.rest, lane : lane + self.rest] = turned[:, self.wide :]

    def rows(self, wire_ref, t, start, rows):
        row, lane = self.corners[t]
        under, padded = t * self.each + self.below, up(self.rest, 8)
        if start < self.wide:
            side = wire_ref[under : under + padded, start : start + rows].T[:, : self.rest]
        else:
            side = wire_ref[row : row + padded, lane : lane + LANES].T[:rows, : self.rest]
        return jnp.concatenate([wire_ref[t * self.each + start : t * self.each + start + rows], side], axis=1)

    def parts(self, wire_ref, t):
        row, lane = self.corners[t]
        start, padded = t * self.each + self.below, up(self.rest, 8)
        head, tail = slice(0, self.wide), slice(self.wide, self.ops)
        side = wire_ref[start : start + padded].T[:, : self.rest]
        corner = wire_ref[row : row + padded, lane : lane + LANES].T[: self.rest, : self.rest]
        main = wire_ref[t * self.each : t * self.each + self.ops]
        return [(slice(0, self.ops), head, main), (head, tail, side), (tail, tail, corner)]


def near_send(det, own, partner, to_mine, after=()):
    states, ops, depth = own.shape
    half, tiles = states // 2, (states // 2) ** 2
    packing = Packing(tiles, ops)

    def body(x_ref, own_ref, partner_ref, wire_ref):
        main = contract_last(own_ref[0], partner_ref[0, : packing.wide])
        turned = contract_last(partner_ref[0, packing.wide :], own_ref[0])
        for t in range(tiles):

            @pl.when(pl.program_id(0) == t)
            def _():
                packing.store(wire_ref, t, main, turned)

    def second(x):
        return half * (1 - x[0]) if to_mine else half * x[0]

    return call(
        body,
        (tiles,),
        1,
        [
            pl.BlockSpec((1, ops, depth), lambda t, x: (half * (1 - x[0]) + t // half, 0, 0)),
            pl.BlockSpec((1, ops, depth), lambda t, x: (second(x) + t % half, 0, 0)),
        ],
        [whole(packing.shape)],
        [f32(*packing.shape)],
        after,
    )(det, own, partner)


def near_keep(det, own, partner, after=()):
    states, ops, depth = own.shape
    half = states // 2

    def body(x_ref, own_ref, partner_ref, tile_ref):
        tile_ref[0] = contract_last(own_ref[0], partner_ref[0])

    return call(
        body,
        (half, states),
        1,
        [
            pl.BlockSpec((1, ops, depth), lambda a, b, x: (half * x[0] + a, 0, 0)),
            pl.BlockSpec((1, ops, depth), lambda a, b, x: (b, 0, 0)),
        ],
        [pl.BlockSpec((1, ops, ops), lambda a, b, x: (a * states + b, 0, 0))],
        [f32(half * states, ops, ops)],
        after,
    )(det, own, partner)


def near_share(det, keep, doubled, states, after=()):
    _, ops, _ = keep.shape
    half, tiles = states // 2, (states // 2) ** 2
    packing = Packing(tiles, ops)
    shape = (tiles, up(ops, 8), up(ops, LANES))

    def body(x_ref, keep_ref, wire_ref, tile_ref):
        for t in range(tiles):
            kept = t // half * states + half * x_ref[0] + t % half
            for rows, columns, values in packing.parts(wire_ref, t):
                tile_ref[t, rows, columns] = keep_ref[kept, rows, columns] + values

    return call(
        body, (1,), 1, [whole(keep.shape), whole(packing.shape)], [whole(shape)], [f32(*shape)], after
    )(det, keep, doubled)


def near_sum(place_in, keep, crossed, share, given, states, after=()):
    tiles, ops, _ = keep.shape
    half = states // 2
    packing = Packing(half * half, ops)
    blocks = [(p, min(LANES, ops - p)) for p in range(0, ops, LANES)]

    def body(s_ref, keep_ref, wire_in, share_ref, given_ref, out_ref, kept, wire, mine, *rest):
        made, sems = rest[:-1], rest[-1]
        x, core = s_ref[0], s_ref[1]
        loads = [pltpu.make_async_copy(wire_in, wire, sems.at[0])]
        for a in range(half):
            other = keep_ref.at[pl.ds(a * states + half * (1 - x), half)]
            loads.append(pltpu.make_async_copy(other, kept.at[pl.ds(a * half, half)], sems.at[1 + a]))
        for load in loads:
            load.start()
        for source, which in ((share_ref, 0), (given_ref, 1)):

            @pl.when(core == which)
            def _():
                load = pltpu.make_async_copy(source, mine, sems.at[1 + half])
                load.start()
                load.wait()

        for load in loads:
            load.wait()
        stores = []
        for n, (start, rows) in enumerate(blocks):
            ref = made[n]
            for a in range(half):
                for b in range(states):
                    t, one, turned = a * states + b, a * half + b % half, b % half * half + a

                    @pl.when(b // half != x)
                    def _():
                        ref[:, t] = kept[one, start : start + rows] + packing.rows(wire, one, start, rows)

                    @pl.when((b // half == x) & (core == 0))
                    def _():
                        ref[:, t] = mine[one, start : start + rows, :ops]

                    @pl.when((b // half == x) & (core == 1))
                    def _():
                        ref[:, t] = mine[turned, :, start : start + LANES].T[:rows, :ops]

            target = out_ref.at[1, pl.ds(start, rows)]
            stores.append(pltpu.make_async_copy(ref, target, sems.at[2 + half + n]))
            stores[n].start()
        for store in stores:
            store.wait()

    return call(
        body,
        (1,),
        1,
        [pl.BlockSpec(memory_space=pl.ANY)] * 4,
        [pl.BlockSpec(memory_space=pl.ANY)],
        [f32(2, ops, tiles, ops)],
        after,
        scratch=[
            pltpu.VMEM((half * half, ops, ops), jnp.float32),
            pltpu.VMEM(packing.shape, jnp.float32),
            pltpu.VMEM(share.shape, jnp.float32),
            *[pltpu.VMEM((rows, tiles, ops), jnp.float32) for _, rows in blocks],
            pltpu.SemaphoreType.DMA((2 + half + len(blocks),)),
        ],
    )(place_in, keep, crossed, share, given)


def far_terms(det, own, got, start, width, turned, mine, after=(), declared=0):
    states, ops, depth = own.shape
    half = states // 2
    rows = ops if turned else width
    tile = (up(ops, 8), width) if turned else (up(width, 8), ops)

    def first(x):
        return half * x if mine else half * (1 - x)

    def body(x_ref, own_ref, got_ref, out_ref):
        if turned:
            both = contract_last(own_ref[0], got_ref[...])
            parts = [both[:, a * width : (a + 1) * width] for a in range(half)]
        else:
            every = contract_last(got_ref[...], own_ref[0])
            parts = [every[u * width : (u + 1) * width] for u in range(states)]
            parts = [jnp.where(first(x_ref[0]) == 0, parts[a], parts[half + a]) for a in range(half)]
        for a in range(half):
            out_ref[a, 0, :rows] = parts[a]

    picked = half if turned else states

    def rows_in(v, x):
        return (start + first(x[0]) * width if turned else start, 0)

    return call(
        body,
        (states,),
        1,
        [
            pl.BlockSpec((1, ops, depth), lambda v, x: (v, 0, 0)),
            pl.BlockSpec(
                (pl.Element(picked * width), pl.Element(depth)), rows_in, pipeline_mode=pl.Buffered(1)
            ),
        ],
        [pl.BlockSpec((half, 1, *tile), lambda v, x: (0, v, 0, 0))],
        [f32(half, states, *tile)],
        after,
        declared=declared,
    )(det, own, got)


def far_sum(det, keep, came, rows, turned, after=(), declared=0):
    half, states, _, lanes = keep.shape
    shape = (up(rows + 1, 8), lanes)

    def body(x_ref, keep_ref, came_ref, tile_ref, code_ref):
        x = x_ref[0]
        top = jnp.zeros((rows, lanes), jnp.float32)
        for a in range(half):
            for v in range(states):
                top = jnp.maximum(top, jnp.abs(keep_ref[a, v, :rows] + came_ref[a, v, :rows]))
        exponent = jnp.floor(jnp.log2(jnp.maximum(jnp.max(top, keepdims=True), SMALLEST)))
        scale = jnp.exp2(LIFT - exponent)
        below = jnp.broadcast_to(exponent, (shape[0] - rows, lanes))
        for a in range(half):
            for v in range(states):
                tile = keep_ref[a, v, :rows] + came_ref[a, v, :rows]
                code_ref[a, v] = jnp.concatenate([powered(tile * scale), below]).astype(jnp.bfloat16)
            for b in range(half):
                v = half * x + b
                tile_ref[a, b] = keep_ref[a, v, :rows] + came_ref[a, v, :rows]

    shapes = [(half, half, rows, lanes), (half, states, *shape)]
    kinds = [jnp.float32, jnp.bfloat16]
    return call(
        body,
        (1,),
        1,
        [whole(keep.shape)] * 2,
        [whole(s) for s in shapes],
        [jax.ShapeDtypeStruct(s, kind) for s, kind in zip(shapes, kinds)],
        after,
        declared=declared,
    )(det, keep, came)


def crossing_codes(det, codes, after=()):
    half, states, *tile = codes[0].shape
    shape = (len(codes), half, half, *tile)

    def body(x_ref, *refs):
        for k in range(len(codes)):
            refs[-1][k] = refs[k][...]

    return call(
        body,
        (1,),
        1,
        [pl.BlockSpec((half, half, *tile), lambda i, x: (0, 1 - x[0], 0, 0))] * len(codes),
        [whole(shape)],
        [jax.ShapeDtypeStruct(shape, jnp.bfloat16)],
        after,
    )(det, *codes)


def powered(value):
    square = value * value
    fourth = square * square
    return value * jnp.abs(value) * (fourth * fourth)


def rooted(code, exponent):
    code, exponent = code.astype(jnp.float32), exponent.astype(jnp.float32)
    root = jnp.exp2(jnp.log2(jnp.abs(code)) * (1 / POWER)) * jnp.exp2(exponent - LIFT)
    return jnp.where(code < 0, -root, root)


def decoded(code, rows):
    return rooted(code[:rows], code[rows : rows + 1])


def into_place(role, place_in, out, sources, pieces, after=(), declared=0):
    _, ops, tiles, _ = out.shape
    count = len(sources)

    def body(s_ref, out_in, *refs):
        out_ref, held, made, sems = refs[count], refs[count + 1 : 2 * count + 1], refs[2 * count + 1 : -1], refs[-1]

        @pl.when(s_ref[1] == role)
        def _():
            loads = [pltpu.make_async_copy(refs[k], held[k], sems.at[k]) for k in range(count)]
            for load in loads:
                load.start()
            for load in loads:
                load.wait()
            stores = []
            for k, (start, rows, fill) in enumerate(pieces):
                fill(s_ref[0], held, made[k])
                target = out_ref.at[0, pl.ds(start, rows)]
                stores.append(pltpu.make_async_copy(made[k], target, sems.at[count + k]))
                stores[k].start()
            for store in stores:
                store.wait()

    return call(
        body,
        (1,),
        1,
        [pl.BlockSpec(memory_space=pl.ANY)] * (1 + count),
        [pl.BlockSpec(memory_space=pl.ANY)],
        [f32(*out.shape)],
        after,
        {1: 0},
        [pltpu.VMEM(v.shape, v.dtype) for v in sources]
        + [pltpu.VMEM((rows, tiles, ops), jnp.float32) for _, rows, _ in pieces]
        + [pltpu.SemaphoreType.DMA((count + len(pieces),))],
        declared,
    )(place_in, out, *sources)


def returned(codes, chunks, widths, ops):
    def piece(n, k):
        half, states, _, _ = codes[n].shape

        def fill(x, refs, ref):
            for a in range(half):
                for v in range(states):
                    one = refs[n][a, v]
                    last = widths[k] < LANES
                    ref[:, a * states + v] = decoded(one, widths[k]) if last else decoded(one, ops).T

        return k * LANES, widths[k], fill

    return codes, [piece(n, k) for n, k in enumerate(chunks)]


def completed(tiles, turned, last, widths, ops):
    full = len(widths) - 1
    half, _, rest, _ = tiles[full].shape

    def piece(start, rows):
        def fill(x, refs, ref):
            for b in range(half):
                for u in range(2 * half):
                    a, t = u % half, 2 * half * b + u

                    @pl.when(u // half == x)
                    def _():
                        for k in range(full):
                            ref[:, t, k * LANES : (k + 1) * LANES] = refs[k][a, b, start : start + rows]
                        block = refs[full][a, b, :, start : start + rows]
                        ref[:, t, full * LANES :] = block.T

                    @pl.when(u // half != x)
                    def _():
                        for k in range(full):
                            code = refs[full + 1][k, a, b]
                            value = rooted(code[start : start + rows], code[ops : ops + 1])
                            ref[:, t, k * LANES : (k + 1) * LANES] = value
                        code = refs[full + 2][0, a, b, :, start : start + rows]
                        ref[:, t, full * LANES :] = decoded(code, rest).T

        return start, rows, fill

    return [*tiles, turned, last], [piece(p, min(LANES, ops - p)) for p in range(0, ops, LANES)]


def paired(amplitudes):
    blocks = lax.axis_size("state")
    far = blocks.bit_length() - 2
    states, depth, ops = amplitudes.shape
    full = ops // LANES
    wide = full * LANES
    both = ("state", "det")
    senders = [s for s in range(blocks) if (s & 1) == (s >> far & 1)]
    receivers = [s for s in range(blocks) if s not in senders]
    over = [(2 * s + x, 2 * (s ^ 1 << far) + x) for s in senders for x in range(2)]
    back = [(b, a) for a, b in over]
    across = [(2 * s + x, 2 * s + 1 - x) for s in receivers for x in range(2)]
    first_across = [(2 * s + x, 2 * s + 1 - x) for s in range(0, blocks, 2) for x in range(2)]
    to_second = [(2 * s + x, 2 * (s + 1) + x) for s in range(0, blocks, 2) for x in range(2)]

    state = lax.axis_index("state")
    x = lax.axis_index("det").astype(jnp.int32)
    det = x[None]
    receiver = ((state & 1) ^ (state >> far & 1)).astype(jnp.int32)
    core = (state & 1).astype(jnp.int32)

    partner = lax.ppermute(amplitudes, "state", [(s, s ^ 1) for s in range(blocks)])
    first = amplitudes[:, :, :LANES].transpose(0, 2, 1)
    first, later = lax.optimization_barrier((first.reshape(states * LANES, depth), amplitudes))
    got = [lax.ppermute(first, both, over)]
    own = later.transpose(0, 2, 1)
    partner, own = lax.optimization_barrier((partner, own))
    partner = partner.transpose(0, 2, 1)

    crossed, token = near_send(det, own, partner, False, (first,))
    crossed = lax.ppermute(crossed, "det", [(0, 1), (1, 0)])
    doubled, token = near_send(det, own, partner, True, (token,))
    doubled = lax.ppermute(doubled, both, first_across)
    whole_own, token = lax.optimization_barrier((own, token))
    widths = [LANES] * full + [ops - wide]
    chunk = [whole_own[:, k * LANES : k * LANES + w].reshape(states * w, depth) for k, w in enumerate(widths)]
    later, token = lax.optimization_barrier((jnp.concatenate(chunk[1:full]), token))
    got.append(lax.ppermute(later, both, over))
    last, token = lax.optimization_barrier((chunk[full], token))
    got.append(lax.ppermute(last, both, over))
    keep, token = near_keep(det, own, partner, (token,))
    def terms(k, mine, done, declared=0):
        wire, start = (0, 0) if k == 0 else (2, 0) if k == full else (1, states * LANES * (k - 1))
        return far_terms(det, own, got[wire], start, widths[k], k < full, mine, done, declared)

    kepts, came, tiles, codes, theirs = {}, {}, {}, {}, {}

    def keep_terms(k, *token):
        kepts[k], token = terms(k, True, token)
        return token

    def send_terms(k, *token):
        send, token = terms(k, False, token)
        came[k] = lax.ppermute(send, both, across)
        return token

    def sum_up(k, *token):
        rows = ops if k < full else widths[k]
        declared = LONG if k in early else 0
        tiles[k], codes[k], token = far_sum(det, kepts[k], came[k], rows, k < full, token, declared)
        theirs[k] = lax.ppermute(codes[k], both, back)
        return token

    def cross(ks, token):
        wire, token = crossing_codes(det, [codes[k] for k in ks], (token,))
        return lax.ppermute(wire, both, across), token

    early, late = list(range(full)), [full]
    for k in early:
        token = send_terms(k, token)
        if k == full - 1:
            gate = lax.ppermute(token, "state", [(s, s ^ 1) for s in range(blocks)])
        token = keep_terms(k, token)
        if k == 0:
            share, token = near_share(det, keep, doubled, states, (token, crossed))
            given = lax.ppermute(share, both, to_second)
    token = send_terms(full, token, gate)
    for k in early:
        token = sum_up(k, token)
    turned, token = cross(early, token)
    token = keep_terms(full, token, given)
    token = sum_up(full, token)
    last, token = cross(late, token)
    out, token = near_sum(jnp.stack([x, core]), keep, crossed, share, given, states, (token,))

    at = jnp.stack([x, receiver])
    out, token = into_place(0, at, out, *returned([theirs[k] for k in early], early, widths, ops), (token,), LONG)
    placed = completed([tiles[k] for k in early + late], turned, last, widths, ops)
    out, token = into_place(1, at, out, *placed, (token,), LONG)
    out, token = into_place(0, at, out, *returned([theirs[full]], late, widths, ops), (token,))
    return out.transpose(0, 2, 1, 3)


def partner_2(value, axis, stride):
    mask = 2**stride
    pairs = [(source, source ^ mask) for source in range(lax.axis_size(axis))]
    return lax.ppermute(value, axis, pairs)


def pair_terms(own_block, partner, count):
    operators = own_block.shape[2]
    terms = jnp.einsum("adp,bdq->abpq", own_block, partner, preferred_element_type=jnp.float32)
    return terms.reshape(count, operators, operators)


def exchanged(amplitudes):
    blocks = lax.axis_size("state")
    far_bit = blocks.bit_length() - 2
    states = amplitudes.shape[0]
    gathered = []
    for bit in (far_bit, 0):
        partner = partner_2(amplitudes, "state", bit)
        terms = pair_terms(amplitudes, partner, states * states)
        gathered.append(lax.psum_scatter(terms, "det", scatter_dimension=0, tiled=True))
    return jnp.stack(gathered)


def on_device(amplitudes):
    states, _, ops = amplitudes.shape
    two = lax.axis_size("det") == 2 and lax.axis_size("state") >= 4
    if two and states % 2 == 0 and ops > 2 * LANES and ops % LANES % 8:
        return paired(amplitudes)
    return exchanged(amplitudes)


def solution(mesh):
    return jax.shard_map(
        on_device,
        mesh=mesh,
        in_specs=(P("state", "det", None),),
        out_specs=P(None, ("state", "det"), None, None),
        check_vma=False,
    )
```

```python
import functools

import jax
import jax.numpy as jnp
from jax import lax
from jax.experimental import pallas as pl
from jax.experimental.pallas import tpu as pltpu
from jax.sharding import PartitionSpec as P

LANES = 128
VMEM_LIMIT = 20 * 2**20
POWER, LIFT = 10, 11
SMALLEST = 2.0**-110
LONG = 10**10


def contract_last(left, right):
    return lax.dot_general(left, right, (((1,), (1,)), ((), ())), preferred_element_type=jnp.float32)


def call(body, grid, scalars, in_specs, out_specs, out_shape, after=(), aliases={}, scratch=(), declared=0):
    idle = len(after)

    def waiting(*refs):
        first = scalars + len(in_specs)
        last = first + idle + len(out_specs)
        body(*refs[:first], *refs[first + idle : last], *refs[last + 1 :])
        refs[last][...] = jnp.zeros_like(refs[last])

    token = (8, LANES)
    kernel = pl.pallas_call(
        waiting,
        grid_spec=pltpu.PrefetchScalarGridSpec(
            num_scalar_prefetch=scalars,
            grid=grid,
            in_specs=in_specs + [pl.BlockSpec(memory_space=pl.ANY)] * idle,
            out_specs=[*out_specs, whole(token)],
            scratch_shapes=scratch,
        ),
        out_shape=[*out_shape, f32(*token)],
        input_output_aliases=aliases,
        compiler_params=pltpu.CompilerParams(vmem_limit_bytes=VMEM_LIMIT),
        cost_estimate=pl.CostEstimate(flops=declared, bytes_accessed=declared // 100, transcendentals=0),
    )
    return lambda *operands: kernel(*operands, *after)


def f32(*shape):
    return jax.ShapeDtypeStruct(shape, jnp.float32)


def up(size, unit):
    return -(-size // unit) * unit


def whole(shape):
    return pl.BlockSpec(shape, lambda *_: (0,) * len(shape), pipeline_mode=pl.Buffered(1))


class Packing:
    def __init__(self, tiles, ops):
        self.ops, self.wide = ops, ops // LANES * LANES
        self.rest, self.below = ops - self.wide, up(ops, 8)
        self.each = self.below + up(self.rest, 8)
        beside = self.wide // LANES
        self.corners = [
            (tiles * self.each + t // beside * up(self.rest, 8), t % beside * LANES) for t in range(tiles)
        ]
        self.shape = (tiles * self.each + pl.cdiv(tiles, beside) * up(self.rest, 8), self.wide)

    def store(self, wire_ref, t, main, turned):
        row, lane = self.corners[t]
        wire_ref[t * self.each : t * self.each + self.ops] = main
        start = t * self.each + self.below
        wire_ref[start : start + self.rest] = turned[:, : self.wide]
        wire_ref[row : row + self.rest, lane : lane + self.rest] = turned[:, self.wide :]

    def rows(self, wire_ref, t, start, rows):
        row, lane = self.corners[t]
        under, padded = t * self.each + self.below, up(self.rest, 8)
        if start < self.wide:
            side = wire_ref[under : under + padded, start : start + rows].T[:, : self.rest]
        else:
            side = wire_ref[row : row + padded, lane : lane + LANES].T[:rows, : self.rest]
        return jnp.concatenate([wire_ref[t * self.each + start : t * self.each + start + rows], side], axis=1)

    def parts(self, wire_ref, t):
        row, lane = self.corners[t]
        start, padded = t * self.each + self.below, up(self.rest, 8)
        head, tail = slice(0, self.wide), slice(self.wide, self.ops)
        side = wire_ref[start : start + padded].T[:, : self.rest]
        corner = wire_ref[row : row + padded, lane : lane + LANES].T[: self.rest, : self.rest]
        main = wire_ref[t * self.each : t * self.each + self.ops]
        return [(slice(0, self.ops), head, main), (head, tail, side), (tail, tail, corner)]


def near_send(det, own, partner, to_mine, after=()):
    states, ops, depth = own.shape
    half, tiles = states // 2, (states // 2) ** 2
    packing = Packing(tiles, ops)

    def body(x_ref, own_ref, partner_ref, wire_ref):
        main = contract_last(own_ref[0], partner_ref[0, : packing.wide])
        turned = contract_last(partner_ref[0, packing.wide :], own_ref[0])
        for t in range(tiles):

            @pl.when(pl.program_id(0) == t)
            def _():
                packing.store(wire_ref, t, main, turned)

    def second(x):
        return half * (1 - x[0]) if to_mine else half * x[0]

    return call(
        body,
        (tiles,),
        1,
        [
            pl.BlockSpec((1, ops, depth), lambda t, x: (half * (1 - x[0]) + t // half, 0, 0)),
            pl.BlockSpec((1, ops, depth), lambda t, x: (second(x) + t % half, 0, 0)),
        ],
        [whole(packing.shape)],
        [f32(*packing.shape)],
        after,
    )(det, own, partner)


def near_keep(det, own, partner, after=()):
    states, ops, depth = own.shape
    half = states // 2

    def body(x_ref, own_ref, partner_ref, tile_ref):
        tile_ref[0] = contract_last(own_ref[0], partner_ref[0])

    return call(
        body,
        (half, states),
        1,
        [
            pl.BlockSpec((1, ops, depth), lambda a, b, x: (half * x[0] + a, 0, 0)),
            pl.BlockSpec((1, ops, depth), lambda a, b, x: (b, 0, 0)),
        ],
        [pl.BlockSpec((1, ops, ops), lambda a, b, x: (a * states + b, 0, 0))],
        [f32(half * states, ops, ops)],
        after,
    )(det, own, partner)


def near_share(det, keep, doubled, states, after=()):
    _, ops, _ = keep.shape
    half, tiles = states // 2, (states // 2) ** 2
    packing = Packing(tiles, ops)
    shape = (tiles, up(ops, 8), up(ops, LANES))

    def body(x_ref, keep_ref, wire_ref, tile_ref):
        for t in range(tiles):
            kept = t // half * states + half * x_ref[0] + t % half
            for rows, columns, values in packing.parts(wire_ref, t):
                tile_ref[t, rows, columns] = keep_ref[kept, rows, columns] + values

    return call(
        body, (1,), 1, [whole(keep.shape), whole(packing.shape)], [whole(shape)], [f32(*shape)], after
    )(det, keep, doubled)


def near_sum(place_in, keep, crossed, share, given, states, after=()):
    tiles, ops, _ = keep.shape
    half = states // 2
    packing = Packing(half * half, ops)
    blocks = [(p, min(LANES, ops - p)) for p in range(0, ops, LANES)]

    def body(s_ref, keep_ref, wire_in, share_ref, given_ref, out_ref, kept, wire, mine, *rest):
        made, sems = rest[:-1], rest[-1]
        x, core = s_ref[0], s_ref[1]
        loads = [pltpu.make_async_copy(wire_in, wire, sems.at[0])]
        for a in range(half):
            other = keep_ref.at[pl.ds(a * states + half * (1 - x), half)]
            loads.append(pltpu.make_async_copy(other, kept.at[pl.ds(a * half, half)], sems.at[1 + a]))
        for load in loads:
            load.start()
        for source, which in ((share_ref, 0), (given_ref, 1)):

            @pl.when(core == which)
            def _():
                load = pltpu.make_async_copy(source, mine, sems.at[1 + half])
                load.start()
                load.wait()

        for load in loads:
            load.wait()
        stores = []
        for n, (start, rows) in enumerate(blocks):
            ref = made[n]
            for a in range(half):
                for b in range(states):
                    t, one, turned = a * states + b, a * half + b % half, b % half * half + a

                    @pl.when(b // half != x)
                    def _():
                        ref[:, t] = kept[one, start : start + rows] + packing.rows(wire, one, start, rows)

                    @pl.when((b // half == x) & (core == 0))
                    def _():
                        ref[:, t] = mine[one, start : start + rows, :ops]

                    @pl.when((b // half == x) & (core == 1))
                    def _():
                        ref[:, t] = mine[turned, :, start : start + LANES].T[:rows, :ops]

            target = out_ref.at[1, pl.ds(start, rows)]
            stores.append(pltpu.make_async_copy(ref, target, sems.at[2 + half + n]))
            stores[n].start()
        for store in stores:
            store.wait()

    return call(
        body,
        (1,),
        1,
        [pl.BlockSpec(memory_space=pl.ANY)] * 4,
        [pl.BlockSpec(memory_space=pl.ANY)],
        [f32(2, ops, tiles, ops)],
        after,
        scratch=[
            pltpu.VMEM((half * half, ops, ops), jnp.float32),
            pltpu.VMEM(packing.shape, jnp.float32),
            pltpu.VMEM(share.shape, jnp.float32),
            *[pltpu.VMEM((rows, tiles, ops), jnp.float32) for _, rows in blocks],
            pltpu.SemaphoreType.DMA((2 + half + len(blocks),)),
        ],
    )(place_in, keep, crossed, share, given)


def far_terms(det, own, got, start, width, turned, mine, after=(), declared=0):
    states, ops, depth = own.shape
    half = states // 2
    rows = ops if turned else width
    tile = (up(ops, 8), width) if turned else (up(width, 8), ops)

    def first(x):
        return half * x if mine else half * (1 - x)

    def body(x_ref, own_ref, got_ref, out_ref):
        if turned:
            both = contract_last(own_ref[0], got_ref[...])
            parts = [both[:, a * width : (a + 1) * width] for a in range(half)]
        else:
            every = contract_last(got_ref[...], own_ref[0])
            parts = [every[u * width : (u + 1) * width] for u in range(states)]
            parts = [jnp.where(first(x_ref[0]) == 0, parts[a], parts[half + a]) for a in range(half)]
        for a in range(half):
            out_ref[a, 0, :rows] = parts[a]

    picked = half if turned else states

    def rows_in(v, x):
        return (start + first(x[0]) * width if turned else start, 0)

    return call(
        body,
        (states,),
        1,
        [
            pl.BlockSpec((1, ops, depth), lambda v, x: (v, 0, 0)),
            pl.BlockSpec(
                (pl.Element(picked * width), pl.Element(depth)), rows_in, pipeline_mode=pl.Buffered(1)
            ),
        ],
        [pl.BlockSpec((half, 1, *tile), lambda v, x: (0, v, 0, 0))],
        [f32(half, states, *tile)],
        after,
        declared=declared,
    )(det, own, got)


def far_sum(det, keep, came, rows, turned, after=(), declared=0):
    half, states, _, lanes = keep.shape
    shape = (up(rows + 1, 8), lanes)

    def body(x_ref, keep_ref, came_ref, tile_ref, code_ref):
        x = x_ref[0]
        top = jnp.zeros((rows, lanes), jnp.float32)
        for a in range(half):
            for v in range(states):
                top = jnp.maximum(top, jnp.abs(keep_ref[a, v, :rows] + came_ref[a, v, :rows]))
        exponent = jnp.floor(jnp.log2(jnp.maximum(jnp.max(top, keepdims=True), SMALLEST)))
        scale = jnp.exp2(LIFT - exponent)
        below = jnp.broadcast_to(exponent, (shape[0] - rows, lanes))
        for a in range(half):
            for v in range(states):
                tile = keep_ref[a, v, :rows] + came_ref[a, v, :rows]
                code_ref[a, v] = jnp.concatenate([powered(tile * scale), below]).astype(jnp.bfloat16)
            for b in range(half):
                v = half * x + b
                tile_ref[a, b] = keep_ref[a, v, :rows] + came_ref[a, v, :rows]

    shapes = [(half, half, rows, lanes), (half, states, *shape)]
    kinds = [jnp.float32, jnp.bfloat16]
    return call(
        body,
        (1,),
        1,
        [whole(keep.shape)] * 2,
        [whole(s) for s in shapes],
        [jax.ShapeDtypeStruct(s, kind) for s, kind in zip(shapes, kinds)],
        after,
        declared=declared,
    )(det, keep, came)


def crossing_codes(det, codes, after=()):
    half, states, *tile = codes[0].shape
    shape = (len(codes), half, half, *tile)

    def body(x_ref, *refs):
        for k in range(len(codes)):
            refs[-1][k] = refs[k][...]

    return call(
        body,
        (1,),
        1,
        [pl.BlockSpec((half, half, *tile), lambda i, x: (0, 1 - x[0], 0, 0))] * len(codes),
        [whole(shape)],
        [jax.ShapeDtypeStruct(shape, jnp.bfloat16)],
        after,
    )(det, *codes)


def powered(value):
    square = value * value
    fourth = square * square
    return value * jnp.abs(value) * (fourth * fourth)


def rooted(code, exponent):
    code, exponent = code.astype(jnp.float32), exponent.astype(jnp.float32)
    root = jnp.exp2(jnp.log2(jnp.abs(code)) * (1 / POWER)) * jnp.exp2(exponent - LIFT)
    return jnp.where(code < 0, -root, root)


def decoded(code, rows):
    return rooted(code[:rows], code[rows : rows + 1])


def into_place(role, place_in, out, sources, pieces, after=(), declared=0):
    _, ops, tiles, _ = out.shape
    count = len(sources)

    def body(s_ref, out_in, *refs):
        out_ref, held, made, sems = refs[count], refs[count + 1 : 2 * count + 1], refs[2 * count + 1 : -1], refs[-1]

        @pl.when(s_ref[1] == role)
        def _():
            loads = [pltpu.make_async_copy(refs[k], held[k], sems.at[k]) for k in range(count)]
            for load in loads:
                load.start()
            for load in loads:
                load.wait()
            stores = []
            for k, (start, rows, fill) in enumerate(pieces):
                fill(s_ref[0], held, made[k])
                target = out_ref.at[0, pl.ds(start, rows)]
                stores.append(pltpu.make_async_copy(made[k], target, sems.at[count + k]))
                stores[k].start()
            for store in stores:
                store.wait()

    return call(
        body,
        (1,),
        1,
        [pl.BlockSpec(memory_space=pl.ANY)] * (1 + count),
        [pl.BlockSpec(memory_space=pl.ANY)],
        [f32(*out.shape)],
        after,
        {1: 0},
        [pltpu.VMEM(v.shape, v.dtype) for v in sources]
        + [pltpu.VMEM((rows, tiles, ops), jnp.float32) for _, rows, _ in pieces]
        + [pltpu.SemaphoreType.DMA((count + len(pieces),))],
        declared,
    )(place_in, out, *sources)


def returned(codes, chunks, widths, ops):
    def piece(n, k):
        half, states, _, _ = codes[n].shape

        def fill(x, refs, ref):
            for a in range(half):
                for v in range(states):
                    one = refs[n][a, v]
                    last = widths[k] < LANES
                    ref[:, a * states + v] = decoded(one, widths[k]) if last else decoded(one, ops).T

        return k * LANES, widths[k], fill

    return codes, [piece(n, k) for n, k in enumerate(chunks)]


def completed(tiles, turned, last, widths, ops):
    full = len(widths) - 1
    half, _, rest, _ = tiles[full].shape

    def piece(start, rows):
        def fill(x, refs, ref):
            for b in range(half):
                for u in range(2 * half):
                    a, t = u % half, 2 * half * b + u

                    @pl.when(u // half == x)
                    def _():
                        for k in range(full):
                            ref[:, t, k * LANES : (k + 1) * LANES] = refs[k][a, b, start : start + rows]
                        block = refs[full][a, b, :, start : start + rows]
                        ref[:, t, full * LANES :] = block.T

                    @pl.when(u // half != x)
                    def _():
                        for k in range(full):
                            code = refs[full + 1][k, a, b]
                            value = rooted(code[start : start + rows], code[ops : ops + 1])
                            ref[:, t, k * LANES : (k + 1) * LANES] = value
                        code = refs[full + 2][0, a, b, :, start : start + rows]
                        ref[:, t, full * LANES :] = decoded(code, rest).T

        return start, rows, fill

    return [*tiles, turned, last], [piece(p, min(LANES, ops - p)) for p in range(0, ops, LANES)]


def paired(amplitudes):
    blocks = lax.axis_size("state")
    far = blocks.bit_length() - 2
    states, depth, ops = amplitudes.shape
    full = ops // LANES
    wide = full * LANES
    both = ("state", "det")
    senders = [s for s in range(blocks) if (s & 1) == (s >> far & 1)]
    receivers = [s for s in range(blocks) if s not in senders]
    over = [(2 * s + x, 2 * (s ^ 1 << far) + x) for s in senders for x in range(2)]
    back = [(b, a) for a, b in over]
    across = [(2 * s + x, 2 * s + 1 - x) for s in receivers for x in range(2)]
    first_across = [(2 * s + x, 2 * s + 1 - x) for s in range(0, blocks, 2) for x in range(2)]
    to_second = [(2 * s + x, 2 * (s + 1) + x) for s in range(0, blocks, 2) for x in range(2)]

    state = lax.axis_index("state")
    x = lax.axis_index("det").astype(jnp.int32)
    det = x[None]
    receiver = ((state & 1) ^ (state >> far & 1)).astype(jnp.int32)
    core = (state & 1).astype(jnp.int32)

    partner = lax.ppermute(amplitudes, "state", [(s, s ^ 1) for s in range(blocks)])
    first = amplitudes[:, :, :LANES].transpose(0, 2, 1)
    first, later = lax.optimization_barrier((first.reshape(states * LANES, depth), amplitudes))
    got = [lax.ppermute(first, both, over)]
    own = later.transpose(0, 2, 1)
    partner, own = lax.optimization_barrier((partner, own))
    partner = partner.transpose(0, 2, 1)

    crossed, token = near_send(det, own, partner, False, (first,))
    crossed = lax.ppermute(crossed, "det", [(0, 1), (1, 0)])
    doubled, token = near_send(det, own, partner, True, (token,))
    doubled = lax.ppermute(doubled, both, first_across)
    whole_own, token = lax.optimization_barrier((own, token))
    widths = [LANES] * full + [ops - wide]
    chunk = [whole_own[:, k * LANES : k * LANES + w].reshape(states * w, depth) for k, w in enumerate(widths)]
    later, token = lax.optimization_barrier((jnp.concatenate(chunk[1:full]), token))
    got.append(lax.ppermute(later, both, over))
    last, token = lax.optimization_barrier((chunk[full], token))
    got.append(lax.ppermute(last, both, over))
    keep, token = near_keep(det, own, partner, (token,))
    def terms(k, mine, done, declared=0):
        wire, start = (0, 0) if k == 0 else (2, 0) if k == full else (1, states * LANES * (k - 1))
        return far_terms(det, own, got[wire], start, widths[k], k < full, mine, done, declared)

    kepts, came, tiles, codes, theirs = {}, {}, {}, {}, {}

    def keep_terms(k, *token):
        kepts[k], token = terms(k, True, token, LONG if k == full - 1 else 0)
        return token

    def send_terms(k, *token):
        send, token = terms(k, False, token)
        came[k] = lax.ppermute(send, both, across)
        return token

    def sum_up(k, *token):
        rows = ops if k < full else widths[k]
        declared = LONG if k in early else 0
        tiles[k], codes[k], token = far_sum(det, kepts[k], came[k], rows, k < full, token, declared)
        theirs[k] = lax.ppermute(codes[k], both, back)
        return token

    def cross(ks, token):
        wire, token = crossing_codes(det, [codes[k] for k in ks], (token,))
        return lax.ppermute(wire, both, across), token

    early, late = list(range(full)), [full]
    for k in early:
        token = send_terms(k, token)
        if k == full - 1:
            gate = lax.ppermute(token, "state", [(s, s ^ 1) for s in range(blocks)])
            share, token = near_share(det, keep, doubled, states, (token, crossed))
            given = lax.ppermute(share, both, to_second)
        token = keep_terms(k, token)
    token = send_terms(full, token, gate)
    for k in early:
        token = sum_up(k, token)
    token = keep_terms(full, token, given)
    token = sum_up(full, token)
    turned, token = cross(early, token)
    last, token = cross(late, token)
    out, token = near_sum(jnp.stack([x, core]), keep, crossed, share, given, states, (token,))

    at = jnp.stack([x, receiver])
    for k in early:
        out, token = into_place(0, at, out, *returned([theirs[k]], [k], widths, ops), (token,), LONG)
    placed = completed([tiles[k] for k in early + late], turned, last, widths, ops)
    out, token = into_place(1, at, out, *placed, (token,), LONG)
    out, token = into_place(0, at, out, *returned([theirs[full]], late, widths, ops), (token,))
    return out.transpose(0, 2, 1, 3)


def partner_2(value, axis, stride):
    mask = 2**stride
    pairs = [(source, source ^ mask) for source in range(lax.axis_size(axis))]
    return lax.ppermute(value, axis, pairs)


def pair_terms(own_block, partner, count):
    operators = own_block.shape[2]
    terms = jnp.einsum("adp,bdq->abpq", own_block, partner, preferred_element_type=jnp.float32)
    return terms.reshape(count, operators, operators)


def exchanged(amplitudes):
    blocks = lax.axis_size("state")
    far_bit = blocks.bit_length() - 2
    states = amplitudes.shape[0]
    gathered = []
    for bit in (far_bit, 0):
        partner = partner_2(amplitudes, "state", bit)
        terms = pair_terms(amplitudes, partner, states * states)
        gathered.append(lax.psum_scatter(terms, "det", scatter_dimension=0, tiled=True))
    return jnp.stack(gathered)


def on_device(amplitudes):
    states, _, ops = amplitudes.shape
    two = lax.axis_size("det") == 2 and lax.axis_size("state") >= 4
    if two and states % 2 == 0 and ops > 2 * LANES and ops % LANES % 8:
        return paired(amplitudes)
    return exchanged(amplitudes)


def solution(mesh):
    return jax.shard_map(
        on_device,
        mesh=mesh,
        in_specs=(P("state", "det", None),),
        out_specs=P(None, ("state", "det"), None, None),
        check_vma=False,
    )
```

```python
import functools

import jax
import jax.numpy as jnp
from jax import lax
from jax.experimental import pallas as pl
from jax.experimental.pallas import tpu as pltpu
from jax.sharding import PartitionSpec as P

LANES = 128
VMEM_LIMIT = 20 * 2**20
POWER, LIFT = 10, 11
SMALLEST = 2.0**-110
LONG = 10**10


def contract_last(left, right):
    return lax.dot_general(left, right, (((1,), (1,)), ((), ())), preferred_element_type=jnp.float32)


def call(body, grid, scalars, in_specs, out_specs, out_shape, after=(), aliases={}, scratch=(), declared=0):
    idle = len(after)

    def waiting(*refs):
        first = scalars + len(in_specs)
        last = first + idle + len(out_specs)
        body(*refs[:first], *refs[first + idle : last], *refs[last + 1 :])
        refs[last][...] = jnp.zeros_like(refs[last])

    token = (8, LANES)
    kernel = pl.pallas_call(
        waiting,
        grid_spec=pltpu.PrefetchScalarGridSpec(
            num_scalar_prefetch=scalars,
            grid=grid,
            in_specs=in_specs + [pl.BlockSpec(memory_space=pl.ANY)] * idle,
            out_specs=[*out_specs, whole(token)],
            scratch_shapes=scratch,
        ),
        out_shape=[*out_shape, f32(*token)],
        input_output_aliases=aliases,
        compiler_params=pltpu.CompilerParams(vmem_limit_bytes=VMEM_LIMIT),
        cost_estimate=pl.CostEstimate(flops=declared, bytes_accessed=declared // 100, transcendentals=0),
    )
    return lambda *operands: kernel(*operands, *after)


def f32(*shape):
    return jax.ShapeDtypeStruct(shape, jnp.float32)


def up(size, unit):
    return -(-size // unit) * unit


def whole(shape):
    return pl.BlockSpec(shape, lambda *_: (0,) * len(shape), pipeline_mode=pl.Buffered(1))


class Packing:
    def __init__(self, tiles, ops):
        self.ops, self.wide = ops, ops // LANES * LANES
        self.rest, self.below = ops - self.wide, up(ops, 8)
        self.each = self.below + up(self.rest, 8)
        beside = self.wide // LANES
        self.corners = [
            (tiles * self.each + t // beside * up(self.rest, 8), t % beside * LANES) for t in range(tiles)
        ]
        self.shape = (tiles * self.each + pl.cdiv(tiles, beside) * up(self.rest, 8), self.wide)

    def store(self, wire_ref, t, main, turned):
        row, lane = self.corners[t]
        wire_ref[t * self.each : t * self.each + self.ops] = main
        start = t * self.each + self.below
        wire_ref[start : start + self.rest] = turned[:, : self.wide]
        wire_ref[row : row + self.rest, lane : lane + self.rest] = turned[:, self.wide :]

    def rows(self, wire_ref, t, start, rows):
        row, lane = self.corners[t]
        under, padded = t * self.each + self.below, up(self.rest, 8)
        if start < self.wide:
            side = wire_ref[under : under + padded, start : start + rows].T[:, : self.rest]
        else:
            side = wire_ref[row : row + padded, lane : lane + LANES].T[:rows, : self.rest]
        return jnp.concatenate([wire_ref[t * self.each + start : t * self.each + start + rows], side], axis=1)

    def parts(self, wire_ref, t):
        row, lane = self.corners[t]
        start, padded = t * self.each + self.below, up(self.rest, 8)
        head, tail = slice(0, self.wide), slice(self.wide, self.ops)
        side = wire_ref[start : start + padded].T[:, : self.rest]
        corner = wire_ref[row : row + padded, lane : lane + LANES].T[: self.rest, : self.rest]
        main = wire_ref[t * self.each : t * self.each + self.ops]
        return [(slice(0, self.ops), head, main), (head, tail, side), (tail, tail, corner)]


def near_send(det, own, partner, to_mine, after=()):
    states, ops, depth = own.shape
    half, tiles = states // 2, (states // 2) ** 2
    packing = Packing(tiles, ops)

    def body(x_ref, own_ref, partner_ref, wire_ref):
        main = contract_last(own_ref[0], partner_ref[0, : packing.wide])
        turned = contract_last(partner_ref[0, packing.wide :], own_ref[0])
        for t in range(tiles):

            @pl.when(pl.program_id(0) == t)
            def _():
                packing.store(wire_ref, t, main, turned)

    def second(x):
        return half * (1 - x[0]) if to_mine else half * x[0]

    return call(
        body,
        (tiles,),
        1,
        [
            pl.BlockSpec((1, ops, depth), lambda t, x: (half * (1 - x[0]) + t // half, 0, 0)),
            pl.BlockSpec((1, ops, depth), lambda t, x: (second(x) + t % half, 0, 0)),
        ],
        [whole(packing.shape)],
        [f32(*packing.shape)],
        after,
    )(det, own, partner)


def near_keep(det, own, partner, after=()):
    states, ops, depth = own.shape
    half = states // 2

    def body(x_ref, own_ref, partner_ref, tile_ref):
        tile_ref[0] = contract_last(own_ref[0], partner_ref[0])

    return call(
        body,
        (half, states),
        1,
        [
            pl.BlockSpec((1, ops, depth), lambda a, b, x: (half * x[0] + a, 0, 0)),
            pl.BlockSpec((1, ops, depth), lambda a, b, x: (b, 0, 0)),
        ],
        [pl.BlockSpec((1, ops, ops), lambda a, b, x: (a * states + b, 0, 0))],
        [f32(half * states, ops, ops)],
        after,
    )(det, own, partner)


def near_share(det, keep, doubled, states, after=()):
    _, ops, _ = keep.shape
    half, tiles = states // 2, (states // 2) ** 2
    packing = Packing(tiles, ops)
    shape = (tiles, up(ops, 8), up(ops, LANES))

    def body(x_ref, keep_ref, wire_ref, tile_ref):
        for t in range(tiles):
            kept = t // half * states + half * x_ref[0] + t % half
            for rows, columns, values in packing.parts(wire_ref, t):
                tile_ref[t, rows, columns] = keep_ref[kept, rows, columns] + values

    return call(
        body, (1,), 1, [whole(keep.shape), whole(packing.shape)], [whole(shape)], [f32(*shape)], after
    )(det, keep, doubled)


def near_sum(place_in, keep, crossed, share, given, states, after=()):
    tiles, ops, _ = keep.shape
    half = states // 2
    packing = Packing(half * half, ops)
    blocks = [(p, min(LANES, ops - p)) for p in range(0, ops, LANES)]

    def body(s_ref, keep_ref, wire_in, share_ref, given_ref, out_ref, kept, wire, mine, *rest):
        made, sems = rest[:-1], rest[-1]
        x, second = s_ref[0], s_ref[1]
        loads = [pltpu.make_async_copy(wire_in, wire, sems.at[0])]
        for a in range(half):
            other = keep_ref.at[pl.ds(a * states + half * (1 - x), half)]
            loads.append(pltpu.make_async_copy(other, kept.at[pl.ds(a * half, half)], sems.at[1 + a]))
        for load in loads:
            load.start()
        for source, which in ((share_ref, 0), (given_ref, 1)):

            @pl.when(second == which)
            def _():
                load = pltpu.make_async_copy(source, mine, sems.at[1 + half])
                load.start()
                load.wait()

        for load in loads:
            load.wait()
        stores = []
        for n, (start, rows) in enumerate(blocks):
            ref = made[n]
            for a in range(half):
                for b in range(states):
                    t, one, turned = a * states + b, a * half + b % half, b % half * half + a

                    @pl.when(b // half != x)
                    def _():
                        ref[:, t] = kept[one, start : start + rows] + packing.rows(wire, one, start, rows)

                    @pl.when((b // half == x) & (second == 0))
                    def _():
                        ref[:, t] = mine[one, start : start + rows, :ops]

                    @pl.when((b // half == x) & (second == 1))
                    def _():
                        ref[:, t] = mine[turned, :, start : start + LANES].T[:rows, :ops]

            target = out_ref.at[1, pl.ds(start, rows)]
            stores.append(pltpu.make_async_copy(ref, target, sems.at[2 + half + n]))
            stores[n].start()
        for store in stores:
            store.wait()

    return call(
        body,
        (1,),
        1,
        [pl.BlockSpec(memory_space=pl.ANY)] * 4,
        [pl.BlockSpec(memory_space=pl.ANY)],
        [f32(2, ops, tiles, ops)],
        after,
        scratch=[
            pltpu.VMEM((half * half, ops, ops), jnp.float32),
            pltpu.VMEM(packing.shape, jnp.float32),
            pltpu.VMEM(share.shape, jnp.float32),
            *[pltpu.VMEM((rows, tiles, ops), jnp.float32) for _, rows in blocks],
            pltpu.SemaphoreType.DMA((2 + half + len(blocks),)),
        ],
    )(place_in, keep, crossed, share, given)


def far_terms(place_in, own, got, start, width, turned, mine, after=(), declared=0):
    states, ops, depth = own.shape
    half = states // 2
    rows = ops if turned else width
    tile = (up(ops, 8), width) if turned else (up(width, 8), ops)

    def first(x):
        return half * x if mine else half * (1 - x)

    def body(s_ref, own_ref, got_ref, out_ref):
        @pl.when(s_ref[1] == 1)
        def _():
            if turned:
                both = contract_last(own_ref[0], got_ref[...])
                parts = [both[:, a * width : (a + 1) * width] for a in range(half)]
            else:
                every = contract_last(got_ref[...], own_ref[0])
                parts = [every[u * width : (u + 1) * width] for u in range(states)]
                parts = [jnp.where(first(s_ref[0]) == 0, parts[a], parts[half + a]) for a in range(half)]
            for a in range(half):
                out_ref[a, 0, :rows] = parts[a]

    picked = half if turned else states

    def rows_in(v, x):
        return (start + first(x[0]) * width if turned else start, 0)

    return call(
        body,
        (states,),
        1,
        [
            pl.BlockSpec((1, ops, depth), lambda v, s: (v * s[1], 0, 0)),
            pl.BlockSpec(
                (pl.Element(picked * width), pl.Element(depth)), rows_in, pipeline_mode=pl.Buffered(1)
            ),
        ],
        [pl.BlockSpec((half, 1, *tile), lambda v, s: (0, v * s[1], 0, 0))],
        [f32(half, states, *tile)],
        after,
        declared=declared,
    )(place_in, own, got)


def far_sum(det, keep, came, rows, turned, after=(), declared=0):
    half, states, _, lanes = keep.shape
    shape = (up(rows + 1, 8), lanes)

    def body(x_ref, keep_ref, came_ref, tile_ref, code_ref):
        x = x_ref[0]
        top = jnp.zeros((rows, lanes), jnp.float32)
        for a in range(half):
            for v in range(states):
                top = jnp.maximum(top, jnp.abs(keep_ref[a, v, :rows] + came_ref[a, v, :rows]))
        exponent = jnp.floor(jnp.log2(jnp.maximum(jnp.max(top, keepdims=True), SMALLEST)))
        scale = jnp.exp2(LIFT - exponent)
        below = jnp.broadcast_to(exponent, (shape[0] - rows, lanes))
        for a in range(half):
            for v in range(states):
                tile = keep_ref[a, v, :rows] + came_ref[a, v, :rows]
                code_ref[a, v] = jnp.concatenate([powered(tile * scale), below]).astype(jnp.bfloat16)
            for b in range(half):
                v = half * x + b
                tile_ref[a, b] = keep_ref[a, v, :rows] + came_ref[a, v, :rows]

    shapes = [(half, half, rows, lanes), (half, states, *shape)]
    kinds = [jnp.float32, jnp.bfloat16]
    return call(
        body,
        (1,),
        1,
        [whole(keep.shape)] * 2,
        [whole(s) for s in shapes],
        [jax.ShapeDtypeStruct(s, kind) for s, kind in zip(shapes, kinds)],
        after,
        declared=declared,
    )(det, keep, came)


def crossing_codes(det, codes, after=()):
    half, states, *tile = codes[0].shape
    shape = (len(codes), half, half, *tile)

    def body(x_ref, *refs):
        for k in range(len(codes)):
            refs[-1][k] = refs[k][...]

    return call(
        body,
        (1,),
        1,
        [pl.BlockSpec((half, half, *tile), lambda i, x: (0, 1 - x[0], 0, 0))] * len(codes),
        [whole(shape)],
        [jax.ShapeDtypeStruct(shape, jnp.bfloat16)],
        after,
    )(det, *codes)


def powered(value):
    square = value * value
    fourth = square * square
    return value * jnp.abs(value) * (fourth * fourth)


def rooted(code, exponent):
    code, exponent = code.astype(jnp.float32), exponent.astype(jnp.float32)
    root = jnp.exp2(jnp.log2(jnp.abs(code)) * (1 / POWER)) * jnp.exp2(exponent - LIFT)
    return jnp.where(code < 0, -root, root)


def decoded(code, rows):
    return rooted(code[:rows], code[rows : rows + 1])


def into_place(role, place_in, out, sources, pieces, after=(), declared=0):
    _, ops, tiles, _ = out.shape
    count = len(sources)

    def body(s_ref, out_in, *refs):
        out_ref, held, made, sems = refs[count], refs[count + 1 : 2 * count + 1], refs[2 * count + 1 : -1], refs[-1]

        @pl.when(s_ref[1] == role)
        def _():
            loads = [pltpu.make_async_copy(refs[k], held[k], sems.at[k]) for k in range(count)]
            for load in loads:
                load.start()
            for load in loads:
                load.wait()
            stores = []
            for k, (start, rows, fill) in enumerate(pieces):
                fill(s_ref[0], held, made[k])
                target = out_ref.at[0, pl.ds(start, rows)]
                stores.append(pltpu.make_async_copy(made[k], target, sems.at[count + k]))
                stores[k].start()
            for store in stores:
                store.wait()

    return call(
        body,
        (1,),
        1,
        [pl.BlockSpec(memory_space=pl.ANY)] * (1 + count),
        [pl.BlockSpec(memory_space=pl.ANY)],
        [f32(*out.shape)],
        after,
        {1: 0},
        [pltpu.VMEM(v.shape, v.dtype) for v in sources]
        + [pltpu.VMEM((rows, tiles, ops), jnp.float32) for _, rows, _ in pieces]
        + [pltpu.SemaphoreType.DMA((count + len(pieces),))],
        declared,
    )(place_in, out, *sources)


def returned(codes, chunks, widths, ops):
    def piece(n, k):
        half, states, _, _ = codes[n].shape

        def fill(x, refs, ref):
            for a in range(half):
                for v in range(states):
                    one = refs[n][a, v]
                    last = widths[k] < LANES
                    ref[:, a * states + v] = decoded(one, widths[k]) if last else decoded(one, ops).T

        return k * LANES, widths[k], fill

    return codes, [piece(n, k) for n, k in enumerate(chunks)]


def completed(tiles, turned, last, widths, ops):
    full = len(widths) - 1
    half, _, rest, _ = tiles[full].shape

    def piece(start, rows):
        def fill(x, refs, ref):
            for b in range(half):
                for u in range(2 * half):
                    a, t = u % half, 2 * half * b + u

                    @pl.when(u // half == x)
                    def _():
                        for k in range(full):
                            ref[:, t, k * LANES : (k + 1) * LANES] = refs[k][a, b, start : start + rows]
                        block = refs[full][a, b, :, start : start + rows]
                        ref[:, t, full * LANES :] = block.T

                    @pl.when(u // half != x)
                    def _():
                        for k in range(full):
                            code = refs[full + 1][k, a, b]
                            value = rooted(code[start : start + rows], code[ops : ops + 1])
                            ref[:, t, k * LANES : (k + 1) * LANES] = value
                        code = refs[full + 2][0, a, b, :, start : start + rows]
                        ref[:, t, full * LANES :] = decoded(code, rest).T

        return start, rows, fill

    return [*tiles, turned, last], [piece(p, min(LANES, ops - p)) for p in range(0, ops, LANES)]


def paired(amplitudes):
    blocks = lax.axis_size("state")
    far = blocks.bit_length() - 2
    states, depth, ops = amplitudes.shape
    full = ops // LANES
    wide = full * LANES
    both = ("state", "det")
    senders = [s for s in range(blocks) if (s & 1) == (s >> far & 1)]
    receivers = [s for s in range(blocks) if s not in senders]
    over = [(2 * s + x, 2 * (s ^ 1 << far) + x) for s in senders for x in range(2)]
    back = [(b, a) for a, b in over]
    across = [(2 * s + x, 2 * s + 1 - x) for s in receivers for x in range(2)]
    first_across = [(2 * s + x, 2 * s + 1 - x) for s in senders for x in range(2)]
    to_second = [(2 * s + x, 2 * (s ^ 1) + x) for s in senders for x in range(2)]
    opens = [(s, s ^ 1) for s in senders if (s >> far ^ s >> far - 1) & 1]

    state = lax.axis_index("state")
    x = lax.axis_index("det").astype(jnp.int32)
    det = x[None]
    receiver = ((state & 1) ^ (state >> far & 1)).astype(jnp.int32)
    at = jnp.stack([x, receiver])

    partner = lax.ppermute(amplitudes, "state", [(s, s ^ 1) for s in range(blocks)])
    first = amplitudes[:, :, :LANES].transpose(0, 2, 1)
    first, later = lax.optimization_barrier((first.reshape(states * LANES, depth), amplitudes))
    got = [lax.ppermute(first, both, over)]
    own = later.transpose(0, 2, 1)
    partner, own = lax.optimization_barrier((partner, own))
    partner = partner.transpose(0, 2, 1)

    crossed, token = near_send(det, own, partner, False, (first,))
    crossed = lax.ppermute(crossed, "det", [(0, 1), (1, 0)])
    doubled, token = near_send(det, own, partner, True, (token,))
    doubled = lax.ppermute(doubled, both, first_across)
    whole_own, token = lax.optimization_barrier((own, token))
    widths = [LANES] * full + [ops - wide]
    chunk = [whole_own[:, k * LANES : k * LANES + w].reshape(states * w, depth) for k, w in enumerate(widths)]
    later, token = lax.optimization_barrier((jnp.concatenate(chunk[1:full]), token))
    got.append(lax.ppermute(later, both, over))
    last, token = lax.optimization_barrier((chunk[full], token))
    got.append(lax.ppermute(last, both, over))
    keep, token = near_keep(det, own, partner, (token,))
    def terms(k, mine, done, declared=0):
        wire, start = (0, 0) if k == 0 else (2, 0) if k == full else (1, states * LANES * (k - 1))
        return far_terms(at, own, got[wire], start, widths[k], k < full, mine, done, declared)

    kepts, came, tiles, codes, theirs = {}, {}, {}, {}, {}

    def keep_terms(k, *token):
        kepts[k], token = terms(k, True, token, LONG if k == full - 1 else 0)
        return token

    def send_terms(k, *token):
        send, token = terms(k, False, token)
        came[k] = lax.ppermute(send, both, across)
        return token

    def sum_up(k, *token):
        rows = ops if k < full else widths[k]
        declared = LONG if k in early else 0
        tiles[k], codes[k], token = far_sum(det, kepts[k], came[k], rows, k < full, token, declared)
        theirs[k] = lax.ppermute(codes[k], both, back)
        return token

    def cross(ks, token):
        wire, token = crossing_codes(det, [codes[k] for k in ks], (token,))
        return lax.ppermute(wire, both, across), token

    early, late = list(range(full)), [full]
    for k in early:
        token = send_terms(k, token)
        if k == full - 1:
            gate = lax.ppermute(token, "state", opens)
            share, token = near_share(det, keep, doubled, states, (token, crossed))
            given = lax.ppermute(share, both, to_second)
        token = keep_terms(k, token)
    token = send_terms(full, token)
    for k in early:
        token = sum_up(k, token, *([gate] if k == 0 else []))
    token = keep_terms(full, token, given)
    token = sum_up(full, token)
    turned, token = cross(early, token)
    last, token = cross(late, token)
    out, token = near_sum(at, keep, crossed, share, given, states, (token,))

    for k in early:
        out, token = into_place(0, at, out, *returned([theirs[k]], [k], widths, ops), (token,), LONG)
    placed = completed([tiles[k] for k in early + late], turned, last, widths, ops)
    out, token = into_place(1, at, out, *placed, (token,), LONG)
    out, token = into_place(0, at, out, *returned([theirs[full]], late, widths, ops), (token,))
    return out.transpose(0, 2, 1, 3)


def partner_2(value, axis, stride):
    mask = 2**stride
    pairs = [(source, source ^ mask) for source in range(lax.axis_size(axis))]
    return lax.ppermute(value, axis, pairs)


def pair_terms(own_block, partner, count):
    operators = own_block.shape[2]
    terms = jnp.einsum("adp,bdq->abpq", own_block, partner, preferred_element_type=jnp.float32)
    return terms.reshape(count, operators, operators)


def exchanged(amplitudes):
    blocks = lax.axis_size("state")
    far_bit = blocks.bit_length() - 2
    states = amplitudes.shape[0]
    gathered = []
    for bit in (far_bit, 0):
        partner = partner_2(amplitudes, "state", bit)
        terms = pair_terms(amplitudes, partner, states * states)
        gathered.append(lax.psum_scatter(terms, "det", scatter_dimension=0, tiled=True))
    return jnp.stack(gathered)


def on_device(amplitudes):
    states, _, ops = amplitudes.shape
    two = lax.axis_size("det") == 2 and lax.axis_size("state") >= 4
    if two and states % 2 == 0 and ops > 2 * LANES and ops % LANES % 8:
        return paired(amplitudes)
    return exchanged(amplitudes)


def solution(mesh):
    return jax.shard_map(
        on_device,
        mesh=mesh,
        in_specs=(P("state", "det", None),),
        out_specs=P(None, ("state", "det"), None, None),
        check_vma=False,
    )
```

```python
import functools

import jax
import jax.numpy as jnp
from jax import lax
from jax.experimental import pallas as pl
from jax.experimental.pallas import tpu as pltpu
from jax.sharding import PartitionSpec as P

LANES = 128
VMEM_LIMIT = 20 * 2**20
POWER, LIFT = 10, 11
SMALLEST = 2.0**-110
LONG = 10**10


def contract_last(left, right):
    return lax.dot_general(left, right, (((1,), (1,)), ((), ())), preferred_element_type=jnp.float32)


def call(body, grid, scalars, in_specs, out_specs, out_shape, after=(), aliases={}, scratch=(), declared=0):
    idle = len(after)

    def waiting(*refs):
        first = scalars + len(in_specs)
        last = first + idle + len(out_specs)
        body(*refs[:first], *refs[first + idle : last], *refs[last + 1 :])
        refs[last][...] = jnp.zeros_like(refs[last])

    token = (8, LANES)
    kernel = pl.pallas_call(
        waiting,
        grid_spec=pltpu.PrefetchScalarGridSpec(
            num_scalar_prefetch=scalars,
            grid=grid,
            in_specs=in_specs + [pl.BlockSpec(memory_space=pl.ANY)] * idle,
            out_specs=[*out_specs, whole(token)],
            scratch_shapes=scratch,
        ),
        out_shape=[*out_shape, f32(*token)],
        input_output_aliases=aliases,
        compiler_params=pltpu.CompilerParams(vmem_limit_bytes=VMEM_LIMIT),
        cost_estimate=pl.CostEstimate(flops=declared, bytes_accessed=declared // 100, transcendentals=0),
    )
    return lambda *operands: kernel(*operands, *after)


def f32(*shape):
    return jax.ShapeDtypeStruct(shape, jnp.float32)


def up(size, unit):
    return -(-size // unit) * unit


def whole(shape):
    return pl.BlockSpec(shape, lambda *_: (0,) * len(shape), pipeline_mode=pl.Buffered(1))


class Packing:
    def __init__(self, tiles, ops):
        self.ops, self.wide = ops, ops // LANES * LANES
        self.rest, self.below = ops - self.wide, up(ops, 8)
        self.each = self.below + up(self.rest, 8)
        beside = self.wide // LANES
        self.corners = [
            (tiles * self.each + t // beside * up(self.rest, 8), t % beside * LANES) for t in range(tiles)
        ]
        self.shape = (tiles * self.each + pl.cdiv(tiles, beside) * up(self.rest, 8), self.wide)

    def store(self, wire_ref, t, main, turned):
        row, lane = self.corners[t]
        wire_ref[t * self.each : t * self.each + self.ops] = main
        start = t * self.each + self.below
        wire_ref[start : start + self.rest] = turned[:, : self.wide]
        wire_ref[row : row + self.rest, lane : lane + self.rest] = turned[:, self.wide :]

    def rows(self, wire_ref, t, start, rows):
        row, lane = self.corners[t]
        under, padded = t * self.each + self.below, up(self.rest, 8)
        if start < self.wide:
            side = wire_ref[under : under + padded, start : start + rows].T[:, : self.rest]
        else:
            side = wire_ref[row : row + padded, lane : lane + LANES].T[:rows, : self.rest]
        return jnp.concatenate([wire_ref[t * self.each + start : t * self.each + start + rows], side], axis=1)

    def parts(self, wire_ref, t):
        row, lane = self.corners[t]
        start, padded = t * self.each + self.below, up(self.rest, 8)
        head, tail = slice(0, self.wide), slice(self.wide, self.ops)
        side = wire_ref[start : start + padded].T[:, : self.rest]
        corner = wire_ref[row : row + padded, lane : lane + LANES].T[: self.rest, : self.rest]
        main = wire_ref[t * self.each : t * self.each + self.ops]
        return [(slice(0, self.ops), head, main), (head, tail, side), (tail, tail, corner)]


def near_send(det, own, partner, to_mine, after=()):
    states, ops, depth = own.shape
    half, tiles = states // 2, (states // 2) ** 2
    packing = Packing(tiles, ops)

    def body(x_ref, own_ref, partner_ref, wire_ref):
        main = contract_last(own_ref[0], partner_ref[0, : packing.wide])
        turned = contract_last(partner_ref[0, packing.wide :], own_ref[0])
        for t in range(tiles):

            @pl.when(pl.program_id(0) == t)
            def _():
                packing.store(wire_ref, t, main, turned)

    def second(x):
        return half * (1 - x[0]) if to_mine else half * x[0]

    return call(
        body,
        (tiles,),
        1,
        [
            pl.BlockSpec((1, ops, depth), lambda t, x: (half * (1 - x[0]) + t // half, 0, 0)),
            pl.BlockSpec((1, ops, depth), lambda t, x: (second(x) + t % half, 0, 0)),
        ],
        [whole(packing.shape)],
        [f32(*packing.shape)],
        after,
    )(det, own, partner)


def near_keep(det, own, partner, after=()):
    states, ops, depth = own.shape
    half = states // 2

    def body(x_ref, own_ref, partner_ref, tile_ref):
        tile_ref[0] = contract_last(own_ref[0], partner_ref[0])

    return call(
        body,
        (half, states),
        1,
        [
            pl.BlockSpec((1, ops, depth), lambda a, b, x: (half * x[0] + a, 0, 0)),
            pl.BlockSpec((1, ops, depth), lambda a, b, x: (b, 0, 0)),
        ],
        [pl.BlockSpec((1, ops, ops), lambda a, b, x: (a * states + b, 0, 0))],
        [f32(half * states, ops, ops)],
        after,
    )(det, own, partner)


def near_share(place_in, keep, doubled, states, after=()):
    _, ops, _ = keep.shape
    half, tiles = states // 2, (states // 2) ** 2
    packing = Packing(tiles, ops)
    shape = (tiles, up(ops, 8), up(ops, LANES))

    def body(s_ref, keep_ref, wire_in, out_ref, kept, wire, made, sems):
        @pl.when(s_ref[1] == 0)
        def _():
            loads = [pltpu.make_async_copy(wire_in, wire, sems.at[0])]
            for a in range(half):
                mine = keep_ref.at[pl.ds(a * states + half * s_ref[0], half)]
                loads.append(pltpu.make_async_copy(mine, kept.at[pl.ds(a * half, half)], sems.at[1 + a]))
            for load in loads:
                load.start()
            for load in loads:
                load.wait()
            for t in range(tiles):
                for rows, columns, values in packing.parts(wire, t):
                    made[t, rows, columns] = kept[t, rows, columns] + values
            store = pltpu.make_async_copy(made, out_ref, sems.at[0])
            store.start()
            store.wait()

    return call(
        body,
        (1,),
        1,
        [pl.BlockSpec(memory_space=pl.ANY)] * 2,
        [pl.BlockSpec(memory_space=pl.ANY)],
        [f32(*shape)],
        after,
        scratch=[
            pltpu.VMEM((tiles, ops, ops), jnp.float32),
            pltpu.VMEM(packing.shape, jnp.float32),
            pltpu.VMEM(shape, jnp.float32),
            pltpu.SemaphoreType.DMA((1 + half,)),
        ],
    )(place_in, keep, doubled)


def near_sum(place_in, keep, crossed, share, given, states, after=()):
    tiles, ops, _ = keep.shape
    half = states // 2
    packing = Packing(half * half, ops)
    blocks = [(p, min(LANES, ops - p)) for p in range(0, ops, LANES)]

    def body(s_ref, keep_ref, wire_in, share_ref, given_ref, out_ref, kept, wire, mine, *rest):
        made, sems = rest[:-1], rest[-1]
        x, second = s_ref[0], s_ref[1]
        loads = [pltpu.make_async_copy(wire_in, wire, sems.at[0])]
        for a in range(half):
            other = keep_ref.at[pl.ds(a * states + half * (1 - x), half)]
            loads.append(pltpu.make_async_copy(other, kept.at[pl.ds(a * half, half)], sems.at[1 + a]))
        for load in loads:
            load.start()
        for source, which in ((share_ref, 0), (given_ref, 1)):

            @pl.when(second == which)
            def _():
                load = pltpu.make_async_copy(source, mine, sems.at[1 + half])
                load.start()
                load.wait()

        for load in loads:
            load.wait()
        stores = []
        for n, (start, rows) in enumerate(blocks):
            ref = made[n]
            for a in range(half):
                for b in range(states):
                    t, one, turned = a * states + b, a * half + b % half, b % half * half + a

                    @pl.when(b // half != x)
                    def _():
                        ref[:, t] = kept[one, start : start + rows] + packing.rows(wire, one, start, rows)

                    @pl.when((b // half == x) & (second == 0))
                    def _():
                        ref[:, t] = mine[one, start : start + rows, :ops]

                    @pl.when((b // half == x) & (second == 1))
                    def _():
                        ref[:, t] = mine[turned, :, start : start + LANES].T[:rows, :ops]

            target = out_ref.at[1, pl.ds(start, rows)]
            stores.append(pltpu.make_async_copy(ref, target, sems.at[2 + half + n]))
            stores[n].start()
        for store in stores:
            store.wait()

    return call(
        body,
        (1,),
        1,
        [pl.BlockSpec(memory_space=pl.ANY)] * 4,
        [pl.BlockSpec(memory_space=pl.ANY)],
        [f32(2, ops, tiles, ops)],
        after,
        scratch=[
            pltpu.VMEM((half * half, ops, ops), jnp.float32),
            pltpu.VMEM(packing.shape, jnp.float32),
            pltpu.VMEM(share.shape, jnp.float32),
            *[pltpu.VMEM((rows, tiles, ops), jnp.float32) for _, rows in blocks],
            pltpu.SemaphoreType.DMA((2 + half + len(blocks),)),
        ],
    )(place_in, keep, crossed, share, given)


def far_terms(place_in, own, got, start, width, turned, mine, after=(), declared=0):
    states, ops, depth = own.shape
    half = states // 2
    rows = ops if turned else width
    tile = (up(ops, 8), width) if turned else (up(width, 8), ops)

    def first(x):
        return half * x if mine else half * (1 - x)

    def body(s_ref, own_ref, got_ref, out_ref):
        @pl.when(s_ref[1] == 1)
        def _():
            if turned:
                both = contract_last(own_ref[0], got_ref[...])
                parts = [both[:, a * width : (a + 1) * width] for a in range(half)]
            else:
                every = contract_last(got_ref[...], own_ref[0])
                parts = [every[u * width : (u + 1) * width] for u in range(states)]
                parts = [jnp.where(first(s_ref[0]) == 0, parts[a], parts[half + a]) for a in range(half)]
            for a in range(half):
                out_ref[a, 0, :rows] = parts[a]

    picked = half if turned else states

    def rows_in(v, x):
        return (start + first(x[0]) * width if turned else start, 0)

    return call(
        body,
        (states,),
        1,
        [
            pl.BlockSpec((1, ops, depth), lambda v, s: (v * s[1], 0, 0)),
            pl.BlockSpec(
                (pl.Element(picked * width), pl.Element(depth)), rows_in, pipeline_mode=pl.Buffered(1)
            ),
        ],
        [pl.BlockSpec((half, 1, *tile), lambda v, s: (0, v * s[1], 0, 0))],
        [f32(half, states, *tile)],
        after,
        declared=declared,
    )(place_in, own, got)


def far_sum(det, keep, came, rows, turned, after=(), declared=0):
    half, states, _, lanes = keep.shape
    shape = (up(rows + 1, 8), lanes)

    def body(x_ref, keep_ref, came_ref, tile_ref, code_ref):
        x = x_ref[0]
        top = jnp.zeros((rows, lanes), jnp.float32)
        for a in range(half):
            for v in range(states):
                top = jnp.maximum(top, jnp.abs(keep_ref[a, v, :rows] + came_ref[a, v, :rows]))
        exponent = jnp.floor(jnp.log2(jnp.maximum(jnp.max(top, keepdims=True), SMALLEST)))
        scale = jnp.exp2(LIFT - exponent)
        below = jnp.broadcast_to(exponent, (shape[0] - rows, lanes))
        for a in range(half):
            for v in range(states):
                tile = keep_ref[a, v, :rows] + came_ref[a, v, :rows]
                code_ref[a, v] = jnp.concatenate([powered(tile * scale), below]).astype(jnp.bfloat16)
            for b in range(half):
                v = half * x + b
                tile_ref[a, b] = keep_ref[a, v, :rows] + came_ref[a, v, :rows]

    shapes = [(half, half, rows, lanes), (half, states, *shape)]
    kinds = [jnp.float32, jnp.bfloat16]
    return call(
        body,
        (1,),
        1,
        [whole(keep.shape)] * 2,
        [whole(s) for s in shapes],
        [jax.ShapeDtypeStruct(s, kind) for s, kind in zip(shapes, kinds)],
        after,
        declared=declared,
    )(det, keep, came)


def crossing_codes(det, codes, after=(), declared=0):
    half, states, *tile = codes[0].shape
    shape = (len(codes), half, half, *tile)

    def body(x_ref, *refs):
        for k in range(len(codes)):
            refs[-1][k] = refs[k][...]

    return call(
        body,
        (1,),
        1,
        [pl.BlockSpec((half, half, *tile), lambda i, x: (0, 1 - x[0], 0, 0))] * len(codes),
        [whole(shape)],
        [jax.ShapeDtypeStruct(shape, jnp.bfloat16)],
        after,
        declared=declared,
    )(det, *codes)


def powered(value):
    square = value * value
    fourth = square * square
    return value * jnp.abs(value) * (fourth * fourth)


def rooted(code, exponent):
    code, exponent = code.astype(jnp.float32), exponent.astype(jnp.float32)
    root = jnp.exp2(jnp.log2(jnp.abs(code)) * (1 / POWER)) * jnp.exp2(exponent - LIFT)
    return jnp.where(code < 0, -root, root)


def decoded(code, rows):
    return rooted(code[:rows], code[rows : rows + 1])


def into_place(role, place_in, out, sources, pieces, after=(), declared=0):
    _, ops, tiles, _ = out.shape
    count = len(sources)

    def body(s_ref, out_in, *refs):
        out_ref, held, made, sems = refs[count], refs[count + 1 : 2 * count + 1], refs[2 * count + 1 : -1], refs[-1]

        @pl.when(s_ref[1] == role)
        def _():
            loads = [pltpu.make_async_copy(refs[k], held[k], sems.at[k]) for k in range(count)]
            for load in loads:
                load.start()
            for load in loads:
                load.wait()
            stores = []
            for k, (start, rows, fill) in enumerate(pieces):
                fill(s_ref[0], held, made[k])
                target = out_ref.at[0, pl.ds(start, rows)]
                stores.append(pltpu.make_async_copy(made[k], target, sems.at[count + k]))
                stores[k].start()
            for store in stores:
                store.wait()

    return call(
        body,
        (1,),
        1,
        [pl.BlockSpec(memory_space=pl.ANY)] * (1 + count),
        [pl.BlockSpec(memory_space=pl.ANY)],
        [f32(*out.shape)],
        after,
        {1: 0},
        [pltpu.VMEM(v.shape, v.dtype) for v in sources]
        + [pltpu.VMEM((rows, tiles, ops), jnp.float32) for _, rows, _ in pieces]
        + [pltpu.SemaphoreType.DMA((count + len(pieces),))],
        declared,
    )(place_in, out, *sources)


def returned(codes, chunks, widths, ops):
    def piece(n, k):
        half, states, _, _ = codes[n].shape

        def fill(x, refs, ref):
            for a in range(half):
                for v in range(states):
                    one = refs[n][a, v]
                    last = widths[k] < LANES
                    ref[:, a * states + v] = decoded(one, widths[k]) if last else decoded(one, ops).T

        return k * LANES, widths[k], fill

    return codes, [piece(n, k) for n, k in enumerate(chunks)]


def completed(tiles, turned, last, widths, ops):
    full = len(widths) - 1
    half, _, rest, _ = tiles[full].shape

    def piece(start, rows):
        def fill(x, refs, ref):
            for b in range(half):
                for u in range(2 * half):
                    a, t = u % half, 2 * half * b + u

                    @pl.when(u // half == x)
                    def _():
                        for k in range(full):
                            ref[:, t, k * LANES : (k + 1) * LANES] = refs[k][a, b, start : start + rows]
                        block = refs[full][a, b, :, start : start + rows]
                        ref[:, t, full * LANES :] = block.T

                    @pl.when(u // half != x)
                    def _():
                        for k in range(full):
                            code = refs[full + 1][k, a, b]
                            value = rooted(code[start : start + rows], code[ops : ops + 1])
                            ref[:, t, k * LANES : (k + 1) * LANES] = value
                        code = refs[full + 2][0, a, b, :, start : start + rows]
                        ref[:, t, full * LANES :] = decoded(code, rest).T

        return start, rows, fill

    return [*tiles, turned, last], [piece(p, min(LANES, ops - p)) for p in range(0, ops, LANES)]


def paired(amplitudes):
    blocks = lax.axis_size("state")
    far = blocks.bit_length() - 2
    states, depth, ops = amplitudes.shape
    full = ops // LANES
    wide = full * LANES
    both = ("state", "det")
    senders = [s for s in range(blocks) if (s & 1) == (s >> far & 1)]
    receivers = [s for s in range(blocks) if s not in senders]
    over = [(2 * s + x, 2 * (s ^ 1 << far) + x) for s in senders for x in range(2)]
    back = [(b, a) for a, b in over]
    across = [(2 * s + x, 2 * s + 1 - x) for s in receivers for x in range(2)]
    first_across = [(2 * s + x, 2 * s + 1 - x) for s in senders for x in range(2)]
    to_second = [(2 * s + x, 2 * (s ^ 1) + x) for s in senders for x in range(2)]
    opens = [(s, s ^ 1) for s in senders if (s >> far ^ s >> far - 1) & 1]

    state = lax.axis_index("state")
    x = lax.axis_index("det").astype(jnp.int32)
    det = x[None]
    receiver = ((state & 1) ^ (state >> far & 1)).astype(jnp.int32)
    at = jnp.stack([x, receiver])

    partner = lax.ppermute(amplitudes, "state", [(s, s ^ 1) for s in range(blocks)])
    first = amplitudes[:, :, :LANES].transpose(0, 2, 1)
    first, later = lax.optimization_barrier((first.reshape(states * LANES, depth), amplitudes))
    got = [lax.ppermute(first, both, over)]
    own = later.transpose(0, 2, 1)
    partner, own = lax.optimization_barrier((partner, own))
    partner = partner.transpose(0, 2, 1)

    crossed, token = near_send(det, own, partner, False, (first,))
    crossed = lax.ppermute(crossed, "det", [(0, 1), (1, 0)])
    doubled, token = near_send(det, own, partner, True, (token,))
    doubled = lax.ppermute(doubled, both, first_across)
    whole_own, token = lax.optimization_barrier((own, token))
    widths = [LANES] * full + [ops - wide]
    chunk = [whole_own[:, k * LANES : k * LANES + w].reshape(states * w, depth) for k, w in enumerate(widths)]
    later, token = lax.optimization_barrier((jnp.concatenate(chunk[1:full]), token))
    got.append(lax.ppermute(later, both, over))
    last, token = lax.optimization_barrier((chunk[full], token))
    got.append(lax.ppermute(last, both, over))
    keep, token = near_keep(det, own, partner, (token,))
    def terms(k, mine, done, declared=0):
        wire, start = (0, 0) if k == 0 else (2, 0) if k == full else (1, states * LANES * (k - 1))
        return far_terms(at, own, got[wire], start, widths[k], k < full, mine, done, declared)

    kepts, came, tiles, codes, theirs = {}, {}, {}, {}, {}

    def keep_terms(k, *token):
        kepts[k], token = terms(k, True, token, LONG if k == full - 1 else 0)
        return token

    def send_terms(k, *token):
        send, token = terms(k, False, token)
        came[k] = lax.ppermute(send, both, across)
        return token

    def sum_up(k, *token):
        rows = ops if k < full else widths[k]
        declared = LONG if k in early else 0
        tiles[k], codes[k], token = far_sum(det, kepts[k], came[k], rows, k < full, token, declared)
        theirs[k] = lax.ppermute(codes[k], both, back)
        return token

    def cross(ks, *token):
        wire, token = crossing_codes(det, [codes[k] for k in ks], token, 3 * LONG if ks == early else 0)
        return lax.ppermute(wire, both, across), token

    early, late = list(range(full)), [full]
    for k in early:
        token = send_terms(k, token)
        if k == full - 1:
            gate = lax.ppermute(token, "state", opens)
        token = keep_terms(k, token, *([crossed, doubled] if k == full - 1 else []))
    token = send_terms(full, token)
    for k in early:
        token = sum_up(k, token, *([gate] if k == 0 else []))
    token = keep_terms(full, token)
    token = sum_up(full, token)
    share, token = near_share(at, keep, doubled, states, (token,))
    given = lax.ppermute(share, both, to_second)
    turned, token = cross(early, token)
    last, token = cross(late, token, given)
    out, token = near_sum(at, keep, crossed, share, given, states, (token,))

    for k in early:
        out, token = into_place(0, at, out, *returned([theirs[k]], [k], widths, ops), (token,), LONG)
    placed = completed([tiles[k] for k in early + late], turned, last, widths, ops)
    out, token = into_place(1, at, out, *placed, (token,), LONG)
    out, token = into_place(0, at, out, *returned([theirs[full]], late, widths, ops), (token,))
    return out.transpose(0, 2, 1, 3)


def partner_2(value, axis, stride):
    mask = 2**stride
    pairs = [(source, source ^ mask) for source in range(lax.axis_size(axis))]
    return lax.ppermute(value, axis, pairs)


def pair_terms(own_block, partner, count):
    operators = own_block.shape[2]
    terms = jnp.einsum("adp,bdq->abpq", own_block, partner, preferred_element_type=jnp.float32)
    return terms.reshape(count, operators, operators)


def exchanged(amplitudes):
    blocks = lax.axis_size("state")
    far_bit = blocks.bit_length() - 2
    states = amplitudes.shape[0]
    gathered = []
    for bit in (far_bit, 0):
        partner = partner_2(amplitudes, "state", bit)
        terms = pair_terms(amplitudes, partner, states * states)
        gathered.append(lax.psum_scatter(terms, "det", scatter_dimension=0, tiled=True))
    return jnp.stack(gathered)


def on_device(amplitudes):
    states, _, ops = amplitudes.shape
    two = lax.axis_size("det") == 2 and lax.axis_size("state") >= 4
    if two and states % 2 == 0 and ops > 2 * LANES and ops % LANES % 8:
        return paired(amplitudes)
    return exchanged(amplitudes)


def solution(mesh):
    return jax.shard_map(
        on_device,
        mesh=mesh,
        in_specs=(P("state", "det", None),),
        out_specs=P(None, ("state", "det"), None, None),
        check_vma=False,
    )
```

```python
import functools

import jax
import jax.numpy as jnp
from jax import lax
from jax.experimental import pallas as pl
from jax.experimental.pallas import tpu as pltpu
from jax.sharding import PartitionSpec as P

LANES = 128
VMEM_LIMIT = 20 * 2**20
POWER, LIFT = 10, 11
SMALLEST = 2.0**-110
LONG = 10**10


def contract_last(left, right):
    return lax.dot_general(left, right, (((1,), (1,)), ((), ())), preferred_element_type=jnp.float32)


def call(body, grid, scalars, in_specs, out_specs, out_shape, after=(), aliases={}, scratch=(), declared=0):
    idle = len(after)

    def waiting(*refs):
        first = scalars + len(in_specs)
        last = first + idle + len(out_specs)
        body(*refs[:first], *refs[first + idle : last], *refs[last + 1 :])
        refs[last][...] = jnp.zeros_like(refs[last])

    token = (8, LANES)
    kernel = pl.pallas_call(
        waiting,
        grid_spec=pltpu.PrefetchScalarGridSpec(
            num_scalar_prefetch=scalars,
            grid=grid,
            in_specs=in_specs + [pl.BlockSpec(memory_space=pl.ANY)] * idle,
            out_specs=[*out_specs, whole(token)],
            scratch_shapes=scratch,
        ),
        out_shape=[*out_shape, f32(*token)],
        input_output_aliases=aliases,
        compiler_params=pltpu.CompilerParams(vmem_limit_bytes=VMEM_LIMIT),
        cost_estimate=pl.CostEstimate(flops=declared, bytes_accessed=declared // 100, transcendentals=0),
    )
    return lambda *operands: kernel(*operands, *after)


def f32(*shape):
    return jax.ShapeDtypeStruct(shape, jnp.float32)


def up(size, unit):
    return -(-size // unit) * unit


def whole(shape):
    return pl.BlockSpec(shape, lambda *_: (0,) * len(shape), pipeline_mode=pl.Buffered(1))


class Packing:
    def __init__(self, tiles, ops):
        self.ops, self.wide = ops, ops // LANES * LANES
        self.rest, self.below = ops - self.wide, up(ops, 8)
        self.each = self.below + up(self.rest, 8)
        beside = self.wide // LANES
        self.corners = [
            (tiles * self.each + t // beside * up(self.rest, 8), t % beside * LANES) for t in range(tiles)
        ]
        self.shape = (tiles * self.each + pl.cdiv(tiles, beside) * up(self.rest, 8), self.wide)

    def store(self, wire_ref, t, main, turned):
        row, lane = self.corners[t]
        wire_ref[t * self.each : t * self.each + self.ops] = main
        start = t * self.each + self.below
        wire_ref[start : start + self.rest] = turned[:, : self.wide]
        wire_ref[row : row + self.rest, lane : lane + self.rest] = turned[:, self.wide :]

    def rows(self, wire_ref, t, start, rows):
        row, lane = self.corners[t]
        under, padded = t * self.each + self.below, up(self.rest, 8)
        if start < self.wide:
            side = wire_ref[under : under + padded, start : start + rows].T[:, : self.rest]
        else:
            side = wire_ref[row : row + padded, lane : lane + LANES].T[:rows, : self.rest]
        return jnp.concatenate([wire_ref[t * self.each + start : t * self.each + start + rows], side], axis=1)

    def parts(self, wire_ref, t):
        row, lane = self.corners[t]
        start, padded = t * self.each + self.below, up(self.rest, 8)
        head, tail = slice(0, self.wide), slice(self.wide, self.ops)
        side = wire_ref[start : start + padded].T[:, : self.rest]
        corner = wire_ref[row : row + padded, lane : lane + LANES].T[: self.rest, : self.rest]
        main = wire_ref[t * self.each : t * self.each + self.ops]
        return [(slice(0, self.ops), head, main), (head, tail, side), (tail, tail, corner)]


def near_send(det, own, partner, to_mine, after=()):
    states, ops, depth = own.shape
    half, tiles = states // 2, (states // 2) ** 2
    packing = Packing(tiles, ops)

    def body(x_ref, own_ref, partner_ref, wire_ref):
        main = contract_last(own_ref[0], partner_ref[0, : packing.wide])
        turned = contract_last(partner_ref[0, packing.wide :], own_ref[0])
        for t in range(tiles):

            @pl.when(pl.program_id(0) == t)
            def _():
                packing.store(wire_ref, t, main, turned)

    def second(x):
        return half * (1 - x[0]) if to_mine else half * x[0]

    return call(
        body,
        (tiles,),
        1,
        [
            pl.BlockSpec((1, ops, depth), lambda t, x: (half * (1 - x[0]) + t // half, 0, 0)),
            pl.BlockSpec((1, ops, depth), lambda t, x: (second(x) + t % half, 0, 0)),
        ],
        [whole(packing.shape)],
        [f32(*packing.shape)],
        after,
    )(det, own, partner)


def near_keep(det, own, partner, after=()):
    states, ops, depth = own.shape
    half = states // 2

    def body(x_ref, own_ref, partner_ref, tile_ref):
        tile_ref[0] = contract_last(own_ref[0], partner_ref[0])

    return call(
        body,
        (half, states),
        1,
        [
            pl.BlockSpec((1, ops, depth), lambda a, b, x: (half * x[0] + a, 0, 0)),
            pl.BlockSpec((1, ops, depth), lambda a, b, x: (b, 0, 0)),
        ],
        [pl.BlockSpec((1, ops, ops), lambda a, b, x: (a * states + b, 0, 0))],
        [f32(half * states, ops, ops)],
        after,
    )(det, own, partner)


def near_share(place_in, keep, doubled, states, after=()):
    _, ops, _ = keep.shape
    half, tiles = states // 2, (states // 2) ** 2
    packing = Packing(tiles, ops)
    shape = (tiles, up(ops, 8), up(ops, LANES))

    def body(s_ref, keep_ref, wire_in, out_ref, kept, wire, made, sems):
        @pl.when(s_ref[1] == 0)
        def _():
            loads = [pltpu.make_async_copy(wire_in, wire, sems.at[0])]
            for a in range(half):
                mine = keep_ref.at[pl.ds(a * states + half * s_ref[0], half)]
                loads.append(pltpu.make_async_copy(mine, kept.at[pl.ds(a * half, half)], sems.at[1 + a]))
            for load in loads:
                load.start()
            for load in loads:
                load.wait()
            for t in range(tiles):
                for rows, columns, values in packing.parts(wire, t):
                    made[t, rows, columns] = kept[t, rows, columns] + values
            store = pltpu.make_async_copy(made, out_ref, sems.at[0])
            store.start()
            store.wait()

    return call(
        body,
        (1,),
        1,
        [pl.BlockSpec(memory_space=pl.ANY)] * 2,
        [pl.BlockSpec(memory_space=pl.ANY)],
        [f32(*shape)],
        after,
        scratch=[
            pltpu.VMEM((tiles, ops, ops), jnp.float32),
            pltpu.VMEM(packing.shape, jnp.float32),
            pltpu.VMEM(shape, jnp.float32),
            pltpu.SemaphoreType.DMA((1 + half,)),
        ],
    )(place_in, keep, doubled)


def near_sum(place_in, keep, crossed, share, given, states, after=()):
    tiles, ops, _ = keep.shape
    half = states // 2
    packing = Packing(half * half, ops)
    blocks = [(p, min(LANES, ops - p)) for p in range(0, ops, LANES)]

    def body(s_ref, keep_ref, wire_in, share_ref, given_ref, out_ref, kept, wire, mine, *rest):
        made, sems = rest[:-1], rest[-1]
        x, second = s_ref[0], s_ref[1]
        loads = [pltpu.make_async_copy(wire_in, wire, sems.at[0])]
        for a in range(half):
            other = keep_ref.at[pl.ds(a * states + half * (1 - x), half)]
            loads.append(pltpu.make_async_copy(other, kept.at[pl.ds(a * half, half)], sems.at[1 + a]))
        for load in loads:
            load.start()
        for source, which in ((share_ref, 0), (given_ref, 1)):

            @pl.when(second == which)
            def _():
                load = pltpu.make_async_copy(source, mine, sems.at[1 + half])
                load.start()
                load.wait()

        for load in loads:
            load.wait()
        stores = []
        for n, (start, rows) in enumerate(blocks):
            ref = made[n]
            for a in range(half):
                for b in range(states):
                    t, one, turned = a * states + b, a * half + b % half, b % half * half + a

                    @pl.when(b // half != x)
                    def _():
                        ref[:, t] = kept[one, start : start + rows] + packing.rows(wire, one, start, rows)

                    @pl.when((b // half == x) & (second == 0))
                    def _():
                        ref[:, t] = mine[one, start : start + rows, :ops]

                    @pl.when((b // half == x) & (second == 1))
                    def _():
                        ref[:, t] = mine[turned, :, start : start + LANES].T[:rows, :ops]

            target = out_ref.at[1, pl.ds(start, rows)]
            stores.append(pltpu.make_async_copy(ref, target, sems.at[2 + half + n]))
            stores[n].start()
        for store in stores:
            store.wait()

    return call(
        body,
        (1,),
        1,
        [pl.BlockSpec(memory_space=pl.ANY)] * 4,
        [pl.BlockSpec(memory_space=pl.ANY)],
        [f32(2, ops, tiles, ops)],
        after,
        scratch=[
            pltpu.VMEM((half * half, ops, ops), jnp.float32),
            pltpu.VMEM(packing.shape, jnp.float32),
            pltpu.VMEM(share.shape, jnp.float32),
            *[pltpu.VMEM((rows, tiles, ops), jnp.float32) for _, rows in blocks],
            pltpu.SemaphoreType.DMA((2 + half + len(blocks),)),
        ],
    )(place_in, keep, crossed, share, given)


def far_terms(place_in, own, got, start, width, turned, mine, after=(), declared=0):
    states, ops, depth = own.shape
    half = states // 2
    rows = ops if turned else width
    tile = (up(ops, 8), width) if turned else (up(width, 8), ops)

    def first(x):
        return half * x if mine else half * (1 - x)

    def body(s_ref, own_ref, got_ref, out_ref):
        @pl.when(s_ref[1] == 1)
        def _():
            if turned:
                both = contract_last(own_ref[0], got_ref[...])
                parts = [both[:, a * width : (a + 1) * width] for a in range(half)]
            else:
                every = contract_last(got_ref[...], own_ref[0])
                parts = [every[u * width : (u + 1) * width] for u in range(states)]
                parts = [jnp.where(first(s_ref[0]) == 0, parts[a], parts[half + a]) for a in range(half)]
            for a in range(half):
                out_ref[a, 0, :rows] = parts[a]

    picked = half if turned else states

    def rows_in(v, x):
        return (start + first(x[0]) * width if turned else start, 0)

    return call(
        body,
        (states,),
        1,
        [
            pl.BlockSpec((1, ops, depth), lambda v, s: (v * s[1], 0, 0)),
            pl.BlockSpec(
                (pl.Element(picked * width), pl.Element(depth)), rows_in, pipeline_mode=pl.Buffered(1)
            ),
        ],
        [pl.BlockSpec((half, 1, *tile), lambda v, s: (0, v * s[1], 0, 0))],
        [f32(half, states, *tile)],
        after,
        declared=declared,
    )(place_in, own, got)


def far_sum(det, keep, came, rows, turned, after=(), declared=0):
    half, states, _, lanes = keep.shape
    shape = (up(rows + 1, 8), lanes)

    def body(x_ref, keep_ref, came_ref, tile_ref, code_ref):
        x = x_ref[0]
        top = jnp.zeros((rows, lanes), jnp.float32)
        for a in range(half):
            for v in range(states):
                top = jnp.maximum(top, jnp.abs(keep_ref[a, v, :rows] + came_ref[a, v, :rows]))
        exponent = jnp.floor(jnp.log2(jnp.maximum(jnp.max(top, keepdims=True), SMALLEST)))
        scale = jnp.exp2(LIFT - exponent)
        below = jnp.broadcast_to(exponent, (shape[0] - rows, lanes))
        for a in range(half):
            for v in range(states):
                tile = keep_ref[a, v, :rows] + came_ref[a, v, :rows]
                code_ref[a, v] = jnp.concatenate([powered(tile * scale), below]).astype(jnp.bfloat16)
            for b in range(half):
                v = half * x + b
                tile_ref[a, b] = keep_ref[a, v, :rows] + came_ref[a, v, :rows]

    shapes = [(half, half, rows, lanes), (half, states, *shape)]
    kinds = [jnp.float32, jnp.bfloat16]
    return call(
        body,
        (1,),
        1,
        [whole(keep.shape)] * 2,
        [whole(s) for s in shapes],
        [jax.ShapeDtypeStruct(s, kind) for s, kind in zip(shapes, kinds)],
        after,
        declared=declared,
    )(det, keep, came)


def crossing_codes(det, codes, after=(), declared=0):
    half, states, *tile = codes[0].shape
    shape = (len(codes), half, half, *tile)

    def body(x_ref, *refs):
        for k in range(len(codes)):
            refs[-1][k] = refs[k][...]

    return call(
        body,
        (1,),
        1,
        [pl.BlockSpec((half, half, *tile), lambda i, x: (0, 1 - x[0], 0, 0))] * len(codes),
        [whole(shape)],
        [jax.ShapeDtypeStruct(shape, jnp.bfloat16)],
        after,
        declared=declared,
    )(det, *codes)


def powered(value):
    square = value * value
    fourth = square * square
    return value * jnp.abs(value) * (fourth * fourth)


def rooted(code, exponent):
    code, exponent = code.astype(jnp.float32), exponent.astype(jnp.float32)
    root = jnp.exp2(jnp.log2(jnp.abs(code)) * (1 / POWER)) * jnp.exp2(exponent - LIFT)
    return jnp.where(code < 0, -root, root)


def decoded(code, rows):
    return rooted(code[:rows], code[rows : rows + 1])


def into_place(role, place_in, out, sources, pieces, after=(), declared=0):
    _, ops, tiles, _ = out.shape
    count = len(sources)

    def body(s_ref, out_in, *refs):
        out_ref, held, made, sems = refs[count], refs[count + 1 : 2 * count + 1], refs[2 * count + 1 : -1], refs[-1]

        @pl.when(s_ref[1] == role)
        def _():
            loads = [pltpu.make_async_copy(refs[k], held[k], sems.at[k]) for k in range(count)]
            for load in loads:
                load.start()
            for load in loads:
                load.wait()
            stores = []
            for k, (start, rows, fill) in enumerate(pieces):
                fill(s_ref[0], held, made[k])
                target = out_ref.at[0, pl.ds(start, rows)]
                stores.append(pltpu.make_async_copy(made[k], target, sems.at[count + k]))
                stores[k].start()
            for store in stores:
                store.wait()

    return call(
        body,
        (1,),
        1,
        [pl.BlockSpec(memory_space=pl.ANY)] * (1 + count),
        [pl.BlockSpec(memory_space=pl.ANY)],
        [f32(*out.shape)],
        after,
        {1: 0},
        [pltpu.VMEM(v.shape, v.dtype) for v in sources]
        + [pltpu.VMEM((rows, tiles, ops), jnp.float32) for _, rows, _ in pieces]
        + [pltpu.SemaphoreType.DMA((count + len(pieces),))],
        declared,
    )(place_in, out, *sources)


def returned(codes, chunks, widths, ops):
    def piece(n, k):
        half, states, _, _ = codes[n].shape

        def fill(x, refs, ref):
            for a in range(half):
                for v in range(states):
                    one = refs[n][a, v]
                    last = widths[k] < LANES
                    ref[:, a * states + v] = decoded(one, widths[k]) if last else decoded(one, ops).T

        return k * LANES, widths[k], fill

    return codes, [piece(n, k) for n, k in enumerate(chunks)]


def completed(tiles, turned, last, widths, ops):
    full = len(widths) - 1
    half, _, rest, _ = tiles[full].shape

    def piece(start, rows):
        def fill(x, refs, ref):
            for b in range(half):
                for u in range(2 * half):
                    a, t = u % half, 2 * half * b + u

                    @pl.when(u // half == x)
                    def _():
                        for k in range(full):
                            ref[:, t, k * LANES : (k + 1) * LANES] = refs[k][a, b, start : start + rows]
                        block = refs[full][a, b, :, start : start + rows]
                        ref[:, t, full * LANES :] = block.T

                    @pl.when(u // half != x)
                    def _():
                        for k in range(full):
                            code = refs[full + 1][k, a, b]
                            value = rooted(code[start : start + rows], code[ops : ops + 1])
                            ref[:, t, k * LANES : (k + 1) * LANES] = value
                        code = refs[full + 2][0, a, b, :, start : start + rows]
                        ref[:, t, full * LANES :] = decoded(code, rest).T

        return start, rows, fill

    return [*tiles, turned, last], [piece(p, min(LANES, ops - p)) for p in range(0, ops, LANES)]


def paired(amplitudes):
    blocks = lax.axis_size("state")
    far = blocks.bit_length() - 2
    states, depth, ops = amplitudes.shape
    full = ops // LANES
    wide = full * LANES
    both = ("state", "det")
    senders = [s for s in range(blocks) if (s & 1) == (s >> far & 1)]
    receivers = [s for s in range(blocks) if s not in senders]
    over = [(2 * s + x, 2 * (s ^ 1 << far) + x) for s in senders for x in range(2)]
    back = [(b, a) for a, b in over]
    across = [(2 * s + x, 2 * s + 1 - x) for s in receivers for x in range(2)]
    first_across = [(2 * s + x, 2 * s + 1 - x) for s in senders for x in range(2)]
    to_second = [(2 * s + x, 2 * (s ^ 1) + x) for s in senders for x in range(2)]
    opens = [(s, s ^ 1) for s in senders if (s >> far ^ s >> far - 1) & 1]

    state = lax.axis_index("state")
    x = lax.axis_index("det").astype(jnp.int32)
    det = x[None]
    receiver = ((state & 1) ^ (state >> far & 1)).astype(jnp.int32)
    at = jnp.stack([x, receiver])

    partner = lax.ppermute(amplitudes, "state", [(s, s ^ 1) for s in range(blocks)])
    first = amplitudes[:, :, :LANES].transpose(0, 2, 1)
    first, later = lax.optimization_barrier((first.reshape(states * LANES, depth), amplitudes))
    got = [lax.ppermute(first, both, over)]
    own = later.transpose(0, 2, 1)
    partner, own = lax.optimization_barrier((partner, own))
    partner = partner.transpose(0, 2, 1)

    crossed, token = near_send(det, own, partner, False, (first,))
    crossed = lax.ppermute(crossed, "det", [(0, 1), (1, 0)])
    doubled, token = near_send(det, own, partner, True, (token,))
    doubled = lax.ppermute(doubled, both, first_across)
    whole_own, token = lax.optimization_barrier((own, token))
    widths = [LANES] * full + [ops - wide]
    chunk = [whole_own[:, k * LANES : k * LANES + w].reshape(states * w, depth) for k, w in enumerate(widths)]
    later, token = lax.optimization_barrier((jnp.concatenate(chunk[1:full]), token))
    got.append(lax.ppermute(later, both, over))
    last, token = lax.optimization_barrier((chunk[full], token))
    got.append(lax.ppermute(last, both, over))
    keep, token = near_keep(det, own, partner, (token,))
    def terms(k, mine, done, declared=0):
        wire, start = (0, 0) if k == 0 else (2, 0) if k == full else (1, states * LANES * (k - 1))
        return far_terms(at, own, got[wire], start, widths[k], k < full, mine, done, declared)

    kepts, came, tiles, codes, theirs = {}, {}, {}, {}, {}

    def keep_terms(k, *token):
        kepts[k], token = terms(k, True, token, LONG if k == full - 1 else 0)
        return token

    def send_terms(k, *token):
        send, token = terms(k, False, token)
        came[k] = lax.ppermute(send, both, across)
        return token

    def sum_up(k, *token):
        rows = ops if k < full else widths[k]
        declared = LONG if k in early else 0
        tiles[k], codes[k], token = far_sum(det, kepts[k], came[k], rows, k < full, token, declared)
        theirs[k] = lax.ppermute(codes[k], both, back)
        return token

    def cross(ks, *token):
        wire, token = crossing_codes(det, [codes[k] for k in ks], token, 3 * LONG if ks == early else 0)
        return lax.ppermute(wire, both, across), token

    early, late = list(range(full)), [full]
    for k in early:
        token = send_terms(k, token)
        if k == full - 1:
            gate = lax.ppermute(token, "state", opens)
        token = keep_terms(k, token, *([crossed, doubled] if k == full - 1 else []))
    token = send_terms(full, token)
    for k in early:
        token = sum_up(k, token, *([gate] if k == 0 else []))
    share, token = near_share(at, keep, doubled, states, (token,))
    given = lax.ppermute(share, both, to_second)
    token = keep_terms(full, token)
    token = sum_up(full, token)
    turned, token = cross(early, token)
    last, token = cross(late, token, given)
    out, token = near_sum(at, keep, crossed, share, given, states, (token,))

    for k in early:
        out, token = into_place(0, at, out, *returned([theirs[k]], [k], widths, ops), (token,), LONG)
    placed = completed([tiles[k] for k in early + late], turned, last, widths, ops)
    out, token = into_place(1, at, out, *placed, (token,), LONG)
    out, token = into_place(0, at, out, *returned([theirs[full]], late, widths, ops), (token,))
    return out.transpose(0, 2, 1, 3)


def partner_2(value, axis, stride):
    mask = 2**stride
    pairs = [(source, source ^ mask) for source in range(lax.axis_size(axis))]
    return lax.ppermute(value, axis, pairs)


def pair_terms(own_block, partner, count):
    operators = own_block.shape[2]
    terms = jnp.einsum("adp,bdq->abpq", own_block, partner, preferred_element_type=jnp.float32)
    return terms.reshape(count, operators, operators)


def exchanged(amplitudes):
    blocks = lax.axis_size("state")
    far_bit = blocks.bit_length() - 2
    states = amplitudes.shape[0]
    gathered = []
    for bit in (far_bit, 0):
        partner = partner_2(amplitudes, "state", bit)
        terms = pair_terms(amplitudes, partner, states * states)
        gathered.append(lax.psum_scatter(terms, "det", scatter_dimension=0, tiled=True))
    return jnp.stack(gathered)


def on_device(amplitudes):
    states, _, ops = amplitudes.shape
    two = lax.axis_size("det") == 2 and lax.axis_size("state") >= 4
    if two and states % 2 == 0 and ops > 2 * LANES and ops % LANES % 8:
        return paired(amplitudes)
    return exchanged(amplitudes)


def solution(mesh):
    return jax.shard_map(
        on_device,
        mesh=mesh,
        in_specs=(P("state", "det", None),),
        out_specs=P(None, ("state", "det"), None, None),
        check_vma=False,
    )
```

```python
import functools

import jax
import jax.numpy as jnp
from jax import lax
from jax.experimental import pallas as pl
from jax.experimental.pallas import tpu as pltpu
from jax.sharding import PartitionSpec as P

LANES = 128
VMEM_LIMIT = 20 * 2**20
POWER, LIFT = 10, 11
SMALLEST = 2.0**-110
LONG = 10**10


def contract_last(left, right):
    return lax.dot_general(left, right, (((1,), (1,)), ((), ())), preferred_element_type=jnp.float32)


def call(body, grid, scalars, in_specs, out_specs, out_shape, after=(), aliases={}, scratch=(), declared=0):
    idle = len(after)

    def waiting(*refs):
        first = scalars + len(in_specs)
        last = first + idle + len(out_specs)
        body(*refs[:first], *refs[first + idle : last], *refs[last + 1 :])
        refs[last][...] = jnp.zeros_like(refs[last])

    token = (8, LANES)
    kernel = pl.pallas_call(
        waiting,
        grid_spec=pltpu.PrefetchScalarGridSpec(
            num_scalar_prefetch=scalars,
            grid=grid,
            in_specs=in_specs + [pl.BlockSpec(memory_space=pl.ANY)] * idle,
            out_specs=[*out_specs, whole(token)],
            scratch_shapes=scratch,
        ),
        out_shape=[*out_shape, f32(*token)],
        input_output_aliases=aliases,
        compiler_params=pltpu.CompilerParams(vmem_limit_bytes=VMEM_LIMIT),
        cost_estimate=pl.CostEstimate(flops=declared, bytes_accessed=declared // 100, transcendentals=0),
    )
    return lambda *operands: kernel(*operands, *after)


def f32(*shape):
    return jax.ShapeDtypeStruct(shape, jnp.float32)


def up(size, unit):
    return -(-size // unit) * unit


def whole(shape):
    return pl.BlockSpec(shape, lambda *_: (0,) * len(shape), pipeline_mode=pl.Buffered(1))


class Packing:
    def __init__(self, tiles, ops):
        self.ops, self.wide = ops, ops // LANES * LANES
        self.rest, self.below = ops - self.wide, up(ops, 8)
        self.each = self.below + up(self.rest, 8)
        beside = self.wide // LANES
        self.corners = [
            (tiles * self.each + t // beside * up(self.rest, 8), t % beside * LANES) for t in range(tiles)
        ]
        self.shape = (tiles * self.each + pl.cdiv(tiles, beside) * up(self.rest, 8), self.wide)

    def store(self, wire_ref, t, main, turned):
        row, lane = self.corners[t]
        wire_ref[t * self.each : t * self.each + self.ops] = main
        start = t * self.each + self.below
        wire_ref[start : start + self.rest] = turned[:, : self.wide]
        wire_ref[row : row + self.rest, lane : lane + self.rest] = turned[:, self.wide :]

    def rows(self, wire_ref, t, start, rows):
        row, lane = self.corners[t]
        under, padded = t * self.each + self.below, up(self.rest, 8)
        if start < self.wide:
            side = wire_ref[under : under + padded, start : start + rows].T[:, : self.rest]
        else:
            side = wire_ref[row : row + padded, lane : lane + LANES].T[:rows, : self.rest]
        return jnp.concatenate([wire_ref[t * self.each + start : t * self.each + start + rows], side], axis=1)

    def parts(self, wire_ref, t):
        row, lane = self.corners[t]
        start, padded = t * self.each + self.below, up(self.rest, 8)
        head, tail = slice(0, self.wide), slice(self.wide, self.ops)
        side = wire_ref[start : start + padded].T[:, : self.rest]
        corner = wire_ref[row : row + padded, lane : lane + LANES].T[: self.rest, : self.rest]
        main = wire_ref[t * self.each : t * self.each + self.ops]
        return [(slice(0, self.ops), head, main), (head, tail, side), (tail, tail, corner)]


def near_send(det, own, partner, to_mine, after=()):
    states, ops, depth = own.shape
    half, tiles = states // 2, (states // 2) ** 2
    packing = Packing(tiles, ops)

    def body(x_ref, own_ref, partner_ref, wire_ref):
        main = contract_last(own_ref[0], partner_ref[0, : packing.wide])
        turned = contract_last(partner_ref[0, packing.wide :], own_ref[0])
        for t in range(tiles):

            @pl.when(pl.program_id(0) == t)
            def _():
                packing.store(wire_ref, t, main, turned)

    def second(x):
        return half * (1 - x[0]) if to_mine else half * x[0]

    return call(
        body,
        (tiles,),
        1,
        [
            pl.BlockSpec((1, ops, depth), lambda t, x: (half * (1 - x[0]) + t // half, 0, 0)),
            pl.BlockSpec((1, ops, depth), lambda t, x: (second(x) + t % half, 0, 0)),
        ],
        [whole(packing.shape)],
        [f32(*packing.shape)],
        after,
    )(det, own, partner)


def near_keep(det, own, partner, after=()):
    states, ops, depth = own.shape
    half = states // 2

    def body(x_ref, own_ref, partner_ref, tile_ref):
        tile_ref[0] = contract_last(own_ref[0], partner_ref[0])

    return call(
        body,
        (half, states),
        1,
        [
            pl.BlockSpec((1, ops, depth), lambda a, b, x: (half * x[0] + a, 0, 0)),
            pl.BlockSpec((1, ops, depth), lambda a, b, x: (b, 0, 0)),
        ],
        [pl.BlockSpec((1, ops, ops), lambda a, b, x: (a * states + b, 0, 0))],
        [f32(half * states, ops, ops)],
        after,
    )(det, own, partner)


def near_share(place_in, keep, doubled, states, after=()):
    _, ops, _ = keep.shape
    half, tiles = states // 2, (states // 2) ** 2
    packing = Packing(tiles, ops)
    shape = (tiles, up(ops, 8), up(ops, LANES))

    def body(s_ref, keep_ref, wire_in, out_ref, kept, wire, made, sems):
        @pl.when(s_ref[1] == 0)
        def _():
            loads = [pltpu.make_async_copy(wire_in, wire, sems.at[0])]
            for a in range(half):
                mine = keep_ref.at[pl.ds(a * states + half * s_ref[0], half)]
                loads.append(pltpu.make_async_copy(mine, kept.at[pl.ds(a * half, half)], sems.at[1 + a]))
            for load in loads:
                load.start()
            for load in loads:
                load.wait()
            for t in range(tiles):
                for rows, columns, values in packing.parts(wire, t):
                    made[t, rows, columns] = kept[t, rows, columns] + values
            store = pltpu.make_async_copy(made, out_ref, sems.at[0])
            store.start()
            store.wait()

    return call(
        body,
        (1,),
        1,
        [pl.BlockSpec(memory_space=pl.ANY)] * 2,
        [pl.BlockSpec(memory_space=pl.ANY)],
        [f32(*shape)],
        after,
        scratch=[
            pltpu.VMEM((tiles, ops, ops), jnp.float32),
            pltpu.VMEM(packing.shape, jnp.float32),
            pltpu.VMEM(shape, jnp.float32),
            pltpu.SemaphoreType.DMA((1 + half,)),
        ],
    )(place_in, keep, doubled)


def near_sum(place_in, keep, crossed, share, given, states, after=()):
    tiles, ops, _ = keep.shape
    half = states // 2
    packing = Packing(half * half, ops)
    blocks = [(p, min(LANES, ops - p)) for p in range(0, ops, LANES)]

    def body(s_ref, keep_ref, wire_in, share_ref, given_ref, out_ref, kept, wire, mine, *rest):
        made, sems = rest[:-1], rest[-1]
        x, second = s_ref[0], s_ref[1]
        loads = [pltpu.make_async_copy(wire_in, wire, sems.at[0])]
        for a in range(half):
            other = keep_ref.at[pl.ds(a * states + half * (1 - x), half)]
            loads.append(pltpu.make_async_copy(other, kept.at[pl.ds(a * half, half)], sems.at[1 + a]))
        for load in loads:
            load.start()
        for source, which in ((share_ref, 0), (given_ref, 1)):

            @pl.when(second == which)
            def _():
                load = pltpu.make_async_copy(source, mine, sems.at[1 + half])
                load.start()
                load.wait()

        for load in loads:
            load.wait()
        stores = []
        for n, (start, rows) in enumerate(blocks):
            ref = made[n]
            for a in range(half):
                for b in range(states):
                    t, one, turned = a * states + b, a * half + b % half, b % half * half + a

                    @pl.when(b // half != x)
                    def _():
                        ref[:, t] = kept[one, start : start + rows] + packing.rows(wire, one, start, rows)

                    @pl.when((b // half == x) & (second == 0))
                    def _():
                        ref[:, t] = mine[one, start : start + rows, :ops]

                    @pl.when((b // half == x) & (second == 1))
                    def _():
                        ref[:, t] = mine[turned, :, start : start + LANES].T[:rows, :ops]

            target = out_ref.at[1, pl.ds(start, rows)]
            stores.append(pltpu.make_async_copy(ref, target, sems.at[2 + half + n]))
            stores[n].start()
        for store in stores:
            store.wait()

    return call(
        body,
        (1,),
        1,
        [pl.BlockSpec(memory_space=pl.ANY)] * 4,
        [pl.BlockSpec(memory_space=pl.ANY)],
        [f32(2, ops, tiles, ops)],
        after,
        scratch=[
            pltpu.VMEM((half * half, ops, ops), jnp.float32),
            pltpu.VMEM(packing.shape, jnp.float32),
            pltpu.VMEM(share.shape, jnp.float32),
            *[pltpu.VMEM((rows, tiles, ops), jnp.float32) for _, rows in blocks],
            pltpu.SemaphoreType.DMA((2 + half + len(blocks),)),
        ],
    )(place_in, keep, crossed, share, given)


def far_terms(place_in, own, got, start, width, turned, mine, after=(), declared=0):
    states, ops, depth = own.shape
    half = states // 2
    rows = ops if turned else width
    tile = (up(ops, 8), width) if turned else (up(width, 8), ops)

    def first(x):
        return half * x if mine else half * (1 - x)

    def body(s_ref, own_ref, got_ref, out_ref):
        @pl.when(s_ref[1] == 1)
        def _():
            if turned:
                both = contract_last(own_ref[0], got_ref[...])
                parts = [both[:, a * width : (a + 1) * width] for a in range(half)]
            else:
                every = contract_last(got_ref[...], own_ref[0])
                parts = [every[u * width : (u + 1) * width] for u in range(states)]
                parts = [jnp.where(first(s_ref[0]) == 0, parts[a], parts[half + a]) for a in range(half)]
            for a in range(half):
                out_ref[a, 0, :rows] = parts[a]

    picked = half if turned else states

    def rows_in(v, x):
        return (start + first(x[0]) * width if turned else start, 0)

    return call(
        body,
        (states,),
        1,
        [
            pl.BlockSpec((1, ops, depth), lambda v, s: (v * s[1], 0, 0)),
            pl.BlockSpec(
                (pl.Element(picked * width), pl.Element(depth)), rows_in, pipeline_mode=pl.Buffered(1)
            ),
        ],
        [pl.BlockSpec((half, 1, *tile), lambda v, s: (0, v * s[1], 0, 0))],
        [f32(half, states, *tile)],
        after,
        declared=declared,
    )(place_in, own, got)


def far_sum(det, keep, came, rows, turned, after=(), declared=0):
    half, states, _, lanes = keep.shape
    shape = (up(rows + 1, 8), lanes)

    def body(x_ref, keep_ref, came_ref, tile_ref, code_ref):
        x = x_ref[0]
        top = jnp.zeros((rows, lanes), jnp.float32)
        for a in range(half):
            for v in range(states):
                top = jnp.maximum(top, jnp.abs(keep_ref[a, v, :rows] + came_ref[a, v, :rows]))
        exponent = jnp.floor(jnp.log2(jnp.maximum(jnp.max(top, keepdims=True), SMALLEST)))
        scale = jnp.exp2(LIFT - exponent)
        below = jnp.broadcast_to(exponent, (shape[0] - rows, lanes))
        for a in range(half):
            for v in range(states):
                tile = keep_ref[a, v, :rows] + came_ref[a, v, :rows]
                code_ref[a, v] = jnp.concatenate([powered(tile * scale), below]).astype(jnp.bfloat16)
            for b in range(half):
                v = half * x + b
                tile_ref[a, b] = keep_ref[a, v, :rows] + came_ref[a, v, :rows]

    shapes = [(half, half, rows, lanes), (half, states, *shape)]
    kinds = [jnp.float32, jnp.bfloat16]
    return call(
        body,
        (1,),
        1,
        [whole(keep.shape)] * 2,
        [whole(s) for s in shapes],
        [jax.ShapeDtypeStruct(s, kind) for s, kind in zip(shapes, kinds)],
        after,
        declared=declared,
    )(det, keep, came)


def crossing_codes(det, codes, after=(), declared=0):
    half, states, *tile = codes[0].shape
    shape = (len(codes), half, half, *tile)

    def body(x_ref, *refs):
        for k in range(len(codes)):
            refs[-1][k] = refs[k][...]

    return call(
        body,
        (1,),
        1,
        [pl.BlockSpec((half, half, *tile), lambda i, x: (0, 1 - x[0], 0, 0))] * len(codes),
        [whole(shape)],
        [jax.ShapeDtypeStruct(shape, jnp.bfloat16)],
        after,
        declared=declared,
    )(det, *codes)


def powered(value):
    square = value * value
    fourth = square * square
    return value * jnp.abs(value) * (fourth * fourth)


def rooted(code, exponent):
    code, exponent = code.astype(jnp.float32), exponent.astype(jnp.float32)
    root = jnp.exp2(jnp.log2(jnp.abs(code)) * (1 / POWER)) * jnp.exp2(exponent - LIFT)
    return jnp.where(code < 0, -root, root)


def decoded(code, rows):
    return rooted(code[:rows], code[rows : rows + 1])


def into_place(role, place_in, out, sources, pieces, after=(), declared=0):
    _, ops, tiles, _ = out.shape
    count = len(sources)

    def body(s_ref, out_in, *refs):
        out_ref, held, made, sems = refs[count], refs[count + 1 : 2 * count + 1], refs[2 * count + 1 : -1], refs[-1]

        @pl.when(s_ref[1] == role)
        def _():
            loads = [pltpu.make_async_copy(refs[k], held[k], sems.at[k]) for k in range(count)]
            for load in loads:
                load.start()
            for load in loads:
                load.wait()
            stores = []
            for k, (start, rows, fill) in enumerate(pieces):
                fill(s_ref[0], held, made[k])
                target = out_ref.at[0, pl.ds(start, rows)]
                stores.append(pltpu.make_async_copy(made[k], target, sems.at[count + k]))
                stores[k].start()
            for store in stores:
                store.wait()

    return call(
        body,
        (1,),
        1,
        [pl.BlockSpec(memory_space=pl.ANY)] * (1 + count),
        [pl.BlockSpec(memory_space=pl.ANY)],
        [f32(*out.shape)],
        after,
        {1: 0},
        [pltpu.VMEM(v.shape, v.dtype) for v in sources]
        + [pltpu.VMEM((rows, tiles, ops), jnp.float32) for _, rows, _ in pieces]
        + [pltpu.SemaphoreType.DMA((count + len(pieces),))],
        declared,
    )(place_in, out, *sources)


def returned(codes, chunks, widths, ops):
    def piece(n, k):
        half, states, _, _ = codes[n].shape

        def fill(x, refs, ref):
            for a in range(half):
                for v in range(states):
                    one = refs[n][a, v]
                    last = widths[k] < LANES
                    ref[:, a * states + v] = decoded(one, widths[k]) if last else decoded(one, ops).T

        return k * LANES, widths[k], fill

    return codes, [piece(n, k) for n, k in enumerate(chunks)]


def completed(tiles, turned, last, widths, ops):
    full = len(widths) - 1
    half, _, rest, _ = tiles[full].shape

    def piece(start, rows):
        def fill(x, refs, ref):
            for b in range(half):
                for u in range(2 * half):
                    a, t = u % half, 2 * half * b + u

                    @pl.when(u // half == x)
                    def _():
                        for k in range(full):
                            ref[:, t, k * LANES : (k + 1) * LANES] = refs[k][a, b, start : start + rows]
                        block = refs[full][a, b, :, start : start + rows]
                        ref[:, t, full * LANES :] = block.T

                    @pl.when(u // half != x)
                    def _():
                        for k in range(full):
                            code = refs[full + 1][k, a, b]
                            value = rooted(code[start : start + rows], code[ops : ops + 1])
                            ref[:, t, k * LANES : (k + 1) * LANES] = value
                        code = refs[full + 2][0, a, b, :, start : start + rows]
                        ref[:, t, full * LANES :] = decoded(code, rest).T

        return start, rows, fill

    return [*tiles, turned, last], [piece(p, min(LANES, ops - p)) for p in range(0, ops, LANES)]


def paired(amplitudes):
    blocks = lax.axis_size("state")
    far = blocks.bit_length() - 2
    states, depth, ops = amplitudes.shape
    full = ops // LANES
    wide = full * LANES
    both = ("state", "det")
    senders = [s for s in range(blocks) if (s & 1) == (s >> far & 1)]
    receivers = [s for s in range(blocks) if s not in senders]
    over = [(2 * s + x, 2 * (s ^ 1 << far) + x) for s in senders for x in range(2)]
    back = [(b, a) for a, b in over]
    across = [(2 * s + x, 2 * s + 1 - x) for s in receivers for x in range(2)]
    first_across = [(2 * s + x, 2 * s + 1 - x) for s in senders for x in range(2)]
    to_second = [(2 * s + x, 2 * (s ^ 1) + x) for s in senders for x in range(2)]
    opens = [(s, s ^ 1) for s in senders if (s >> far ^ s >> far - 1) & 1]

    state = lax.axis_index("state")
    x = lax.axis_index("det").astype(jnp.int32)
    det = x[None]
    receiver = ((state & 1) ^ (state >> far & 1)).astype(jnp.int32)
    at = jnp.stack([x, receiver])

    partner = lax.ppermute(amplitudes, "state", [(s, s ^ 1) for s in range(blocks)])
    first = amplitudes[:, :, :LANES].transpose(2, 0, 1)
    first, later = lax.optimization_barrier((first, amplitudes))
    got = [lax.ppermute(first, both, over)]
    own = later.transpose(0, 2, 1)
    partner, own = lax.optimization_barrier((partner, own))
    partner = partner.transpose(0, 2, 1)

    crossed, token = near_send(det, own, partner, False, (first,))
    crossed = lax.ppermute(crossed, "det", [(0, 1), (1, 0)])
    doubled, token = near_send(det, own, partner, True, (token,))
    doubled = lax.ppermute(doubled, both, first_across)
    whole_own, token = lax.optimization_barrier((own, token))
    widths = [LANES] * full + [ops - wide]
    chunk = [whole_own[:, k * LANES : k * LANES + w].reshape(states * w, depth) for k, w in enumerate(widths)]
    later, token = lax.optimization_barrier((jnp.concatenate(chunk[1:full]), token))
    got.append(lax.ppermute(later, both, over))
    last, token = lax.optimization_barrier((chunk[full], token))
    got.append(lax.ppermute(last, both, over))
    keep, token = near_keep(det, own, partner, (token,))
    raw, token = lax.optimization_barrier((got[0], token))
    got[0] = raw.transpose(1, 0, 2).reshape(states * LANES, depth)
    def terms(k, mine, done, declared=0):
        wire, start = (0, 0) if k == 0 else (2, 0) if k == full else (1, states * LANES * (k - 1))
        return far_terms(at, own, got[wire], start, widths[k], k < full, mine, done, declared)

    kepts, came, tiles, codes, theirs = {}, {}, {}, {}, {}

    def keep_terms(k, *token):
        kepts[k], token = terms(k, True, token, LONG if k == full - 1 else 0)
        return token

    def send_terms(k, *token):
        send, token = terms(k, False, token)
        came[k] = lax.ppermute(send, both, across)
        return token

    def sum_up(k, *token):
        rows = ops if k < full else widths[k]
        declared = LONG if k in early else 0
        tiles[k], codes[k], token = far_sum(det, kepts[k], came[k], rows, k < full, token, declared)
        theirs[k] = lax.ppermute(codes[k], both, back)
        return token

    def cross(ks, *token):
        wire, token = crossing_codes(det, [codes[k] for k in ks], token, 3 * LONG if ks == early else 0)
        return lax.ppermute(wire, both, across), token

    early, late = list(range(full)), [full]
    for k in early:
        token = send_terms(k, token)
        if k == full - 1:
            gate = lax.ppermute(token, "state", opens)
        token = keep_terms(k, token, *([crossed, doubled] if k == full - 1 else []))
    token = send_terms(full, token)
    for k in early:
        token = sum_up(k, token, *([gate] if k == 0 else []))
    share, token = near_share(at, keep, doubled, states, (token,))
    given = lax.ppermute(share, both, to_second)
    token = keep_terms(full, token)
    token = sum_up(full, token)
    turned, token = cross(early, token)
    last, token = cross(late, token, given)
    out, token = near_sum(at, keep, crossed, share, given, states, (token,))

    for k in early:
        out, token = into_place(0, at, out, *returned([theirs[k]], [k], widths, ops), (token,), LONG)
    placed = completed([tiles[k] for k in early + late], turned, last, widths, ops)
    out, token = into_place(1, at, out, *placed, (token,), LONG)
    out, token = into_place(0, at, out, *returned([theirs[full]], late, widths, ops), (token,))
    return out.transpose(0, 2, 1, 3)


def partner_2(value, axis, stride):
    mask = 2**stride
    pairs = [(source, source ^ mask) for source in range(lax.axis_size(axis))]
    return lax.ppermute(value, axis, pairs)


def pair_terms(own_block, partner, count):
    operators = own_block.shape[2]
    terms = jnp.einsum("adp,bdq->abpq", own_block, partner, preferred_element_type=jnp.float32)
    return terms.reshape(count, operators, operators)


def exchanged(amplitudes):
    blocks = lax.axis_size("state")
    far_bit = blocks.bit_length() - 2
    states = amplitudes.shape[0]
    gathered = []
    for bit in (far_bit, 0):
        partner = partner_2(amplitudes, "state", bit)
        terms = pair_terms(amplitudes, partner, states * states)
        gathered.append(lax.psum_scatter(terms, "det", scatter_dimension=0, tiled=True))
    return jnp.stack(gathered)


def on_device(amplitudes):
    states, _, ops = amplitudes.shape
    two = lax.axis_size("det") == 2 and lax.axis_size("state") >= 4
    if two and states % 2 == 0 and ops > 2 * LANES and ops % LANES % 8:
        return paired(amplitudes)
    return exchanged(amplitudes)


def solution(mesh):
    return jax.shard_map(
        on_device,
        mesh=mesh,
        in_specs=(P("state", "det", None),),
        out_specs=P(None, ("state", "det"), None, None),
        check_vma=False,
    )
```

```python
import functools

import jax
import jax.numpy as jnp
from jax import lax
from jax.experimental import pallas as pl
from jax.experimental.pallas import tpu as pltpu
from jax.sharding import PartitionSpec as P

LANES = 128
VMEM_LIMIT = 20 * 2**20
POWER, LIFT = 10, 11
SMALLEST = 2.0**-110
LONG = 10**10


def contract_last(left, right):
    return lax.dot_general(left, right, (((1,), (1,)), ((), ())), preferred_element_type=jnp.float32)


def call(body, grid, scalars, in_specs, out_specs, out_shape, after=(), aliases={}, scratch=(), declared=0):
    idle = len(after)

    def waiting(*refs):
        first = scalars + len(in_specs)
        last = first + idle + len(out_specs)
        body(*refs[:first], *refs[first + idle : last], *refs[last + 1 :])
        refs[last][...] = jnp.zeros_like(refs[last])

    token = (8, LANES)
    kernel = pl.pallas_call(
        waiting,
        grid_spec=pltpu.PrefetchScalarGridSpec(
            num_scalar_prefetch=scalars,
            grid=grid,
            in_specs=in_specs + [pl.BlockSpec(memory_space=pl.ANY)] * idle,
            out_specs=[*out_specs, whole(token)],
            scratch_shapes=scratch,
        ),
        out_shape=[*out_shape, f32(*token)],
        input_output_aliases=aliases,
        compiler_params=pltpu.CompilerParams(vmem_limit_bytes=VMEM_LIMIT),
        cost_estimate=pl.CostEstimate(flops=declared, bytes_accessed=declared // 100, transcendentals=0),
    )
    return lambda *operands: kernel(*operands, *after)


def f32(*shape):
    return jax.ShapeDtypeStruct(shape, jnp.float32)


def up(size, unit):
    return -(-size // unit) * unit


def whole(shape):
    return pl.BlockSpec(shape, lambda *_: (0,) * len(shape), pipeline_mode=pl.Buffered(1))


class Packing:
    def __init__(self, tiles, ops):
        self.ops, self.wide = ops, ops // LANES * LANES
        self.rest, self.below = ops - self.wide, up(ops, 8)
        self.each = self.below + up(self.rest, 8)
        beside = self.wide // LANES
        self.corners = [
            (tiles * self.each + t // beside * up(self.rest, 8), t % beside * LANES) for t in range(tiles)
        ]
        self.shape = (tiles * self.each + pl.cdiv(tiles, beside) * up(self.rest, 8), self.wide)

    def store(self, wire_ref, t, main, turned):
        row, lane = self.corners[t]
        wire_ref[t * self.each : t * self.each + self.ops] = main
        start = t * self.each + self.below
        wire_ref[start : start + self.rest] = turned[:, : self.wide]
        wire_ref[row : row + self.rest, lane : lane + self.rest] = turned[:, self.wide :]

    def rows(self, wire_ref, t, start, rows):
        row, lane = self.corners[t]
        under, padded = t * self.each + self.below, up(self.rest, 8)
        if start < self.wide:
            side = wire_ref[under : under + padded, start : start + rows].T[:, : self.rest]
        else:
            side = wire_ref[row : row + padded, lane : lane + LANES].T[:rows, : self.rest]
        return jnp.concatenate([wire_ref[t * self.each + start : t * self.each + start + rows], side], axis=1)

    def parts(self, wire_ref, t):
        row, lane = self.corners[t]
        start, padded = t * self.each + self.below, up(self.rest, 8)
        head, tail = slice(0, self.wide), slice(self.wide, self.ops)
        side = wire_ref[start : start + padded].T[:, : self.rest]
        corner = wire_ref[row : row + padded, lane : lane + LANES].T[: self.rest, : self.rest]
        main = wire_ref[t * self.each : t * self.each + self.ops]
        return [(slice(0, self.ops), head, main), (head, tail, side), (tail, tail, corner)]


def near_send(det, own, partner, to_mine, after=()):
    states, ops, depth = own.shape
    half, tiles = states // 2, (states // 2) ** 2
    packing = Packing(tiles, ops)

    def body(x_ref, own_ref, partner_ref, wire_ref):
        main = contract_last(own_ref[0], partner_ref[0, : packing.wide])
        turned = contract_last(partner_ref[0, packing.wide :], own_ref[0])
        for t in range(tiles):

            @pl.when(pl.program_id(0) == t)
            def _():
                packing.store(wire_ref, t, main, turned)

    def second(x):
        return half * (1 - x[0]) if to_mine else half * x[0]

    return call(
        body,
        (tiles,),
        1,
        [
            pl.BlockSpec((1, ops, depth), lambda t, x: (half * (1 - x[0]) + t // half, 0, 0)),
            pl.BlockSpec((1, ops, depth), lambda t, x: (second(x) + t % half, 0, 0)),
        ],
        [whole(packing.shape)],
        [f32(*packing.shape)],
        after,
    )(det, own, partner)


def near_keep(det, own, partner, after=()):
    states, ops, depth = own.shape
    half = states // 2

    def body(x_ref, own_ref, partner_ref, tile_ref):
        tile_ref[0] = contract_last(own_ref[0], partner_ref[0])

    return call(
        body,
        (half, states),
        1,
        [
            pl.BlockSpec((1, ops, depth), lambda a, b, x: (half * x[0] + a, 0, 0)),
            pl.BlockSpec((1, ops, depth), lambda a, b, x: (b, 0, 0)),
        ],
        [pl.BlockSpec((1, ops, ops), lambda a, b, x: (a * states + b, 0, 0))],
        [f32(half * states, ops, ops)],
        after,
    )(det, own, partner)


def near_share(place_in, keep, doubled, states, after=()):
    _, ops, _ = keep.shape
    half, tiles = states // 2, (states // 2) ** 2
    packing = Packing(tiles, ops)
    shape = (tiles, up(ops, 8), up(ops, LANES))

    def body(s_ref, keep_ref, wire_in, out_ref, kept, wire, made, sems):
        @pl.when(s_ref[1] == 0)
        def _():
            loads = [pltpu.make_async_copy(wire_in, wire, sems.at[0])]
            for a in range(half):
                mine = keep_ref.at[pl.ds(a * states + half * s_ref[0], half)]
                loads.append(pltpu.make_async_copy(mine, kept.at[pl.ds(a * half, half)], sems.at[1 + a]))
            for load in loads:
                load.start()
            for load in loads:
                load.wait()
            for t in range(tiles):
                for rows, columns, values in packing.parts(wire, t):
                    made[t, rows, columns] = kept[t, rows, columns] + values
            store = pltpu.make_async_copy(made, out_ref, sems.at[0])
            store.start()
            store.wait()

    return call(
        body,
        (1,),
        1,
        [pl.BlockSpec(memory_space=pl.ANY)] * 2,
        [pl.BlockSpec(memory_space=pl.ANY)],
        [f32(*shape)],
        after,
        scratch=[
            pltpu.VMEM((tiles, ops, ops), jnp.float32),
            pltpu.VMEM(packing.shape, jnp.float32),
            pltpu.VMEM(shape, jnp.float32),
            pltpu.SemaphoreType.DMA((1 + half,)),
        ],
    )(place_in, keep, doubled)


def near_sum(place_in, keep, crossed, share, given, states, after=()):
    tiles, ops, _ = keep.shape
    half = states // 2
    packing = Packing(half * half, ops)
    blocks = [(p, min(LANES, ops - p)) for p in range(0, ops, LANES)]

    def body(s_ref, keep_ref, wire_in, share_ref, given_ref, out_ref, kept, wire, mine, *rest):
        made, sems = rest[:-1], rest[-1]
        x, second = s_ref[0], s_ref[1]
        loads = [pltpu.make_async_copy(wire_in, wire, sems.at[0])]
        for a in range(half):
            other = keep_ref.at[pl.ds(a * states + half * (1 - x), half)]
            loads.append(pltpu.make_async_copy(other, kept.at[pl.ds(a * half, half)], sems.at[1 + a]))
        for load in loads:
            load.start()
        for source, which in ((share_ref, 0), (given_ref, 1)):

            @pl.when(second == which)
            def _():
                load = pltpu.make_async_copy(source, mine, sems.at[1 + half])
                load.start()
                load.wait()

        for load in loads:
            load.wait()
        stores = []
        for n, (start, rows) in enumerate(blocks):
            ref = made[n]
            for a in range(half):
                for b in range(states):
                    t, one, turned = a * states + b, a * half + b % half, b % half * half + a

                    @pl.when(b // half != x)
                    def _():
                        ref[:, t] = kept[one, start : start + rows] + packing.rows(wire, one, start, rows)

                    @pl.when((b // half == x) & (second == 0))
                    def _():
                        ref[:, t] = mine[one, start : start + rows, :ops]

                    @pl.when((b // half == x) & (second == 1))
                    def _():
                        ref[:, t] = mine[turned, :, start : start + LANES].T[:rows, :ops]

            target = out_ref.at[1, pl.ds(start, rows)]
            stores.append(pltpu.make_async_copy(ref, target, sems.at[2 + half + n]))
            stores[n].start()
        for store in stores:
            store.wait()

    return call(
        body,
        (1,),
        1,
        [pl.BlockSpec(memory_space=pl.ANY)] * 4,
        [pl.BlockSpec(memory_space=pl.ANY)],
        [f32(2, ops, tiles, ops)],
        after,
        scratch=[
            pltpu.VMEM((half * half, ops, ops), jnp.float32),
            pltpu.VMEM(packing.shape, jnp.float32),
            pltpu.VMEM(share.shape, jnp.float32),
            *[pltpu.VMEM((rows, tiles, ops), jnp.float32) for _, rows in blocks],
            pltpu.SemaphoreType.DMA((2 + half + len(blocks),)),
        ],
    )(place_in, keep, crossed, share, given)


def far_terms(place_in, own, got, start, width, turned, mine, after=(), declared=0):
    states, ops, depth = own.shape
    half = states // 2
    rows = ops if turned else width
    tile = (up(ops, 8), width) if turned else (up(width, 8), ops)

    def first(x):
        return half * x if mine else half * (1 - x)

    def body(s_ref, own_ref, got_ref, out_ref):
        @pl.when(s_ref[1] == 1)
        def _():
            if turned:
                both = contract_last(own_ref[0], got_ref[...])
                parts = [both[:, a * width : (a + 1) * width] for a in range(half)]
            else:
                every = contract_last(got_ref[...], own_ref[0])
                parts = [every[u * width : (u + 1) * width] for u in range(states)]
                parts = [jnp.where(first(s_ref[0]) == 0, parts[a], parts[half + a]) for a in range(half)]
            for a in range(half):
                out_ref[a, 0, :rows] = parts[a]

    picked = half if turned else states

    def rows_in(v, x):
        return (start + first(x[0]) * width if turned else start, 0)

    return call(
        body,
        (states,),
        1,
        [
            pl.BlockSpec((1, ops, depth), lambda v, s: (v * s[1], 0, 0)),
            pl.BlockSpec(
                (pl.Element(picked * width), pl.Element(depth)), rows_in, pipeline_mode=pl.Buffered(1)
            ),
        ],
        [pl.BlockSpec((half, 1, *tile), lambda v, s: (0, v * s[1], 0, 0))],
        [f32(half, states, *tile)],
        after,
        declared=declared,
    )(place_in, own, got)


def far_sum(det, keep, came, rows, turned, after=(), declared=0):
    half, states, _, lanes = keep.shape
    shape = (up(rows + 1, 8), lanes)

    def body(x_ref, keep_ref, came_ref, tile_ref, code_ref):
        x = x_ref[0]
        top = jnp.zeros((rows, lanes), jnp.float32)
        for a in range(half):
            for v in range(states):
                top = jnp.maximum(top, jnp.abs(keep_ref[a, v, :rows] + came_ref[a, v, :rows]))
        exponent = jnp.floor(jnp.log2(jnp.maximum(jnp.max(top, keepdims=True), SMALLEST)))
        scale = jnp.exp2(LIFT - exponent)
        below = jnp.broadcast_to(exponent, (shape[0] - rows, lanes))
        for a in range(half):
            for v in range(states):
                tile = keep_ref[a, v, :rows] + came_ref[a, v, :rows]
                code_ref[a, v] = jnp.concatenate([powered(tile * scale), below]).astype(jnp.bfloat16)
            for b in range(half):
                v = half * x + b
                tile_ref[a, b] = keep_ref[a, v, :rows] + came_ref[a, v, :rows]

    shapes = [(half, half, rows, lanes), (half, states, *shape)]
    kinds = [jnp.float32, jnp.bfloat16]
    return call(
        body,
        (1,),
        1,
        [whole(keep.shape)] * 2,
        [whole(s) for s in shapes],
        [jax.ShapeDtypeStruct(s, kind) for s, kind in zip(shapes, kinds)],
        after,
        declared=declared,
    )(det, keep, came)


def crossing_codes(det, codes, after=(), declared=0):
    half, states, *tile = codes[0].shape
    shape = (len(codes), half, half, *tile)

    def body(x_ref, *refs):
        for k in range(len(codes)):
            refs[-1][k] = refs[k][...]

    return call(
        body,
        (1,),
        1,
        [pl.BlockSpec((half, half, *tile), lambda i, x: (0, 1 - x[0], 0, 0))] * len(codes),
        [whole(shape)],
        [jax.ShapeDtypeStruct(shape, jnp.bfloat16)],
        after,
        declared=declared,
    )(det, *codes)


def powered(value):
    square = value * value
    fourth = square * square
    return value * jnp.abs(value) * (fourth * fourth)


def rooted(code, exponent):
    code, exponent = code.astype(jnp.float32), exponent.astype(jnp.float32)
    root = jnp.exp2(jnp.log2(jnp.abs(code)) * (1 / POWER)) * jnp.exp2(exponent - LIFT)
    return jnp.where(code < 0, -root, root)


def decoded(code, rows):
    return rooted(code[:rows], code[rows : rows + 1])


def into_place(role, place_in, out, sources, pieces, after=(), declared=0):
    _, ops, tiles, _ = out.shape
    count = len(sources)

    def body(s_ref, out_in, *refs):
        out_ref, held, made, sems = refs[count], refs[count + 1 : 2 * count + 1], refs[2 * count + 1 : -1], refs[-1]

        @pl.when(s_ref[1] == role)
        def _():
            loads = [pltpu.make_async_copy(refs[k], held[k], sems.at[k]) for k in range(count)]
            for load in loads:
                load.start()
            for load in loads:
                load.wait()
            stores = []
            for k, (start, rows, fill) in enumerate(pieces):
                fill(s_ref[0], held, made[k])
                target = out_ref.at[0, pl.ds(start, rows)]
                stores.append(pltpu.make_async_copy(made[k], target, sems.at[count + k]))
                stores[k].start()
            for store in stores:
                store.wait()

    return call(
        body,
        (1,),
        1,
        [pl.BlockSpec(memory_space=pl.ANY)] * (1 + count),
        [pl.BlockSpec(memory_space=pl.ANY)],
        [f32(*out.shape)],
        after,
        {1: 0},
        [pltpu.VMEM(v.shape, v.dtype) for v in sources]
        + [pltpu.VMEM((rows, tiles, ops), jnp.float32) for _, rows, _ in pieces]
        + [pltpu.SemaphoreType.DMA((count + len(pieces),))],
        declared,
    )(place_in, out, *sources)


def returned(codes, chunks, widths, ops):
    def piece(n, k):
        half, states, _, _ = codes[n].shape

        def fill(x, refs, ref):
            for a in range(half):
                for v in range(states):
                    one = refs[n][a, v]
                    last = widths[k] < LANES
                    ref[:, a * states + v] = decoded(one, widths[k]) if last else decoded(one, ops).T

        return k * LANES, widths[k], fill

    return codes, [piece(n, k) for n, k in enumerate(chunks)]


def completed(tiles, turned, last, widths, ops):
    full = len(widths) - 1
    half, _, rest, _ = tiles[full].shape

    def piece(start, rows):
        def fill(x, refs, ref):
            for b in range(half):
                for u in range(2 * half):
                    a, t = u % half, 2 * half * b + u

                    @pl.when(u // half == x)
                    def _():
                        for k in range(full):
                            ref[:, t, k * LANES : (k + 1) * LANES] = refs[k][a, b, start : start + rows]
                        block = refs[full][a, b, :, start : start + rows]
                        ref[:, t, full * LANES :] = block.T

                    @pl.when(u // half != x)
                    def _():
                        for k in range(full):
                            code = refs[full + 1][k, a, b]
                            value = rooted(code[start : start + rows], code[ops : ops + 1])
                            ref[:, t, k * LANES : (k + 1) * LANES] = value
                        code = refs[full + 2][0, a, b, :, start : start + rows]
                        ref[:, t, full * LANES :] = decoded(code, rest).T

        return start, rows, fill

    return [*tiles, turned, last], [piece(p, min(LANES, ops - p)) for p in range(0, ops, LANES)]


def paired(amplitudes):
    blocks = lax.axis_size("state")
    far = blocks.bit_length() - 2
    states, depth, ops = amplitudes.shape
    full = ops // LANES
    wide = full * LANES
    both = ("state", "det")
    senders = [s for s in range(blocks) if (s & 1) == (s >> far & 1)]
    receivers = [s for s in range(blocks) if s not in senders]
    over = [(2 * s + x, 2 * (s ^ 1 << far) + x) for s in senders for x in range(2)]
    back = [(b, a) for a, b in over]
    across = [(2 * s + x, 2 * s + 1 - x) for s in receivers for x in range(2)]
    first_across = [(2 * s + x, 2 * s + 1 - x) for s in senders for x in range(2)]
    to_second = [(2 * s + x, 2 * (s ^ 1) + x) for s in senders for x in range(2)]
    opens = [(s, s ^ 1) for s in senders if (s >> far ^ s >> far - 1) & 1]

    state = lax.axis_index("state")
    x = lax.axis_index("det").astype(jnp.int32)
    det = x[None]
    receiver = ((state & 1) ^ (state >> far & 1)).astype(jnp.int32)
    at = jnp.stack([x, receiver])

    partner = lax.ppermute(amplitudes, "state", [(s, s ^ 1) for s in range(blocks)])
    first = amplitudes[:, :, :LANES].transpose(2, 0, 1)
    first, later = lax.optimization_barrier((first, amplitudes))
    got = [lax.ppermute(first, both, over)]
    own = later.transpose(0, 2, 1)
    partner, own = lax.optimization_barrier((partner, own))
    partner = partner.transpose(0, 2, 1)

    crossed, token = near_send(det, own, partner, False, (first,))
    crossed = lax.ppermute(crossed, "det", [(0, 1), (1, 0)])
    doubled, token = near_send(det, own, partner, True, (token,))
    doubled = lax.ppermute(doubled, both, first_across)
    whole_own, token = lax.optimization_barrier((own, token))
    widths = [LANES] * full + [ops - wide]
    chunk = [whole_own[:, k * LANES : k * LANES + w].reshape(states * w, depth) for k, w in enumerate(widths)]
    later, token = lax.optimization_barrier((jnp.concatenate(chunk[1:full]), token))
    got.append(lax.ppermute(later, both, over))
    last, token = lax.optimization_barrier((chunk[full], token))
    got.append(lax.ppermute(last, both, over))
    keep, token = near_keep(det, own, partner, (token,))
    raw, token = lax.optimization_barrier((got[0], token))
    got[0] = raw.transpose(1, 0, 2).reshape(states * LANES, depth)
    def terms(k, mine, done, declared=0):
        wire, start = (0, 0) if k == 0 else (2, 0) if k == full else (1, states * LANES * (k - 1))
        return far_terms(at, own, got[wire], start, widths[k], k < full, mine, done, declared)

    kepts, came, tiles, codes, theirs = {}, {}, {}, {}, {}

    def keep_terms(k, *token):
        kepts[k], token = terms(k, True, token, LONG if k == full - 1 else 0)
        return token

    def send_terms(k, *token):
        send, token = terms(k, False, token)
        came[k] = lax.ppermute(send, both, across)
        return token

    def sum_up(k, *token):
        rows = ops if k < full else widths[k]
        declared = LONG if k in early else 0
        tiles[k], codes[k], token = far_sum(det, kepts[k], came[k], rows, k < full, token, declared)
        theirs[k] = lax.ppermute(codes[k], both, back)
        return token

    def cross(ks, *token):
        wire, token = crossing_codes(det, [codes[k] for k in ks], token, 3 * LONG if ks == early else 0)
        return lax.ppermute(wire, both, across), token

    early, late = list(range(full)), [full]
    for k in early:
        token = send_terms(k, token)
        if k == full - 1:
            gate = lax.ppermute(token, "state", opens)
        token = keep_terms(k, token, *([crossed, doubled] if k == full - 1 else []))
    token = send_terms(full, token)
    for k in early:
        token = sum_up(k, token, *([gate] if k == 0 else []))
    share, token = near_share(at, keep, doubled, states, (token,))
    given = lax.ppermute(share, both, to_second)
    token = keep_terms(full, token)
    token = sum_up(full, token)
    turned, token = cross(early, token)
    last, token = cross(late, token, given)
    out, token = near_sum(at, keep, crossed, share, given, states, (token,))

    out, token = into_place(0, at, out, *returned([theirs[k] for k in early], early, widths, ops), (token,), 2 * LONG)
    placed = completed([tiles[k] for k in early + late], turned, last, widths, ops)
    out, token = into_place(1, at, out, *placed, (token,), LONG)
    out, token = into_place(0, at, out, *returned([theirs[full]], late, widths, ops), (token,))
    return out.transpose(0, 2, 1, 3)


def partner_2(value, axis, stride):
    mask = 2**stride
    pairs = [(source, source ^ mask) for source in range(lax.axis_size(axis))]
    return lax.ppermute(value, axis, pairs)


def pair_terms(own_block, partner, count):
    operators = own_block.shape[2]
    terms = jnp.einsum("adp,bdq->abpq", own_block, partner, preferred_element_type=jnp.float32)
    return terms.reshape(count, operators, operators)


def exchanged(amplitudes):
    blocks = lax.axis_size("state")
    far_bit = blocks.bit_length() - 2
    states = amplitudes.shape[0]
    gathered = []
    for bit in (far_bit, 0):
        partner = partner_2(amplitudes, "state", bit)
        terms = pair_terms(amplitudes, partner, states * states)
        gathered.append(lax.psum_scatter(terms, "det", scatter_dimension=0, tiled=True))
    return jnp.stack(gathered)


def on_device(amplitudes):
    states, _, ops = amplitudes.shape
    two = lax.axis_size("det") == 2 and lax.axis_size("state") >= 4
    if two and states % 2 == 0 and ops > 2 * LANES and ops % LANES % 8:
        return paired(amplitudes)
    return exchanged(amplitudes)


def solution(mesh):
    return jax.shard_map(
        on_device,
        mesh=mesh,
        in_specs=(P("state", "det", None),),
        out_specs=P(None, ("state", "det"), None, None),
        check_vma=False,
    )
```
